32 devices in a mesh: dp: 8 (over y, x, core), batch: 4 (over z).
Axes of the slice: x: 2, y: 2, z: 4, core: 2. Of those that a mesh axis runs over, the one named last changes fastest.
Arguments:
- activations_in: float32 [32, 1024, 512], P(('dp', 'batch')), may hold values from -6 to 6
- gains: float32 [2, 2, 512], replicated, may hold values from 0.5 to 1.5
- shifts: float32 [2, 2, 512], replicated, may hold values from -2.5 to 2.5
- qkv_weights: bfloat16 [2, 3, 512, 512], replicated, may hold values from -0.25 to 0.25
- out_weights: bfloat16 [2, 512, 512], replicated, may hold values from -2 to 2
- up_weights: bfloat16 [2, 512, 2048], replicated, may hold values from -0.25 to 0.25
- up_bias: float32 [2, 2048], replicated, may hold values from -2.5 to 2.5
- down_weights: bfloat16 [2, 2048, 512], replicated, may hold values from -0.125 to 0.125
- down_bias: float32 [2, 512], replicated, may hold values from -2.5 to 2.5
- feature_maps: float32 [2, 8, 64, 256], replicated, may hold values from -4 to 4
- lengths: int32 [32, 6], P(('dp', 'batch')), may hold values from 18 to 146, as said below
- cotangent: float32 [32, 1024, 512], P(('dp', 'batch')), may hold values from -6 to 6
Outputs:
- activations_out: float32 [32, 1024, 512], P(('dp', 'batch'))
- input_grad: float32 [32, 1024, 512], P(('dp', 'batch'))
- gains_grad: float32 [2, 2, 512], P(None, None, 'batch')
- shifts_grad: float32 [2, 2, 512], P(None, None, 'batch')
- qkv_grad: float32 [2, 3, 512, 512], P(None, None, None, 'batch')
- out_grad: float32 [2, 512, 512], P(None, None, 'batch')
- up_grad: float32 [2, 512, 2048], P(None, None, 'batch')
- up_bias_grad: float32 [2, 2048], P(None, 'batch')
- down_grad: float32 [2, 2048, 512], P(None, None, 'batch')
- down_bias_grad: float32 [2, 512], P(None, 'batch')
The draws below stay inside these ranges and needn't reach their ends.
Inputs may be any that keep to these rules, and one draw needn't show every extreme that they name: `lengths`: each of a row's 6 proteins has 18 to 146 tokens; in every row one protein has exactly 146 and another exactly 18; the remaining positions of the row are padding.
All inputs are finite; a program needn't handle non-finite values.
Results may differ from the reference program's by a relative error of at most 0.015.
The reference program's roundings to bfloat16 on the way count: a program that leaves them out, or rounds other values in their place, can miss the bound.
Values sent between devices are 32-bit elements; how exact they have to be, the bound alone decides.
No kernel may reach another device: no remote copies, remote signals or barrier semaphores. Data moves between devices by JAX's collectives and lax.ppermute only.
A program may use at most 384 MiB of HBM per device.

```python
import functools
import math
import jax
import jax.numpy as jnp
from jax import lax

D = 512
H = 8
E = 64
M = 256
FF = 2048
LAYERS = 2
S = 1024
C = 256
NDOC = 6
ROWS = 32
LMAX = 146
LMIN = 18


def draw_lengths(key, part):
    key = jax.random.fold_in(key, 7)
    first_key, second_key = jax.random.split(key)
    drawn = jax.random.randint(first_key, (ROWS, NDOC), LMIN, LMAX + 1)
    longest = jax.random.randint(second_key, (ROWS, 1), 0, NDOC)
    columns = jnp.arange(NDOC)[None, :]
    drawn = jnp.where(columns == longest, LMAX, drawn)
    drawn = jnp.where(columns == (longest + 1) % NDOC, LMIN, drawn)
    return drawn.astype(jnp.int32)


def block_scale(rng, extent, pieces, low, high):
    gain = 1.0
    for dim, parts in pieces:
        steps = jax.random.uniform(jax.random.fold_in(jax.random.fold_in(rng, 6), dim), (parts,), jnp.float32, low / len(pieces), high / len(pieces))
        gain = gain * jnp.repeat(jnp.exp(steps), extent[dim] // parts).reshape((-1,) + (1,) * (len(extent) - 1 - dim))
    return gain


def centred(rng, dims, scale, most, shards=(), held_as=jnp.bfloat16):
    gain = block_scale(rng, dims, shards, -0.22, 0.18) if shards else 1.0
    values = jax.random.normal(rng, dims, jnp.float32) * scale * gain
    return jnp.minimum(jnp.maximum(values, -most), most).astype(held_as)


def setup_inputs(seed: int = 0) -> dict:
    key_list = jax.random.split(jax.random.key(seed), 13)
    return {
        "activations_in": centred(key_list[0], (ROWS, S, D), 1.0, 6.0, ((0, 32),), jnp.float32),
        "gains": jnp.clip(1.0 + 0.1 * jax.random.normal(key_list[1], (LAYERS, 2, D), jnp.float32), 0.5, 1.5),
        "shifts": centred(key_list[2], (LAYERS, 2, D), 0.3, 2.5, (), jnp.float32),
        "qkv_weights": centred(key_list[3], (LAYERS, 3, D, D), D ** -0.5, 0.25),
        "out_weights": centred(key_list[4], (LAYERS, D, D), (max(D // 64, 1)) ** -0.5, 2.0),
        "up_weights": centred(key_list[5], (LAYERS, D, FF), D ** -0.5, 0.25),
        "up_bias": centred(key_list[6], (LAYERS, FF), 0.3, 2.5, (), jnp.float32),
        "down_weights": centred(key_list[7], (LAYERS, FF, D), FF ** -0.5, 0.125),
        "down_bias": centred(key_list[8], (LAYERS, D), 0.3, 2.5, (), jnp.float32),
        "feature_maps": centred(key_list[9], (LAYERS, H, E, M), 1.0, 4.0, (), jnp.float32),
        "lengths": draw_lengths(jax.random.fold_in(key_list[12], 71), 0),
        "cotangent": centred(key_list[11], (ROWS, S, D), 1.0, 6.0, ((0, 32),), jnp.float32),
    }


highest = lax.Precision.HIGHEST

@jax.custom_vjp
def low(v):
    return lax.optimization_barrier(v.astype(jnp.bfloat16)).astype(jnp.float32)

@jax.custom_vjp
def low_back(v):
    return v

def low_keep(v):
    return (low(v), None)

def low_pass(kept, grad):
    return (grad,)

def back_keep(v):
    return (v, None)

def back_low(kept, grad):
    return (low(grad),)
low.defvjp(low_keep, low_pass)
low_back.defvjp(back_keep, back_low)

def layer_norm(values, gain_row, shift_row):
    average = lax.optimization_barrier(jnp.mean(values, axis=-1, keepdims=True))
    centered = values - average
    spread = lax.optimization_barrier(jnp.mean(centered * centered, axis=-1, keepdims=True))
    return centered * lax.rsqrt(spread + 1e-05) * gain_row + shift_row

def segments(lengths, length):
    bounds = jnp.cumsum(lengths, axis=-1).astype(jnp.int32)
    position = jnp.arange(length, dtype=jnp.int32)
    segment = lax.optimization_barrier(jnp.sum((position[None, :, None] >= bounds[:, None, :]).astype(jnp.int32), axis=-1)).astype(jnp.int32)
    in_protein = segment < lengths.shape[-1]
    return (segment, in_protein)

def features(values, feature_map):
    factor = values.shape[-1] ** (-0.25)
    projected = jnp.einsum('she,hem->shm', values, feature_map, precision=highest) * factor
    squares = lax.optimization_barrier(jnp.sum(values * values, axis=-1, keepdims=True)) * (factor * factor * 0.5)
    return jnp.exp(projected - squares) * feature_map.shape[-1] ** (-0.5)

def favor_row(queries, keys, values, segment, feature_map, block_len):
    length, head_count, head_dim = values.shape
    feat_count = feature_map.shape[-1]
    blocks = length // block_len
    phi_q = features(queries, feature_map).reshape(blocks, block_len, head_count, feat_count)
    phi_k = features(keys, feature_map).reshape(blocks, block_len, head_count, feat_count)
    value_blocks = values.reshape(blocks, block_len, head_count, head_dim)
    seg_blocks = segment.reshape(blocks, block_len)
    causal = jnp.arange(block_len)[:, None] >= jnp.arange(block_len)[None, :]

    def advance(carried_in, block_in):
        state_kv, state_k, previous = carried_in
        feat_q, feat_k, block_vals, seg_block = block_in
        same_doc = (seg_block[:, None] == seg_block[None, :]) & causal
        kernel = jnp.einsum('thm,shm->hts', feat_q, feat_k, precision=highest) * same_doc.astype(feat_q.dtype)[None]
        carried = (seg_block == previous).astype(feat_q.dtype)[:, None]
        numerator = jnp.einsum('hts,she->the', kernel, block_vals, precision=highest)
        numerator = numerator + carried[:, :, None] * jnp.einsum('thm,hme->the', feat_q, state_kv, precision=highest)
        denominator = lax.optimization_barrier(jnp.sum(kernel, axis=-1)).T + carried * jnp.einsum('thm,hm->th', feat_q, state_k, precision=highest)
        result = numerator / denominator[:, :, None]
        last_seg = seg_block[-1]
        carry_on = (last_seg == previous).astype(feat_q.dtype)
        member = (seg_block == last_seg).astype(feat_q.dtype)[:, None, None]
        kept_keys = feat_k * member
        state_kv = carry_on * state_kv + jnp.einsum('shm,she->hme', kept_keys, block_vals, precision=highest)
        state_k = carry_on * state_k + lax.optimization_barrier(jnp.sum(kept_keys, axis=0))
        return ((state_kv, state_k, last_seg), result)
    start = (jnp.zeros((head_count, feat_count, head_dim), values.dtype), jnp.zeros((head_count, feat_count), values.dtype), jnp.full((), -1, jnp.int32))
    final_state, result = lax.scan(jax.checkpoint(advance), start, (phi_q, phi_k, value_blocks, seg_blocks))
    return result.reshape(length, head_count * head_dim)

def favor(projected, feature_map, segment, block_len):
    head_count = feature_map.shape[0]
    row_count, length, model_dim = projected.shape[1:]
    stacked = projected.reshape(3, row_count, length, head_count, model_dim // head_count)
    per_row = functools.partial(favor_row, feature_map=feature_map, block_len=block_len)
    return jax.vmap(per_row)(stacked[0], stacked[1], stacked[2], segment)

def apply_layer(values, weights, feature_map, segment, in_protein):
    gain_pair, shift_pair, qkv_mats, out_mat, up_mat, up_vec, down_mat, down_vec = weights
    normed = low(layer_norm(values, gain_pair[0], shift_pair[0]))
    projected = low_back(jnp.einsum('rsd,jde->jrse', normed, qkv_mats, precision=highest))
    attended = favor(projected, feature_map, segment, C)
    attn_low = low(attended * in_protein.astype(attended.dtype)[..., None])
    mid_state = values + low_back(jnp.einsum('rsd,de->rse', attn_low, out_mat, precision=highest))
    normed_two = low(layer_norm(mid_state, gain_pair[1], shift_pair[1]))
    pre_act = low_back(jnp.einsum('rsd,df->rsf', normed_two, up_mat, precision=highest) + up_vec)
    activated = low(jax.nn.gelu(pre_act, approximate=False))
    return mid_state + low_back(jnp.einsum('rsf,fd->rsd', activated, down_mat, precision=highest) + down_vec)

def network(values, params, feature_maps, segment, in_protein):
    for layer_id in range(LAYERS):
        weights = tuple((param[layer_id] for param in params))
        values = apply_layer(values, weights, feature_maps[layer_id], segment, in_protein)
    return values

def reference(activations_in, gains, shifts, qkv_weights, out_weights, up_weights, up_bias, down_weights, down_bias, feature_maps, lengths, cotangent):
    params = tuple((param.astype(jnp.float32) for param in (gains, shifts, qkv_weights, out_weights, up_weights, up_bias, down_weights, down_bias)))
    segment, in_protein = segments(lengths, S)
    group_rows = math.gcd(ROWS, max(1, 4096 // S))
    group_count = ROWS // group_rows

    def regroup(array):
        return array.reshape((group_count, group_rows) + array.shape[1:])

    def group_step(running, group_in):
        x_group, cot_group, seg_group, mask_group = group_in
        result, pullback = jax.vjp(lambda inputs, weights: network(inputs, weights, feature_maps, seg_group, mask_group), x_group, params)
        grad_x, grad_params = pullback(cot_group)
        return (jax.tree.map(jnp.add, running, grad_params), (result, grad_x))
    empty_grads = jax.tree.map(jnp.zeros_like, params)
    running, (outputs, input_grads) = lax.scan(group_step, empty_grads, (regroup(activations_in), regroup(cotangent), regroup(segment), regroup(in_protein)))
    return (outputs.reshape(activations_in.shape), input_grads.reshape(activations_in.shape), running[0], running[1], running[2], running[3], running[4], running[5], running[6], running[7])
```

```python
import functools
import math

import jax
import jax.numpy as jnp
from jax import lax
from jax.experimental import pallas as pl
from jax.experimental.pallas import tpu as pltpu
from jax.sharding import PartitionSpec as P

BLOCK = 256
BLOCKS = 3
LIVE = BLOCK * BLOCKS
REACH = 160
LANES = 128
NDOC = 6
MIB = 1 << 20
F32 = jnp.float32
BF16 = jnp.bfloat16
LOG2E = 1.4426950408889634
NT = (((1,), (1,)), ((), ()))
TN = (((0,), (0,)), ((), ()))


def dot(a, b):
    return jnp.dot(a, b, preferred_element_type=F32)


def dot_nt(a, b):
    return lax.dot_general(a, b, NT, preferred_element_type=F32)


def dot_tn(a, b):
    return lax.dot_general(a, b, TN, preferred_element_type=F32)


def params_for(mib):
    return pltpu.CompilerParams(vmem_limit_bytes=mib * MIB)


def cost(flops, traffic, transcendentals=0):
    return pl.CostEstimate(flops=int(flops), bytes_accessed=int(traffic), transcendentals=int(transcendentals))


def normalize(values):
    centered = values - jnp.mean(values, axis=-1, keepdims=True)
    rstd = lax.rsqrt(jnp.mean(centered * centered, axis=-1, keepdims=True) + 1e-05)
    return centered * rstd, rstd


def norm_pull(grad, gain, unit, rstd):
    p = grad * gain
    return rstd * (p - jnp.mean(p, axis=-1, keepdims=True) - unit * jnp.mean(p * unit, axis=-1, keepdims=True))


def split_two(values):
    high = values.astype(BF16)
    return high, (values - high.astype(F32)).astype(BF16)


def protein_ids(len_ref, position):
    bound = jnp.int32(0)
    ids = jnp.zeros(position.shape, jnp.int32)
    for j in range(NDOC):
        bound = bound + len_ref[j]
        ids = ids + (position >= bound).astype(jnp.int32)
    return ids


def token_count(len_ref):
    total = jnp.int32(0)
    for j in range(NDOC):
        total = total + len_ref[j]
    return total


def pair_mask(len_ref, shape, first_row, first_col, causal_rows):
    rows = lax.broadcasted_iota(jnp.int32, shape, 0) + first_row
    cols = lax.broadcasted_iota(jnp.int32, shape, 1) + first_col
    same = protein_ids(len_ref, rows) == protein_ids(len_ref, cols)
    ordered = (rows >= cols) if causal_rows else (cols >= rows)
    return jnp.where(same & ordered, 1.0, 0.0).astype(BF16)


def fill_masks(len_ref, own_ref, before_ref, causal_rows):
    for b in range(BLOCKS):
        own_ref[b] = pair_mask(len_ref, (BLOCK, BLOCK), b * BLOCK, b * BLOCK, causal_rows)
    for b in range(1, BLOCKS):
        if causal_rows:
            before_ref[b - 1] = pair_mask(len_ref, (REACH, BLOCK), b * BLOCK, (b - 1) * BLOCK, True)
        else:
            before_ref[b - 1] = pair_mask(len_ref, (REACH, BLOCK), b * BLOCK - REACH, b * BLOCK, False)


def attn_fwd_body(len_ref, x_ref, gain_ref, shift_ref, w_ref, fm_ref, normed_ref, phi_q_ref, phi_k_ref, uq_ref, uk_ref,
                  v_ref, att_ref, rden_ref, low_ref, proj_ref, own_ref, before_ref, num_ref):
    step = pl.program_id(0)

    @pl.when(step == 0)
    def _():
        fill_masks(len_ref, own_ref, before_ref, True)
        for b in range(BLOCKS):
            rows = pl.ds(b * BLOCK, BLOCK)
            unit, _ = normalize(x_ref[rows, :])
            normed_ref[rows, :] = (unit * gain_ref[...] + shift_ref[...]).astype(BF16)
        for j in range(3):
            for half in range(2):
                got = dot(normed_ref[...], w_ref[j, :, half * 256 : half * 256 + 256])
                proj_ref[j, 2 * half] = got[:, :LANES]
                proj_ref[j, 2 * half + 1] = got[:, LANES:]

    lane = lax.broadcasted_iota(jnp.int32, (BLOCK, LANES), 1) < 64
    uq_ref[0] = proj_ref[0, step]
    uk_ref[0] = proj_ref[1, step]
    v_ref[0] = proj_ref[2, step].astype(BF16)
    for which, phi_ref in ((0, phi_q_ref), (1, phi_k_ref)):
        for head in range(2):
            high, low = split_two(fm_ref[head] * (64.0 ** (-0.25) * LOG2E))
            stacked = jnp.concatenate([high, low, high, low], axis=0)
            for b in range(BLOCKS):
                rows = pl.ds(b * BLOCK, BLOCK)
                u = proj_ref[which, step, rows, :]
                turned = pltpu.roll(u, 64, 1)
                twice = jnp.where(lane, u, turned) if head == 0 else jnp.where(lane, turned, u)
                squares = jnp.sum(twice * twice, axis=-1, keepdims=True) * (LOG2E / 32.0) + 4.0
                u_high, u_low = split_two(twice)
                projected = dot(jnp.concatenate([u_high, u_low], axis=1), stacked)
                phi_ref[head, rows, :] = jnp.exp2(projected - squares).astype(BF16)
    ones = jnp.ones((BLOCK, LANES), BF16)
    for b in range(BLOCKS):
        rows = pl.ds(b * BLOCK, BLOCK)
        v_now = jnp.concatenate([v_ref[0, rows, :], ones], axis=1)
        for head in range(2):
            weights = dot_nt(phi_q_ref[head, rows, :], phi_k_ref[head, rows, :]).astype(BF16) * own_ref[b]
            num_ref[head] = dot(weights, v_now)
            if b > 0:
                earlier = pl.ds((b - 1) * BLOCK, BLOCK)
                v_before = jnp.concatenate([v_ref[0, earlier, :], ones], axis=1)
                weights = dot_nt(phi_q_ref[head, pl.ds(b * BLOCK, REACH), :], phi_k_ref[head, earlier, :])
                num_ref[head, :REACH, :] += dot(weights.astype(BF16) * before_ref[b - 1], v_before)
        rden = 1.0 / jnp.where(lane, num_ref[0, :, LANES:], num_ref[1, :, LANES:])
        attended = jnp.where(lane, num_ref[0, :, :LANES], num_ref[1, :, :LANES]) * rden
        position = lax.broadcasted_iota(jnp.int32, (BLOCK, LANES), 0) + b * BLOCK
        attended = jnp.where(position < token_count(len_ref), attended, 0.0)
        rden_ref[0, rows, :] = rden
        att_ref[0, rows, :] = attended
        low_ref[rows, :] = attended.astype(BF16)


def attn_fwd(lengths, x, gain, shift, w, fm):
    width = x.shape[1]
    heads = fm.shape[0]
    pairs = heads // 2
    per_pair = pl.BlockSpec((1, LIVE, LANES), lambda p, *_: (p, 0, 0))
    per_head = pl.BlockSpec((2, LIVE, 256), lambda p, *_: (p, 0, 0))
    whole = lambda *shape: pl.BlockSpec(shape, lambda p, *_: (0,) * len(shape))
    return pl.pallas_call(
        attn_fwd_body,
        grid_spec=pltpu.PrefetchScalarGridSpec(
            num_scalar_prefetch=1,
            grid=(pairs,),
            in_specs=[
                whole(LIVE, width),
                whole(1, width),
                whole(1, width),
                whole(3, width, width),
                pl.BlockSpec((2, 64, 256), lambda p, *_: (p, 0, 0)),
            ],
            out_specs=[
                whole(LIVE, width),
                per_head,
                per_head,
                per_pair,
                per_pair,
                per_pair,
                per_pair,
                per_pair,
                pl.BlockSpec((LIVE, LANES), lambda p, *_: (0, p)),
            ],
            scratch_shapes=[
                pltpu.VMEM((3, pairs, LIVE, LANES), F32),
                pltpu.VMEM((BLOCKS, BLOCK, BLOCK), BF16),
                pltpu.VMEM((BLOCKS - 1, REACH, BLOCK), BF16),
                pltpu.VMEM((2, BLOCK, 256), F32),
            ],
        ),
        out_shape=[
            jax.ShapeDtypeStruct((LIVE, width), BF16),
            jax.ShapeDtypeStruct((heads, LIVE, 256), BF16),
            jax.ShapeDtypeStruct((heads, LIVE, 256), BF16),
            jax.ShapeDtypeStruct((pairs, LIVE, LANES), F32),
            jax.ShapeDtypeStruct((pairs, LIVE, LANES), F32),
            jax.ShapeDtypeStruct((pairs, LIVE, LANES), BF16),
            jax.ShapeDtypeStruct((pairs, LIVE, LANES), F32),
            jax.ShapeDtypeStruct((pairs, LIVE, LANES), F32),
            jax.ShapeDtypeStruct((LIVE, width), BF16),
        ],
        compiler_params=params_for(48),
        cost_estimate=cost(1.2e10, 2e7, 4e6),
        name="attn_forward",
    )(lengths, x, gain, shift, w, fm)


def ff_fwd_body(x_ref, low_ref, wo_ref, gain_ref, shift_ref, up_ref, up_bias_ref, down_ref, down_bias_ref,
                out_ref, mid_ref, normed_ref, act_ref, slope_ref):
    step = pl.program_id(0)
    mid_ref[...] = x_ref[...]

    @pl.when(step < BLOCKS)
    def _():
        mid_ref[...] += dot(low_ref[...], wo_ref[...])

    mid = mid_ref[...]
    unit, _ = normalize(mid)
    normed = (unit * gain_ref[...] + shift_ref[...]).astype(BF16)
    normed_ref[...] = normed
    total = mid + down_bias_ref[...]
    hidden = up_ref.shape[1]
    for first in range(0, hidden, 512):
        cols = slice(first, first + 512)
        pre = dot(normed, up_ref[:, cols]) + up_bias_ref[:, cols]
        lifted = 0.5 + 0.5 * lax.erf(pre * math.sqrt(0.5))
        slope_ref[:, cols] = lifted + pre * (jnp.exp2(pre * pre * (-0.5 * LOG2E)) * (1.0 / math.sqrt(2.0 * math.pi)))
        act = (pre * lifted).astype(BF16)
        act_ref[:, cols] = act
        total = total + dot(act, down_ref[cols, :])
    out_ref[...] = total


def ff_fwd(x, low, wo, gain, shift, up, up_bias, down, down_bias):
    length, width = x.shape
    hidden = up.shape[1]
    rows = lambda n: pl.BlockSpec((BLOCK, n), lambda i: (i, 0))
    whole = lambda *shape: pl.BlockSpec(shape, lambda i: (0,) * len(shape))
    return pl.pallas_call(
        ff_fwd_body,
        grid=(length // BLOCK,),
        in_specs=[
            rows(width),
            pl.BlockSpec((BLOCK, width), lambda i: (jnp.minimum(i, BLOCKS - 1), 0)),
            whole(width, width),
            whole(1, width),
            whole(1, width),
            whole(width, hidden),
            whole(1, hidden),
            whole(hidden, width),
            whole(1, width),
        ],
        out_specs=[rows(width), rows(width), rows(width), rows(hidden), rows(hidden)],
        out_shape=[
            jax.ShapeDtypeStruct((length, width), F32),
            jax.ShapeDtypeStruct((length, width), F32),
            jax.ShapeDtypeStruct((length, width), BF16),
            jax.ShapeDtypeStruct((length, hidden), BF16),
            jax.ShapeDtypeStruct((length, hidden), F32),
        ],
        compiler_params=params_for(48),
        cost_estimate=cost(2 * length * width * (width + 2 * hidden), 3e7, 2 * length * hidden),
        name="ff_forward",
    )(x, low, wo, gain, shift, up, up_bias, down, down_bias)


def ff_bwd_body(g_ref, slope_ref, mid_ref, gain_ref, up_ref, down_ref, wo_ref,
                g_low_ref, pre_low_ref, mid_g_ref, mid_low_ref, att_g_ref, small_ref, up_bias_ref):
    step = pl.program_id(0)

    @pl.when(step == 0)
    def _():
        small_ref[...] = jnp.zeros_like(small_ref)
        up_bias_ref[...] = jnp.zeros_like(up_bias_ref)

    grad = g_ref[...]
    g_low = grad.astype(BF16)
    g_low_ref[...] = g_low
    back = jnp.zeros(grad.shape, F32)
    hidden = up_ref.shape[1]
    for first in range(0, hidden, 512):
        cols = slice(first, first + 512)
        pre_low = (dot_nt(g_low, down_ref[cols, :]) * slope_ref[:, cols]).astype(BF16)
        pre_low_ref[:, cols] = pre_low
        up_bias_ref[:, cols] += jnp.sum(pre_low.astype(F32), axis=0, keepdims=True)
        back = back + dot_nt(pre_low, up_ref[:, cols])
    unit, rstd = normalize(mid_ref[...])
    mid_g = grad + norm_pull(back, gain_ref[...], unit, rstd)
    mid_g_ref[...] = mid_g
    mid_low = mid_g.astype(BF16)
    mid_low_ref[...] = mid_low
    small_ref[0:1, :] += jnp.sum(back * unit, axis=0, keepdims=True)
    small_ref[1:2, :] += jnp.sum(back, axis=0, keepdims=True)
    small_ref[2:3, :] += jnp.sum(g_low.astype(F32), axis=0, keepdims=True)

    @pl.when(step < BLOCKS)
    def _():
        att_g_ref[...] = dot_nt(mid_low, wo_ref[...])


def ff_bwd(grad, slope, mid, gain, up, down, wo):
    length, width = grad.shape
    hidden = up.shape[1]
    rows = lambda n: pl.BlockSpec((BLOCK, n), lambda i: (i, 0))
    whole = lambda *shape: pl.BlockSpec(shape, lambda i: (0,) * len(shape))
    return pl.pallas_call(
        ff_bwd_body,
        grid=(length // BLOCK,),
        in_specs=[
            rows(width),
            rows(hidden),
            rows(width),
            whole(1, width),
            whole(width, hidden),
            whole(hidden, width),
            whole(width, width),
        ],
        out_specs=[
            rows(width),
            rows(hidden),
            rows(width),
            rows(width),
            pl.BlockSpec((BLOCK, width), lambda i: (jnp.minimum(i, BLOCKS - 1), 0)),
            whole(8, width),
            whole(1, hidden),
        ],
        out_shape=[
            jax.ShapeDtypeStruct((length, width), BF16),
            jax.ShapeDtypeStruct((length, hidden), BF16),
            jax.ShapeDtypeStruct((length, width), F32),
            jax.ShapeDtypeStruct((length, width), BF16),
            jax.ShapeDtypeStruct((LIVE, width), F32),
            jax.ShapeDtypeStruct((8, width), F32),
            jax.ShapeDtypeStruct((1, hidden), F32),
        ],
        compiler_params=params_for(48),
        cost_estimate=cost(2 * length * width * (width + 2 * hidden), 3e7),
        name="ff_backward",
    )(grad, slope, mid, gain, up, down, wo)


def attn_bwd_body(len_ref, att_g_ref, att_ref, rden_ref, phi_q_ref, phi_k_ref, uq_ref, uk_ref, v_ref, fm_ref,
                  dq_ref, dk_ref, dv_ref, own_ref, before_ref, own_t_ref, before_t_ref,
                  x_ref, y_ref, dn_ref, d_phi_q, d_phi_k, d_v, raw_ref):
    step = pl.program_id(0)

    @pl.when(step == 0)
    def _():
        fill_masks(len_ref, own_ref, before_ref, True)
        fill_masks(len_ref, own_t_ref, before_t_ref, False)

    lane = lax.broadcasted_iota(jnp.int32, (BLOCK, LANES), 1) < 64
    one = jnp.ones((BLOCK, LANES), BF16)
    for b in range(BLOCKS):
        rows = pl.ds(b * BLOCK, BLOCK)
        position = lax.broadcasted_iota(jnp.int32, (BLOCK, LANES), 0) + b * BLOCK
        dn = jnp.where(position < token_count(len_ref), att_g_ref[rows, :] * rden_ref[0, rows, :], 0.0)
        turned = pltpu.roll(-(dn * att_ref[0, rows, :]), 64, 1)
        dn_ref[rows, :] = dn.astype(BF16)
        v_low = v_ref[0, rows, :]
        for head in range(2):
            first = lane if head == 0 else jnp.logical_not(lane)
            high, low = split_two(jnp.where(first, dn, turned))
            x_ref[head, rows, :] = jnp.concatenate([high, low], axis=1)
            y = jnp.where(first, v_low.astype(F32), 1.0).astype(BF16)
            y_ref[head, rows, :] = jnp.concatenate([y, y], axis=1)
    for head in range(2):
        for b in range(BLOCKS):
            rows = pl.ds(b * BLOCK, BLOCK)
            x, y = x_ref[head, rows, :], y_ref[head, rows, :]
            phi_q, phi_k = phi_q_ref[head, rows, :], phi_k_ref[head, rows, :]
            d_kernel = dot_nt(x, y).astype(BF16) * own_ref[b]
            d_phi_q[rows, :] = dot(d_kernel, phi_k)
            d_kernel_t = dot_nt(y, x).astype(BF16) * own_t_ref[b]
            d_phi_k[rows, :] = dot(d_kernel_t, phi_q)
            kernel_t = dot_nt(phi_k, phi_q).astype(BF16) * own_t_ref[b]
            d_v[head, rows, :] = dot(kernel_t, dn_ref[rows, :])
            if b > 0:
                earlier = pl.ds((b - 1) * BLOCK, BLOCK)
                top = pl.ds(b * BLOCK, REACH)
                bottom = pl.ds(b * BLOCK - REACH, REACH)
                d_kernel = dot_nt(x_ref[head, top, :], y_ref[head, earlier, :]).astype(BF16) * before_ref[b - 1]
                d_phi_q[top, :] += dot(d_kernel, phi_k_ref[head, earlier, :])
                d_kernel_t = dot_nt(y_ref[head, bottom, :], x).astype(BF16) * before_t_ref[b - 1]
                d_phi_k[bottom, :] += dot(d_kernel_t, phi_q)
                kernel_t = dot_nt(phi_k_ref[head, bottom, :], phi_q).astype(BF16) * before_t_ref[b - 1]
                d_v[head, bottom, :] += dot(kernel_t, dn_ref[rows, :])
        high, low = split_two(fm_ref[head])
        stacked = jnp.concatenate([high, low, jnp.ones((LANES, 256), BF16)], axis=0)
        for which, d_phi, phi_ref in ((0, d_phi_q, phi_q_ref), (1, d_phi_k, phi_k_ref)):
            for b in range(BLOCKS):
                rows = pl.ds(b * BLOCK, BLOCK)
                d_projected = (d_phi[rows, :] * phi_ref[head, rows, :].astype(F32)).astype(BF16)
                raw_ref[which, head, rows, :] = dot_nt(d_projected, stacked)
    for b in range(BLOCKS):
        rows = pl.ds(b * BLOCK, BLOCK)
        for which, u_ref, out_ref in ((0, uq_ref, dq_ref), (1, uk_ref, dk_ref)):
            parts = []
            for head in range(2):
                raw = raw_ref[which, head, rows, :LANES]
                parts.append(raw + pltpu.roll(raw, 64, 1))
            along = jnp.where(lane, parts[0], parts[1])
            total = jnp.where(lane, raw_ref[which, 0, rows, LANES:], raw_ref[which, 1, rows, LANES:])
            grad = along * (64.0 ** (-0.25)) - u_ref[0, rows, :] * total * 0.125
            out_ref[rows, :] = grad.astype(BF16)
        dv_ref[rows, :] = jnp.where(lane, d_v[0, rows, :], d_v[1, rows, :]).astype(BF16)


def attn_bwd(lengths, att_g, att, rden, phi_q, phi_k, uq, uk, v, fm):
    heads = fm.shape[0]
    pairs = heads // 2
    width = att_g.shape[1]
    per_pair = pl.BlockSpec((1, LIVE, LANES), lambda p, *_: (p, 0, 0))
    per_head = pl.BlockSpec((2, LIVE, 256), lambda p, *_: (p, 0, 0))
    columns = pl.BlockSpec((LIVE, LANES), lambda p, *_: (0, p))
    return pl.pallas_call(
        attn_bwd_body,
        grid_spec=pltpu.PrefetchScalarGridSpec(
            num_scalar_prefetch=1,
            grid=(pairs,),
            in_specs=[columns, per_pair, per_pair, per_head, per_head, per_pair, per_pair, per_pair,
                      pl.BlockSpec((2, 64, 256), lambda p, *_: (p, 0, 0))],
            out_specs=[columns] * 3,
            scratch_shapes=[
                pltpu.VMEM((BLOCKS, BLOCK, BLOCK), BF16),
                pltpu.VMEM((BLOCKS - 1, REACH, BLOCK), BF16),
                pltpu.VMEM((BLOCKS, BLOCK, BLOCK), BF16),
                pltpu.VMEM((BLOCKS - 1, REACH, BLOCK), BF16),
                pltpu.VMEM((2, LIVE, 256), BF16),
                pltpu.VMEM((2, LIVE, 256), BF16),
                pltpu.VMEM((LIVE, LANES), BF16),
                pltpu.VMEM((LIVE, 256), F32),
                pltpu.VMEM((LIVE, 256), F32),
                pltpu.VMEM((2, LIVE, LANES), F32),
                pltpu.VMEM((2, 2, LIVE, 256), F32),
            ],
        ),
        out_shape=[jax.ShapeDtypeStruct((LIVE, width), BF16)] * 3,
        compiler_params=params_for(48),
        cost_estimate=cost(3e10, 2e7),
        name="attn_backward",
    )(lengths, att_g, att, rden, phi_q, phi_k, uq, uk, v, fm)


def input_bwd_body(dq_ref, dk_ref, dv_ref, w_ref, x_ref, gain_ref, mid_g_ref, out_ref, small_ref):
    step = pl.program_id(0)

    @pl.when(step == 0)
    def _():
        small_ref[...] = jnp.zeros_like(small_ref)

    @pl.when(step < BLOCKS)
    def _():
        back = dot_nt(dq_ref[...], w_ref[0]) + dot_nt(dk_ref[...], w_ref[1]) + dot_nt(dv_ref[...], w_ref[2])
        unit, rstd = normalize(x_ref[...])
        out_ref[...] = mid_g_ref[...] + norm_pull(back, gain_ref[...], unit, rstd)
        small_ref[0:1, :] += jnp.sum(back * unit, axis=0, keepdims=True)
        small_ref[1:2, :] += jnp.sum(back, axis=0, keepdims=True)

    @pl.when(step >= BLOCKS)
    def _():
        out_ref[...] = mid_g_ref[...]


def input_bwd(dq, dk, dv, w, x, gain, mid_g):
    length, width = x.shape
    rows = pl.BlockSpec((BLOCK, width), lambda i: (i, 0))
    live = pl.BlockSpec((BLOCK, width), lambda i: (jnp.minimum(i, BLOCKS - 1), 0))
    whole = lambda *shape: pl.BlockSpec(shape, lambda i: (0,) * len(shape))
    return pl.pallas_call(
        input_bwd_body,
        grid=(length // BLOCK,),
        in_specs=[live, live, live, whole(3, width, width), rows, whole(1, width), rows],
        out_specs=[rows, whole(8, width)],
        out_shape=[jax.ShapeDtypeStruct((length, width), F32), jax.ShapeDtypeStruct((8, width), F32)],
        compiler_params=params_for(48),
        cost_estimate=cost(6 * LIVE * width * width, 1e7),
        name="input_backward",
    )(dq, dk, dv, w, x, gain, mid_g)


def down_grad_body(id_ref, act_ref, g_ref, out_ref):
    me, here = id_ref[0], id_ref[1]
    group, quarters, rows, _ = out_ref.shape
    total = dot_tn(act_ref[...], g_ref[...])
    for part in range(group):
        for quarter in range(quarters):
            out_ref[part ^ (me & (group - 1)), quarter ^ here] = total[part * rows : part * rows + rows, quarter * LANES : quarter * LANES + LANES]


def down_grad(ids, act, g_low, parts, quarters):
    length, hidden = act.shape
    width = g_low.shape[1]
    steps = 4
    group = parts // steps
    rows = hidden // parts
    return pl.pallas_call(
        down_grad_body,
        grid_spec=pltpu.PrefetchScalarGridSpec(
            num_scalar_prefetch=1,
            grid=(steps,),
            in_specs=[
                pl.BlockSpec((length, hidden // steps), lambda i, ids: (0, i)),
                pl.BlockSpec((length, width), lambda i, ids: (0, 0)),
            ],
            out_specs=pl.BlockSpec((group, quarters, rows, LANES), lambda i, ids: (i ^ (ids[0] // group), 0, 0, 0)),
        ),
        out_shape=jax.ShapeDtypeStruct((parts, quarters, rows, LANES), F32),
        compiler_params=params_for(48),
        cost_estimate=cost(2 * length * hidden * width, 1e7),
        name="down_gradient",
    )(ids, act, g_low)


def up_grad_body(id_ref, normed_ref, pre_ref, out_ref):
    me = id_ref[0]
    parts, _, rows, _ = out_ref.shape
    total = dot_tn(normed_ref[...], pre_ref[...])
    per_tile = total.shape[0] // rows
    for part in range(parts):
        tile, first = part // per_tile, (part % per_tile) * rows
        out_ref[part ^ me, 0] = total[first : first + rows, tile * LANES : tile * LANES + LANES]


def up_grad(ids, normed, pre_low, parts, quarters):
    length, hidden = pre_low.shape
    width = normed.shape[1]
    rows = width * (hidden // quarters // LANES) // parts
    return pl.pallas_call(
        up_grad_body,
        grid_spec=pltpu.PrefetchScalarGridSpec(
            num_scalar_prefetch=1,
            grid=(quarters,),
            in_specs=[
                pl.BlockSpec((length, width), lambda i, ids: (0, 0)),
                pl.BlockSpec((length, hidden // quarters), lambda i, ids: (0, i)),
            ],
            out_specs=pl.BlockSpec((parts, 1, rows, LANES), lambda i, ids: (0, i ^ ids[1], 0, 0)),
        ),
        out_shape=jax.ShapeDtypeStruct((parts, quarters, rows, LANES), F32),
        compiler_params=params_for(48),
        cost_estimate=cost(2 * length * hidden * width, 1e7),
        name="up_gradient",
    )(ids, normed, pre_low)


def square_grad_body(id_ref, left_ref, *refs):
    right_refs, out_ref = refs[:-1], refs[-1]
    me, here = id_ref[0], id_ref[1]
    parts, quarters, rows, _ = out_ref.shape
    for which, right_ref in enumerate(right_refs):
        total = dot_tn(left_ref[...], right_ref[...])
        unit = math.gcd(total.shape[0], rows)
        for first in range(0, total.shape[0], unit):
            part, offset = divmod(which * total.shape[0] + first, rows)
            for quarter in range(quarters):
                out_ref[part ^ me, quarter ^ here, offset : offset + unit, :] = total[first : first + unit, quarter * LANES : quarter * LANES + LANES]


def square_grad(ids, left, rights, parts, quarters, name):
    length, width = left.shape
    rows = len(rights) * width // parts
    whole = pl.BlockSpec((length, width), lambda i, ids: (0, 0))
    return pl.pallas_call(
        square_grad_body,
        grid_spec=pltpu.PrefetchScalarGridSpec(
            num_scalar_prefetch=1,
            grid=(1,),
            in_specs=[whole] * (1 + len(rights)),
            out_specs=pl.BlockSpec((parts, quarters, rows, LANES), lambda i, ids: (0, 0, 0, 0)),
        ),
        out_shape=jax.ShapeDtypeStruct((parts, quarters, rows, LANES), F32),
        compiler_params=params_for(48),
        cost_estimate=cost(2 * length * width * width * len(rights), 6e6),
        name=name,
    )(ids, left, *rights)


def forward_layer(x, weights, fm, lengths):
    gains, shifts, w, wo, up, up_bias, down, down_bias = weights
    normed, phi_q, phi_k, uq, uk, v, att, rden, low = attn_fwd(lengths, x, gains[0:1], shifts[0:1], w, fm)
    out, mid, normed_two, act, slope = ff_fwd(x, low, wo, gains[1:2], shifts[1:2], up, up_bias[None], down, down_bias[None])
    return out, (x, normed, phi_q, phi_k, uq, uk, v, att, rden, low, mid, normed_two, act, slope)


def backward_layer(grad, kept, weights, fm, lengths, ids, parts, quarters, emit):
    gains, shifts, w, wo, up, up_bias, down, down_bias = weights
    x, normed, phi_q, phi_k, uq, uk, v, att, rden, low, mid, normed_two, act, slope = kept
    g_low, pre_low, mid_g, mid_low, att_g, small_two, up_bias_g = ff_bwd(grad, slope, mid, gains[1:2], up, down, wo)
    emit("down", down_grad(ids, act, g_low, parts, quarters))
    emit("up", up_grad(ids, normed_two, pre_low, parts, quarters))
    emit("out", square_grad(ids, low, [mid_low[:LIVE]], parts, quarters, "out_gradient"))
    dq, dk, dv = attn_bwd(lengths, att_g, att, rden, phi_q, phi_k, uq, uk, v, fm)
    emit("qkv", square_grad(ids, normed, [dq, dk, dv], parts, quarters, "qkv_gradient"))
    grad_in, small_one = input_bwd(dq, dk, dv, w, x, gains[0:1], mid_g)
    smalls = jnp.concatenate([small_one[0], small_two[0], small_one[1], small_two[1], up_bias_g[0], small_two[2]])
    return grad_in, smalls


def swap(block, axis_name, bit):
    return lax.ppermute(block, axis_name, [(i, i ^ bit) for i in range(lax.axis_size(axis_name))])


def halve(block, names, order, axis_name):
    names = list(names)
    for bit in order:
        where = names.index(bit)
        kept = lax.index_in_dim(block, 0, where, keepdims=False)
        block = kept + swap(lax.index_in_dim(block, 1, where, keepdims=False), axis_name, bit)
        names.remove(bit)
    return block


def double(block, names, order, axis_name):
    names_now = []
    for bit in reversed(order):
        names_now.append(bit)
        names_now.sort(key=names.index)
        block = jnp.stack([block, swap(block, axis_name, bit)], axis=names_now.index(bit))
    return block


def bits_of(extent):
    return [1 << i for i in range(extent.bit_length() - 1)]


def exchange(block):
    parts, quarters, rows, _ = block.shape
    dp_bits, batch_bits = bits_of(parts), bits_of(quarters)
    near, far = dp_bits[0], dp_bits[1:]
    block = block.reshape((2,) * len(dp_bits) + block.shape[1:])
    block = halve(block, dp_bits, [near], "dp")
    half = rows // 2
    upper = halve(block[..., :half, :], far, far, "dp")
    lower = halve(block[..., half:, :], far, far[::-1], "dp")
    block = jnp.concatenate([upper, lower], axis=-2)
    block = block.reshape((2,) * len(batch_bits) + block.shape[1:])
    block = halve(block, batch_bits[::-1], batch_bits, "batch")
    upper = double(block[:half], far, far, "dp")
    lower = double(block[half:], far, far[::-1], "dp")
    block = jnp.concatenate([upper, lower], axis=-2)
    block = double(block[None], [near], [near], "dp") if not far else jnp.stack([block, swap(block, "dp", near)])
    return block.reshape(parts, rows, LANES)


def unpack_body(id_ref, *refs):
    count = len(refs) // 2
    for which in range(count):
        refs[count + which][...] = refs[which][...].reshape(refs[count + which].shape)


def unpack(ids, pieces, width, quarter_hidden):
    parts = pieces[0]["qkv"].shape[0]
    layers = len(pieces)
    names = ("qkv", "out", "up", "down")
    arrays, in_specs, out_specs, out_shape = [], [], [], []
    for layer in range(layers):
        for name in names:
            array = pieces[layer][name]
            arrays.append(array)
            in_specs.append(pl.BlockSpec((1,) + array.shape[1:], lambda i, ids: (i ^ ids[0], 0, 0)))
            rows = array.shape[1]
            if name == "up":
                per_tile = width // rows
                out_specs.append(pl.BlockSpec((rows, LANES), lambda i, ids, per_tile=per_tile: (i % per_tile, i // per_tile)))
                out_shape.append(jax.ShapeDtypeStruct((width, quarter_hidden), F32))
            else:
                out_specs.append(pl.BlockSpec((rows, LANES), lambda i, ids: (i, 0)))
                out_shape.append(jax.ShapeDtypeStruct((rows * parts, LANES), F32))
    got = pl.pallas_call(
        unpack_body,
        grid_spec=pltpu.PrefetchScalarGridSpec(num_scalar_prefetch=1, grid=(parts,), in_specs=in_specs, out_specs=out_specs),
        out_shape=out_shape,
        compiler_params=params_for(48),
        cost_estimate=cost(0, 2 * sum(a.size * 4 for a in arrays)),
        name="unpack",
    )(ids, *arrays)
    return [jnp.stack([got[layer * len(names) + which] for layer in range(layers)]) for which in range(len(names))]


def reverse_bits(value, extent):
    bits = bits_of(extent)
    return sum(((value // bit) % 2) * (extent // (2 * bit)) for bit in bits)


def per_device(activations_in, gains, shifts, qkv_weights, out_weights, up_weights, up_bias, down_weights, down_bias, feature_maps, lengths, cotangent):
    layers, _, width = gains.shape
    hidden = up_bias.shape[1]
    parts, quarters = lax.axis_size("dp"), lax.axis_size("batch")
    here = lax.axis_index("batch")
    ids = jnp.stack([reverse_bits(lax.axis_index("dp"), parts), here]).astype(jnp.int32)
    params = (gains, shifts, qkv_weights, out_weights, up_weights, up_bias, down_weights, down_bias)
    weights = [tuple(param[layer] for param in params) for layer in range(layers)]
    proteins = lengths[0]
    values, kept = activations_in[0], []
    for layer in range(layers):
        values, saved = forward_layer(values, weights[layer], feature_maps[layer], proteins)
        kept.append(saved)
    grad, smalls, pieces = cotangent[0], [None] * layers, [{} for _ in range(layers)]
    for layer in reversed(range(layers)):
        def emit(name, block, layer=layer):
            pieces[layer][name] = exchange(block)

        grad, smalls[layer] = backward_layer(grad, kept[layer], weights[layer], feature_maps[layer], proteins, ids, parts, quarters, emit)
    small = lax.psum(jnp.stack(smalls), ("dp", "batch"))

    def own(first, *lead):
        count = math.prod(lead)
        piece = small[:, first : first + count].reshape((layers,) + lead[:-1] + (quarters, lead[-1] // quarters))
        return lax.dynamic_index_in_dim(piece, here, axis=piece.ndim - 2, keepdims=False)

    qkv, out, up, down = unpack(ids, pieces, width, hidden // quarters)
    return (
        values[None],
        grad[None],
        own(0, 2, width),
        own(2 * width, 2, width),
        qkv.reshape(layers, 3, width, LANES),
        out,
        up,
        own(4 * width, hidden),
        down,
        own(4 * width + hidden, width),
    )


def solution(mesh):
    rows = P(("dp", "batch"), None, None)
    return jax.shard_map(
        per_device,
        mesh=mesh,
        in_specs=(rows,) + (P(),) * 9 + (P(("dp", "batch"), None), rows),
        out_specs=(
            rows,
            rows,
            P(None, None, "batch"),
            P(None, None, "batch"),
            P(None, None, None, "batch"),
            P(None, None, "batch"),
            P(None, None, "batch"),
            P(None, "batch"),
            P(None, None, "batch"),
            P(None, "batch"),
        ),
        check_vma=False,
    )
```

```python
import functools
import math

import jax
import jax.numpy as jnp
from jax import lax
from jax.experimental import pallas as pl
from jax.experimental.pallas import tpu as pltpu
from jax.sharding import PartitionSpec as P

BLOCK = 256
BLOCKS = 3
LIVE = BLOCK * BLOCKS
REACH = 160
LANES = 128
NDOC = 6
MIB = 1 << 20
F32 = jnp.float32
BF16 = jnp.bfloat16
LOG2E = 1.4426950408889634
NT = (((1,), (1,)), ((), ()))


def dot(a, b):
    return jnp.dot(a, b, preferred_element_type=F32)


def dot_nt(a, b):
    return lax.dot_general(a, b, NT, preferred_element_type=F32)


def params_for(mib):
    return pltpu.CompilerParams(vmem_limit_bytes=mib * MIB)


def call(body, after, *, grid, in_specs, out_specs, out_shape, prefetch, operands, scratch=(), aliases=(), mib=60, us=3.0, name):
    scalars, count = len(prefetch), len(after)

    def ordered(*refs):
        body(*refs[:scalars], *refs[scalars + count :])

    return pl.pallas_call(
        ordered,
        grid_spec=pltpu.PrefetchScalarGridSpec(
            num_scalar_prefetch=scalars,
            grid=grid,
            in_specs=[pl.BlockSpec(memory_space=pl.ANY)] * count + list(in_specs),
            out_specs=out_specs,
            scratch_shapes=list(scratch),
        ),
        out_shape=out_shape,
        input_output_aliases={scalars + count + operand: output for operand, output in aliases},
        compiler_params=params_for(mib),
        cost_estimate=pl.CostEstimate(flops=int(us * 1.15e9), bytes_accessed=0, transcendentals=0),
        name=name,
    )(*prefetch, *after, *operands)


def constant(*shape):
    return pl.BlockSpec(shape, lambda *_: (0,) * len(shape), pipeline_mode=pl.Buffered(1))


def resident(*shape):
    return pl.BlockSpec(shape, lambda *_: (0,) * len(shape))


def of_layer(layer, array):
    return pl.BlockSpec((None,) + array.shape[1:], lambda *_: (layer,) + (0,) * (array.ndim - 1), pipeline_mode=pl.Buffered(1))


def normalize(values):
    centered = values - jnp.mean(values, axis=-1, keepdims=True)
    rstd = lax.rsqrt(jnp.mean(centered * centered, axis=-1, keepdims=True) + 1e-05)
    return centered * rstd, rstd


def norm_pull(grad, gain, unit, rstd):
    p = grad * gain
    return rstd * (p - jnp.mean(p, axis=-1, keepdims=True) - unit * jnp.mean(p * unit, axis=-1, keepdims=True))


def split_two(values):
    high = values.astype(BF16)
    return high, (values - high.astype(F32)).astype(BF16)


def protein_ids(len_ref, position):
    bound = jnp.int32(0)
    ids = jnp.zeros(position.shape, jnp.int32)
    for j in range(NDOC):
        bound = bound + len_ref[j]
        ids = ids + (position >= bound).astype(jnp.int32)
    return ids


def token_count(len_ref):
    total = jnp.int32(0)
    for j in range(NDOC):
        total = total + len_ref[j]
    return total


def pair_mask(len_ref, shape, first_row, first_col, causal_rows):
    rows = lax.broadcasted_iota(jnp.int32, shape, 0) + first_row
    cols = lax.broadcasted_iota(jnp.int32, shape, 1) + first_col
    same = protein_ids(len_ref, rows) == protein_ids(len_ref, cols)
    ordered = (rows >= cols) if causal_rows else (cols >= rows)
    return jnp.where(same & ordered, 1.0, 0.0).astype(BF16)


def fill_masks(len_ref, own_ref, before_ref, causal_rows):
    for b in range(BLOCKS):
        own_ref[b] = pair_mask(len_ref, (BLOCK, BLOCK), b * BLOCK, b * BLOCK, causal_rows)
    for b in range(1, BLOCKS):
        if causal_rows:
            before_ref[b - 1] = pair_mask(len_ref, (REACH, BLOCK), b * BLOCK, (b - 1) * BLOCK, True)
        else:
            before_ref[b - 1] = pair_mask(len_ref, (REACH, BLOCK), b * BLOCK - REACH, b * BLOCK, False)


def attn_fwd_body(layer, len_ref, x_ref, gain_ref, shift_ref, w_ref, fm_ref, normed_t_ref, phi_q_ref, phi_k_ref, uq_ref, uk_ref,
                  v_ref, att_ref, rden_ref, low_ref, low_t_ref, normed_ref, proj_ref, own_ref, before_ref, num_ref):
    step = pl.program_id(0)

    @pl.when(step == 0)
    def _():
        fill_masks(len_ref, own_ref, before_ref, True)
        for b in range(BLOCKS):
            rows = pl.ds(b * BLOCK, BLOCK)
            unit, _ = normalize(x_ref[rows, :])
            normed = (unit * gain_ref[layer, 0:1, :] + shift_ref[layer, 0:1, :]).astype(BF16)
            normed_ref[rows, :] = normed
            normed_t_ref[:, rows] = normed.T
        for j in range(3):
            for half in range(2):
                got = dot(normed_ref[...], w_ref[j, :, half * 256 : half * 256 + 256])
                proj_ref[j, 2 * half] = got[:, :LANES]
                proj_ref[j, 2 * half + 1] = got[:, LANES:]

    lane = lax.broadcasted_iota(jnp.int32, (BLOCK, LANES), 1) < 64
    uq_ref[0] = proj_ref[0, step]
    uk_ref[0] = proj_ref[1, step]
    v_ref[0] = proj_ref[2, step].astype(BF16)
    for which, phi_ref in ((0, phi_q_ref), (1, phi_k_ref)):
        for head in range(2):
            high, low = split_two(fm_ref[head] * (64.0 ** (-0.25) * LOG2E))
            stacked = jnp.concatenate([high, low, high, low], axis=0)
            for b in range(BLOCKS):
                rows = pl.ds(b * BLOCK, BLOCK)
                u = proj_ref[which, step, rows, :]
                turned = pltpu.roll(u, 64, 1)
                twice = jnp.where(lane, u, turned) if head == 0 else jnp.where(lane, turned, u)
                squares = jnp.sum(twice * twice, axis=-1, keepdims=True) * (LOG2E / 32.0) + 4.0
                u_high, u_low = split_two(twice)
                projected = dot(jnp.concatenate([u_high, u_low], axis=1), stacked)
                phi_ref[head, rows, :] = jnp.exp2(projected - squares).astype(BF16)
    ones = jnp.ones((BLOCK, LANES), BF16)
    for b in range(BLOCKS):
        rows = pl.ds(b * BLOCK, BLOCK)
        v_now = jnp.concatenate([v_ref[0, rows, :], ones], axis=1)
        for head in range(2):
            weights = dot_nt(phi_q_ref[head, rows, :], phi_k_ref[head, rows, :]).astype(BF16) * own_ref[b]
            num_ref[head] = dot(weights, v_now)
            if b > 0:
                earlier = pl.ds((b - 1) * BLOCK, BLOCK)
                v_before = jnp.concatenate([v_ref[0, earlier, :], ones], axis=1)
                weights = dot_nt(phi_q_ref[head, pl.ds(b * BLOCK, REACH), :], phi_k_ref[head, earlier, :])
                num_ref[head, :REACH, :] += dot(weights.astype(BF16) * before_ref[b - 1], v_before)
        rden = 1.0 / jnp.where(lane, num_ref[0, :, LANES:], num_ref[1, :, LANES:])
        attended = jnp.where(lane, num_ref[0, :, :LANES], num_ref[1, :, :LANES]) * rden
        position = lax.broadcasted_iota(jnp.int32, (BLOCK, LANES), 0) + b * BLOCK
        attended = jnp.where(position < token_count(len_ref), attended, 0.0)
        rden_ref[0, rows, :] = rden
        att_ref[0, rows, :] = attended
        low = attended.astype(BF16)
        low_ref[rows, :] = low
        low_t_ref[:, rows] = low.T


def attn_fwd(layer, lengths, x, gains, shifts, w, fm, after=()):
    width = x.shape[1]
    heads = fm.shape[1]
    pairs = heads // 2
    per_pair = pl.BlockSpec((1, LIVE, LANES), lambda p, *_: (p, 0, 0))
    per_head = pl.BlockSpec((2, LIVE, 256), lambda p, *_: (p, 0, 0))
    return call(
        functools.partial(attn_fwd_body, layer),
        after,
        grid=(pairs,),
        prefetch=[lengths],
        operands=[x, gains, shifts, w, fm],
        in_specs=[
            constant(LIVE, width),
            constant(*gains.shape),
            constant(*shifts.shape),
            of_layer(layer, w),
            pl.BlockSpec((None, 2) + fm.shape[2:], lambda p, *_: (layer, p, 0, 0)),
        ],
        out_specs=[resident(width, LIVE), per_head, per_head, per_pair, per_pair, per_pair, per_pair, per_pair,
                   pl.BlockSpec((LIVE, LANES), lambda p, *_: (0, p)), pl.BlockSpec((LANES, LIVE), lambda p, *_: (p, 0))],
        scratch=[
            pltpu.VMEM((LIVE, width), BF16),
            pltpu.VMEM((3, pairs, LIVE, LANES), F32),
            pltpu.VMEM((BLOCKS, BLOCK, BLOCK), BF16),
            pltpu.VMEM((BLOCKS - 1, REACH, BLOCK), BF16),
            pltpu.VMEM((2, BLOCK, 256), F32),
        ],
        out_shape=[
            jax.ShapeDtypeStruct((width, LIVE), BF16),
            jax.ShapeDtypeStruct((heads, LIVE, 256), BF16),
            jax.ShapeDtypeStruct((heads, LIVE, 256), BF16),
            jax.ShapeDtypeStruct((pairs, LIVE, LANES), F32),
            jax.ShapeDtypeStruct((pairs, LIVE, LANES), F32),
            jax.ShapeDtypeStruct((pairs, LIVE, LANES), BF16),
            jax.ShapeDtypeStruct((pairs, LIVE, LANES), F32),
            jax.ShapeDtypeStruct((pairs, LIVE, LANES), F32),
            jax.ShapeDtypeStruct((LIVE, width), BF16),
            jax.ShapeDtypeStruct((width, LIVE), BF16),
        ],
        us=15.0,
        name="attn_forward",
    )


def gelu_terms(pre):
    lifted = 0.5 + 0.5 * lax.erf(pre * math.sqrt(0.5))
    return pre * lifted, lifted + pre * (jnp.exp2(pre * pre * (-0.5 * LOG2E)) * (1.0 / math.sqrt(2.0 * math.pi)))


def ff_fwd_body(layer, x_ref, low_ref, wo_ref, gain_ref, shift_ref, up_ref, up_bias_ref, down_ref, down_bias_ref, out_ref, mid_ref):
    step = pl.program_id(0)
    mid_ref[...] = x_ref[...]

    @pl.when(step < BLOCKS)
    def _():
        mid_ref[...] += dot(low_ref[...], wo_ref[...])

    mid = mid_ref[...]
    unit, _ = normalize(mid)
    normed = (unit * gain_ref[layer, 1:2, :] + shift_ref[layer, 1:2, :]).astype(BF16)
    total = mid + down_bias_ref[layer : layer + 1, :]
    for first in range(0, up_ref.shape[1], 512):
        cols = slice(first, first + 512)
        pre = dot(normed, up_ref[:, cols]) + up_bias_ref[layer : layer + 1, cols]
        act = (pre * (0.5 + 0.5 * lax.erf(pre * math.sqrt(0.5)))).astype(BF16)
        total = total + dot(act, down_ref[cols, :])
    out_ref[...] = total


def ff_fwd(layer, x, low, wo, gains, shifts, up, up_bias, down, down_bias, after=()):
    length, width = x.shape
    rows = pl.BlockSpec((BLOCK, width), lambda i: (i, 0))
    return call(
        functools.partial(ff_fwd_body, layer),
        after,
        grid=(length // BLOCK,),
        prefetch=[],
        operands=[x, low, wo, gains, shifts, up, up_bias, down, down_bias],
        in_specs=[
            rows,
            pl.BlockSpec((BLOCK, width), lambda i: (jnp.minimum(i, BLOCKS - 1), 0)),
            of_layer(layer, wo),
            constant(*gains.shape),
            constant(*shifts.shape),
            of_layer(layer, up),
            constant(*up_bias.shape),
            of_layer(layer, down),
            constant(*down_bias.shape),
        ],
        out_specs=[rows, rows],
        out_shape=[jax.ShapeDtypeStruct((length, width), F32)] * 2,
        us=10.0,
        name="ff_forward",
    )


def attn_bwd_body(len_ref, att_g_ref, att_ref, rden_ref, phi_q_ref, phi_k_ref, uq_ref, uk_ref, v_ref, fm_ref,
                  dq_ref, dk_ref, dv_ref, own_ref, before_ref, own_t_ref, before_t_ref,
                  x_ref, y_ref, dn_ref, d_phi_q, d_phi_k, d_v, raw_ref):
    step = pl.program_id(0)

    @pl.when(step == 0)
    def _():
        fill_masks(len_ref, own_ref, before_ref, True)
        fill_masks(len_ref, own_t_ref, before_t_ref, False)

    lane = lax.broadcasted_iota(jnp.int32, (BLOCK, LANES), 1) < 64
    one = jnp.ones((BLOCK, LANES), BF16)
    for b in range(BLOCKS):
        rows = pl.ds(b * BLOCK, BLOCK)
        position = lax.broadcasted_iota(jnp.int32, (BLOCK, LANES), 0) + b * BLOCK
        dn = jnp.where(position < token_count(len_ref), att_g_ref[rows, :] * rden_ref[0, rows, :], 0.0)
        turned = pltpu.roll(-(dn * att_ref[0, rows, :]), 64, 1)
        dn_ref[rows, :] = dn.astype(BF16)
        v_low = v_ref[0, rows, :]
        for head in range(2):
            first = lane if head == 0 else jnp.logical_not(lane)
            high, low = split_two(jnp.where(first, dn, turned))
            x_ref[head, rows, :] = jnp.concatenate([high, low], axis=1)
            y = jnp.where(first, v_low.astype(F32), 1.0).astype(BF16)
            y_ref[head, rows, :] = jnp.concatenate([y, y], axis=1)
    for head in range(2):
        for b in range(BLOCKS):
            rows = pl.ds(b * BLOCK, BLOCK)
            x, y = x_ref[head, rows, :], y_ref[head, rows, :]
            phi_q, phi_k = phi_q_ref[head, rows, :], phi_k_ref[head, rows, :]
            d_kernel = dot_nt(x, y).astype(BF16) * own_ref[b]
            d_phi_q[rows, :] = dot(d_kernel, phi_k)
            d_kernel_t = dot_nt(y, x).astype(BF16) * own_t_ref[b]
            d_phi_k[rows, :] = dot(d_kernel_t, phi_q)
            kernel_t = dot_nt(phi_k, phi_q).astype(BF16) * own_t_ref[b]
            d_v[head, rows, :] = dot(kernel_t, dn_ref[rows, :])
            if b > 0:
                earlier = pl.ds((b - 1) * BLOCK, BLOCK)
                top = pl.ds(b * BLOCK, REACH)
                bottom = pl.ds(b * BLOCK - REACH, REACH)
                d_kernel = dot_nt(x_ref[head, top, :], y_ref[head, earlier, :]).astype(BF16) * before_ref[b - 1]
                d_phi_q[top, :] += dot(d_kernel, phi_k_ref[head, earlier, :])
                d_kernel_t = dot_nt(y_ref[head, bottom, :], x).astype(BF16) * before_t_ref[b - 1]
                d_phi_k[bottom, :] += dot(d_kernel_t, phi_q)
                kernel_t = dot_nt(phi_k_ref[head, bottom, :], phi_q).astype(BF16) * before_t_ref[b - 1]
                d_v[head, bottom, :] += dot(kernel_t, dn_ref[rows, :])
        high, low = split_two(fm_ref[head])
        stacked = jnp.concatenate([high, low, jnp.ones((LANES, 256), BF16)], axis=0)
        for which, d_phi, phi_ref in ((0, d_phi_q, phi_q_ref), (1, d_phi_k, phi_k_ref)):
            for b in range(BLOCKS):
                rows = pl.ds(b * BLOCK, BLOCK)
                d_projected = (d_phi[rows, :] * phi_ref[head, rows, :].astype(F32)).astype(BF16)
                raw_ref[which, head, rows, :] = dot_nt(d_projected, stacked)
    for b in range(BLOCKS):
        rows = pl.ds(b * BLOCK, BLOCK)
        for which, u_ref, out_ref in ((0, uq_ref, dq_ref), (1, uk_ref, dk_ref)):
            parts = []
            for head in range(2):
                raw = raw_ref[which, head, rows, :LANES]
                parts.append(raw + pltpu.roll(raw, 64, 1))
            along = jnp.where(lane, parts[0], parts[1])
            total = jnp.where(lane, raw_ref[which, 0, rows, LANES:], raw_ref[which, 1, rows, LANES:])
            grad = along * (64.0 ** (-0.25)) - u_ref[0, rows, :] * total * 0.125
            out_ref[rows, :] = grad.astype(BF16)
        dv_ref[rows, :] = jnp.where(lane, d_v[0, rows, :], d_v[1, rows, :]).astype(BF16)


def attn_bwd(layer, lengths, att_g, att, rden, phi_q, phi_k, uq, uk, v, fm, first, count, us, after=()):
    per_pair = pl.BlockSpec((1, LIVE, LANES), lambda p, *_: (first + p, 0, 0))
    per_head = pl.BlockSpec((2, LIVE, 256), lambda p, *_: (first + p, 0, 0))
    return call(
        attn_bwd_body,
        after,
        grid=(count,),
        prefetch=[lengths],
        operands=[att_g, att, rden, phi_q, phi_k, uq, uk, v, fm],
        in_specs=[pl.BlockSpec((LIVE, LANES), lambda p, *_: (0, first + p)), per_pair, per_pair, per_head, per_head, per_pair, per_pair, per_pair,
                  pl.BlockSpec((None, 2) + fm.shape[2:], lambda p, *_: (layer, first + p, 0, 0))],
        out_specs=[pl.BlockSpec((LIVE, LANES), lambda p, *_: (0, p))] * 3,
        scratch=[
            pltpu.VMEM((BLOCKS, BLOCK, BLOCK), BF16),
            pltpu.VMEM((BLOCKS - 1, REACH, BLOCK), BF16),
            pltpu.VMEM((BLOCKS, BLOCK, BLOCK), BF16),
            pltpu.VMEM((BLOCKS - 1, REACH, BLOCK), BF16),
            pltpu.VMEM((2, LIVE, 256), BF16),
            pltpu.VMEM((2, LIVE, 256), BF16),
            pltpu.VMEM((LIVE, LANES), BF16),
            pltpu.VMEM((LIVE, 256), F32),
            pltpu.VMEM((LIVE, 256), F32),
            pltpu.VMEM((2, LIVE, LANES), F32),
            pltpu.VMEM((2, 2, LIVE, 256), F32),
        ],
        out_shape=[jax.ShapeDtypeStruct((LIVE, count * LANES), BF16)] * 3,
        us=us,
        name="attn_backward",
    )


GROUPS = 4


def put(out_ref, ids, values, quarter, base):
    me, here = ids
    count = out_ref.shape[0]
    rows = values.shape[0] // count
    for portion in range(count):
        out_ref[portion ^ me, quarter ^ here, base : base + rows, :] = values[portion * rows : portion * rows + rows]


def columns(values, which):
    return values[:, which * LANES : which * LANES + LANES]


def group_of_qkv(half, group, refs):
    normed_t_ref, lefts = refs[0], refs[1:]
    runs = len(lefts) // 3
    tall = normed_t_ref.shape[0] // 2
    height = 3 * tall // GROUPS
    parts = []
    first = group * height
    while first < (group + 1) * height:
        j, start = divmod(first, tall)
        rows = min(tall - start, (group + 1) * height - first)
        normed_t = normed_t_ref[pl.ds(pl.multiple_of(half * tall + start, 16), rows), :]
        parts.append(jnp.concatenate([dot(normed_t, lefts[3 * run + j][...]) for run in range(runs)], axis=1))
        first += rows
    return jnp.concatenate(parts, axis=0) if len(parts) > 1 else parts[0]


def ff_bwd_body(layer, top, runs, parts, id_ref, *refs):
    extra_refs, refs = refs[: 3 * runs + (runs > 0)], refs[3 * runs + (runs > 0) :]
    if top:
        (x_ref, low_ref, g_ref, low_t_ref, gain_ref, shift_ref, up_ref, up_bias_ref, down_ref, down_bias_ref, wo_ref,
         out_ref, mid_g_ref, att_g_ref, small_ref, up_bias_g_ref, sent_ref, kept_ref,
         act_ref, pre_ref, g_t_ref, normed_t_ref, mid_low_ref, mid_ref) = refs
    else:
        (mid_ref, g_ref, low_t_ref, gain_ref, shift_ref, up_ref, up_bias_ref, down_ref, wo_ref,
         mid_g_ref, att_g_ref, small_ref, up_bias_g_ref, sent_ref, kept_ref,
         act_ref, pre_ref, g_t_ref, normed_t_ref, mid_low_ref) = refs
    step = pl.program_id(0)
    hidden = up_ref.shape[1]
    quarters = sent_ref.shape[1]
    length = g_t_ref.shape[1]
    tiles = length // BLOCK
    share = hidden // quarters

    @pl.when(step == 0)
    def _():
        small_ref[...] = jnp.zeros_like(small_ref)
        up_bias_g_ref[...] = jnp.zeros_like(up_bias_g_ref)

    @pl.when(step < tiles)
    def _():
        if top:
            mid_ref[...] = x_ref[...]

            @pl.when(step < BLOCKS)
            def _():
                mid_ref[...] += dot(low_ref[...], wo_ref[...])

        rows = pl.ds(pl.multiple_of(step * BLOCK, BLOCK), BLOCK)
        mid = mid_ref[...]
        unit, rstd = normalize(mid)
        normed = (unit * gain_ref[layer, 1:2, :] + shift_ref[layer, 1:2, :]).astype(BF16)
        normed_t_ref[:, rows] = normed.T
        grad = g_ref[...]
        g_low = grad.astype(BF16)
        g_t_ref[:, rows] = g_low.T
        if top:
            total = mid + down_bias_ref[layer : layer + 1, :]
        back = jnp.zeros(grad.shape, F32)
        for quarter in range(quarters):
            cols = slice(quarter * share, quarter * share + share)
            pre = dot(normed, up_ref[:, cols]) + up_bias_ref[layer : layer + 1, cols]
            act, slope = gelu_terms(pre)
            act = act.astype(BF16)
            per_half = quarters // 2
            act_ref[quarter // per_half, rows, (quarter % per_half) * share : (quarter % per_half) * share + share] = act
            if top:
                total = total + dot(act, down_ref[cols, :])
            pre_low = (dot_nt(g_low, down_ref[cols, :]) * slope).astype(BF16)
            for which in range(share // LANES):
                pre_ref[which, rows, quarter * LANES : quarter * LANES + LANES] = columns(pre_low, which)
            up_bias_g_ref[:, cols] += jnp.sum(pre_low.astype(F32), axis=0, keepdims=True)
            back = back + dot_nt(pre_low, up_ref[:, cols])
        if top:
            out_ref[...] = total
        mid_g = grad + norm_pull(back, gain_ref[layer, 1:2, :], unit, rstd)
        mid_g_ref[...] = mid_g
        mid_low = mid_g.astype(BF16)
        small_ref[0:1, :] += jnp.sum(back * unit, axis=0, keepdims=True)
        small_ref[1:2, :] += jnp.sum(back, axis=0, keepdims=True)
        small_ref[2:3, :] += jnp.sum(g_low.astype(F32), axis=0, keepdims=True)

        @pl.when(step < BLOCKS)
        def _():
            mid_low_ref[rows, :] = mid_low
            att_g_ref[...] = dot_nt(mid_low, wo_ref[...])

    count = sent_ref.shape[0]
    ids = (id_ref[0] & (count - 1), id_ref[1])
    for first, flip, end_ref in ((tiles, 1, sent_ref), (tiles + GROUPS, 0, kept_ref)):
        half = (id_ref[0] // (parts // 2)) ^ flip
        for group in range(GROUPS):

            @pl.when(step == first + group)
            def _(half=half, group=group, end_ref=end_ref):
                wide = act_ref.shape[2] // GROUPS
                down = dot(g_t_ref[...], act_ref[half, :, group * wide : group * wide + wide])
                height = normed_t_ref.shape[0] * (share // LANES // 2) // GROUPS
                per_tile = normed_t_ref.shape[0] // height
                part = group % per_tile
                up = dot(normed_t_ref[part * height : part * height + height, :], pre_ref[half * (share // LANES // 2) + group // per_tile])
                tall = low_t_ref.shape[0] // 2 // GROUPS
                low_rows = pl.ds(pl.multiple_of(half * (low_t_ref.shape[0] // 2) + group * tall, tall), tall)
                out = dot(low_t_ref[low_rows, :], mid_low_ref[...])
                if runs:
                    extra = group_of_qkv(half, group, extra_refs)
                for quarter in range(quarters):
                    rows = slice(quarter * LANES, quarter * LANES + LANES)
                    pieces = [
                        jnp.concatenate([columns(down[rows], which) for which in range(wide // LANES)], axis=0),
                        columns(up, quarter),
                        columns(out, quarter),
                    ]
                    if runs:
                        pieces.append(columns(extra, quarter))
                    base = 0
                    for piece in pieces:
                        put(end_ref, ids, piece, quarter, base)
                        base += piece.shape[0] // count


def ff_bwd(layer, ids, parts, quarters, grad, low_t, gains, shifts, up, up_bias, down, wo, mid=None, top=None, qkv=None, after=()):
    length, width = grad.shape
    hidden = up.shape[2]
    tiles = length // BLOCK
    portions = parts // 2
    group = portions // GROUPS
    rows = pl.BlockSpec((BLOCK, width), lambda i, ids: (jnp.minimum(i, tiles - 1), 0))
    live = pl.BlockSpec((BLOCK, width), lambda i, ids: (jnp.minimum(i, BLOCKS - 1), 0))
    weights = [gains, shifts, up, up_bias, down] + ([top[2]] if top else []) + [wo]
    weight_specs = [constant(*gains.shape), constant(*shifts.shape), of_layer(layer, up), constant(*up_bias.shape), of_layer(layer, down)]
    weight_specs += ([constant(*top[2].shape)] if top else []) + [of_layer(layer, wo)]
    piece_rows = hidden // parts + width * (hidden // quarters // LANES) // parts + width // parts + (3 * width // parts if qkv else 0)
    extra = [qkv[0]] + [part for run in qkv[1] for part in run] if qkv else []
    end = (portions, quarters, piece_rows, LANES)

    def end_spec(first):
        return pl.BlockSpec((group,) + end[1:], lambda i, ids: (jnp.clip(i - first, 0, GROUPS - 1) ^ ((ids[0] & (portions - 1)) // group), 0, 0, 0))

    got = call(
        functools.partial(ff_bwd_body, layer, bool(top), len(extra) // 3, parts),
        after,
        grid=(tiles + 2 * GROUPS,),
        prefetch=[ids],
        operands=extra + ([top[0], top[1]] if top else [mid]) + [grad, low_t] + weights,
        in_specs=[constant(*a.shape) for a in extra] + ([rows, live] if top else [rows]) + [rows, constant(*low_t.shape)] + weight_specs,
        out_specs=([rows] if top else []) + [rows, live, resident(8, width), resident(1, hidden), end_spec(tiles), end_spec(tiles + GROUPS)],
        scratch=[
            pltpu.VMEM((2, length, hidden // 2), BF16),
            pltpu.VMEM((hidden // quarters // LANES, length, quarters * LANES), BF16),
            pltpu.VMEM((width, length), BF16),
            pltpu.VMEM((width, length), BF16),
            pltpu.VMEM((LIVE, width), BF16),
        ] + ([pltpu.VMEM((BLOCK, width), F32)] if top else []),
        out_shape=([jax.ShapeDtypeStruct((length, width), F32)] if top else [])
        + [
            jax.ShapeDtypeStruct((length, width), F32),
            jax.ShapeDtypeStruct((LIVE, width), F32),
            jax.ShapeDtypeStruct((8, width), F32),
            jax.ShapeDtypeStruct((1, hidden), F32),
            jax.ShapeDtypeStruct(end, F32),
            jax.ShapeDtypeStruct(end, F32),
        ],
        us=18.0,
        name="ff_backward",
    )
    return got if top else [None] + list(got)


def input_bwd_body(layer, runs, parts, order, ends, id_ref, *refs):
    left_refs = refs[: 3 * runs]
    w_ref, normed_t_ref, x_ref, gain_ref, mid_g_ref = refs[3 * runs : 3 * runs + 5]
    small_refs = refs[3 * runs + 5 : -4]
    if ends:
        out_ref, small_ref, sent_ref, kept_ref = refs[-4:]
    else:
        out_ref, small_ref = refs[-2:]
    step = pl.program_id(0)
    tiles = pl.num_programs(0) - (2 if ends else 0)

    @pl.when(step == 0)
    def _():
        small_ref[...] = jnp.zeros_like(small_ref)

    @pl.when(step < BLOCKS)
    def _():
        rows = pl.ds(pl.multiple_of(step * BLOCK, BLOCK), BLOCK)
        back = jnp.zeros(x_ref.shape, F32)
        for run in range(runs):
            for j in range(3):
                left = left_refs[3 * run + j]
                wide = left.shape[1]
                back = back + dot_nt(left[rows, :], w_ref[j, :, run * wide : run * wide + wide])
        unit, rstd = normalize(x_ref[...])
        out_ref[...] = mid_g_ref[...] + norm_pull(back, gain_ref[layer, 0:1, :], unit, rstd)
        small_ref[0:1, :] += jnp.sum(back * unit, axis=0, keepdims=True)
        small_ref[1:2, :] += jnp.sum(back, axis=0, keepdims=True)

    @pl.when((step >= BLOCKS) & (step < tiles))
    def _():
        out_ref[...] = mid_g_ref[...]

    if not ends:
        return
    count, quarters = sent_ref.shape[:2]
    ids = (id_ref[0] & (count - 1), id_ref[1])
    for when, flip, end_ref in ((tiles, 1, sent_ref), (tiles + 1, 0, kept_ref)):
        half = (id_ref[0] // (parts // 2)) ^ flip

        @pl.when(step == when)
        def _(half=half, end_ref=end_ref):
            tall = normed_t_ref.shape[0] // 2
            normed_t = normed_t_ref[pl.ds(pl.multiple_of(half * tall, tall), tall), :]
            totals = [jnp.concatenate([dot(normed_t, left_refs[3 * run + j][...]) for run in range(runs)], axis=1) for j in range(3)]
            for quarter in range(quarters):
                put(end_ref, ids, jnp.concatenate([columns(total, quarter) for total in totals], axis=0), quarter, 0)
            base = 3 * tall // count
            if order:
                room = end_ref.shape[2] - base
                end_ref[:, :, base:, :] = jnp.zeros((count, quarters, room, LANES), F32)

                @pl.when(half == 0)
                def _():
                    for at, (array, row, first) in enumerate(order):
                        portion, offset = divmod(at, room)
                        source = small_ref if array < 0 else small_refs[array]
                        per = source.shape[1] // quarters
                        for quarter in range(quarters):
                            start = quarter * per + first
                            end_ref[portion ^ ids[0], quarter ^ ids[1], base + offset : base + offset + 1, :] = source[row : row + 1, start : start + LANES]


def input_bwd(layer, ids, parts, quarters, proj_g, w, normed_t, x, gains, mid_g, smalls=(), order=(), ends=True, after=()):
    length, width = x.shape
    tiles = length // BLOCK
    rows = pl.BlockSpec((BLOCK, width), lambda i, ids: (jnp.minimum(i, tiles - 1), 0))
    lefts = [part for run in proj_g for part in run]
    small_rows = small_rows_of(len(order), parts)
    end = (parts // 2, quarters, 3 * width // parts + small_rows, LANES)
    return call(
        functools.partial(input_bwd_body, layer, len(proj_g), parts, tuple(order), ends),
        after,
        grid=(tiles + (2 if ends else 0),),
        prefetch=[ids],
        operands=lefts + [w, normed_t, x, gains, mid_g] + list(smalls),
        in_specs=[constant(*a.shape) for a in lefts]
        + [of_layer(layer, w), constant(*normed_t.shape), rows, constant(*gains.shape), rows]
        + [constant(*a.shape) for a in smalls],
        out_specs=[rows, resident(8, width)] + [resident(*end)] * (2 if ends else 0),
        out_shape=[jax.ShapeDtypeStruct((length, width), F32), jax.ShapeDtypeStruct((8, width), F32)] + [jax.ShapeDtypeStruct(end, F32)] * (2 if ends else 0),
        us=1.0,
        name="input_backward",
    )


def small_rows_of(count, parts):
    return -(-count // (8 * parts)) * 8


def cut_of(rows):
    return rows // 16 * 8 if rows >= 16 else rows // 2


def fork_body(kept_ref, got_ref, *ends):
    portions = kept_ref.shape[0]
    cut = ends[0].shape[2]
    for slot in range(portions):
        upper, lower = ends[slot // (portions // 2)], ends[2 + slot % 2]
        upper[slot % (portions // 2)] = kept_ref[slot, :, :cut] + got_ref[slot, :, :cut]
        lower[slot // 2] = kept_ref[slot, :, cut:] + got_ref[slot, :, cut:]


def fork(kept, got, after):
    portions, quarters, rows, _ = kept.shape
    cut = cut_of(rows)
    ends = [(portions // 2, quarters, n, LANES) for n in (cut, cut, rows - cut, rows - cut)]
    by_quarter = lambda shape: pl.BlockSpec((shape[0], 1) + shape[2:], lambda i: (0, i, 0, 0))
    return call(
        fork_body,
        after,
        grid=(quarters,),
        prefetch=[],
        operands=[kept, got],
        in_specs=[by_quarter(kept.shape)] * 2,
        out_specs=[by_quarter(end) for end in ends],
        out_shape=[jax.ShapeDtypeStruct(end, F32) for end in ends],
        us=3.0,
        name="fork_terms",
    )


def add_body(count, *refs):
    outs = refs[2 * count :]
    for which in range(count):
        for side in range(2):
            outs[2 * which + side][...] = refs[2 * which][:, side] + refs[2 * which + 1][:, side]


def add_streams(streams, wheres, after):
    operands, shapes = [], []
    for pair, where in zip(streams, wheres):
        shape = pair[0].shape
        flat = (math.prod(shape[:where]), 2, math.prod(shape[where + 1 : -2])) + shape[-2:]
        operands += [part.reshape(flat) for part in pair]
        shapes.append((flat[0],) + flat[2:])
    outs = [shape for shape in shapes for _ in range(2)]
    got = call(
        functools.partial(add_body, len(streams)),
        after,
        grid=(1,),
        prefetch=[],
        operands=operands,
        in_specs=[constant(*a.shape) for a in operands],
        out_specs=[resident(*shape) for shape in outs],
        out_shape=[jax.ShapeDtypeStruct(shape, F32) for shape in outs],
        us=1.5,
        name="add_terms",
    )
    results = []
    for which in range(len(got) // 2):
        shape, where = streams[which][0].shape, wheres[which]
        lead = shape[:where] + shape[where + 1 : -2]
        results.append(tuple(part.reshape(lead + part.shape[-2:]) for part in got[2 * which : 2 * which + 2]))
    return results


def pairs_body(count, *refs):
    kept_ref, sent_ref = refs[2 * count :]
    first = 0
    for which in range(count):
        one, two = refs[2 * which], refs[2 * which + 1]
        rows = one.shape[-2]
        for out_ref, side in ((kept_ref, 0), (sent_ref, 1)):
            out_ref[:, first : first + rows, :] = one[:, side] + two[:, side]
        first += rows


def add_pairs(streams, after):
    operands = [part.reshape((part.shape[0] // 2, 2) + part.shape[1:]) for pair in streams for part in pair]
    shape = (operands[0].shape[0], sum(pair[0].shape[1] for pair in streams), LANES)
    return call(
        functools.partial(pairs_body, len(streams)),
        after,
        grid=(1,),
        prefetch=[],
        operands=operands,
        in_specs=[constant(*a.shape) for a in operands],
        out_specs=[resident(*shape)] * 2,
        out_shape=[jax.ShapeDtypeStruct(shape, F32)] * 2,
        us=1.5,
        name="add_pairs",
    )


def last_add_body(counts, *refs):
    upper_ref, lower_ref = refs[-2:]
    cut = upper_ref.shape[0]
    first, base = 0, 0
    for count in counts:
        total = sum(ref[...] for ref in refs[first : first + count])
        first += count
        rows = total.shape[0]
        split = min(max(cut - base, 0), rows)
        if split:
            upper_ref[base : base + split, :] = total[:split]
        if split < rows:
            lower_ref[base + split - cut : base + rows - cut, :] = total[split:]
        base += rows


def last_add(runs, after):
    operands = [term for run in runs for term in run]
    rows = sum(run[0].shape[0] for run in runs)
    cut = cut_of(rows)
    return call(
        functools.partial(last_add_body, tuple(len(run) for run in runs)),
        after,
        grid=(1,),
        prefetch=[],
        operands=operands,
        in_specs=[constant(*a.shape) for a in operands],
        out_specs=[resident(cut, LANES), resident(rows - cut, LANES)],
        out_shape=[jax.ShapeDtypeStruct((cut, LANES), F32), jax.ShapeDtypeStruct((rows - cut, LANES), F32)],
        us=1.5,
        name="last_terms",
    )


def swap(block, axis_name, bit):
    return lax.ppermute(block, axis_name, [(i, i ^ bit) for i in range(lax.axis_size(axis_name))])


def bits_of(extent):
    return [1 << i for i in range(extent.bit_length() - 1)]


class Line:
    def __init__(self):
        self.last = []

    def __call__(self, function, *args, **kwargs):
        made = function(*args, after=self.last, **kwargs)
        leaves = jax.tree.leaves(made)
        self.last = [min(leaves, key=lambda a: a.size)]
        return made

    def wait(self, *chains):
        self.last = self.last + [array for chain in chains for array in chain.pending]


def scatter(line, sent, kept, parts, quarters):
    dp_bits, batch_bits = bits_of(parts), bits_of(quarters)
    near, far = dp_bits[0], dp_bits[1:]
    got = swap(sent, "dp", near)
    yield [got]
    ends = line(fork, kept, got)
    names = [("dp", bit) for bit in far] + [("batch", bit) for bit in batch_bits[::-1]]
    streams, left = [], []
    for which, order in enumerate((far, far[::-1])):
        kept, sent = ends[2 * which : 2 * which + 2]
        left.append([name for name in names if name != ("dp", order[0])])
        kept, sent = (part.reshape((2,) * len(left[-1]) + part.shape[2:]) for part in (kept, sent))
        streams.append((kept, swap(sent, "dp", order[0])))
    yield [got for _, got in streams]
    for bits in zip(far[1:], far[::-1][1:]):
        wheres = [names_left.index(("dp", bit)) for names_left, bit in zip(left, bits)]
        results = line(add_streams, streams, wheres)
        for which, bit in enumerate(bits):
            left[which].remove(("dp", bit))
            streams[which] = (results[which][0], swap(results[which][1], "dp", bit))
        yield [got for _, got in streams]
    streams = [tuple(part.reshape((quarters,) + part.shape[-2:]) for part in pair) for pair in streams]
    for bit in batch_bits:
        kept, sent = line(add_pairs, streams)
        streams = [(kept, swap(sent, "batch", bit))]
        yield [streams[0][1]]
    return [part[0] for part in streams[0]]


def spread(halves, parts):
    dp_bits = bits_of(parts)
    near, far = dp_bits[0], dp_bits[1:]
    streams = list(halves)
    names = [[], []]
    for bits in zip(far[::-1], far):
        moved = [swap(stream, "dp", bit) for stream, bit in zip(streams, bits)]
        yield moved
        for which, bit in enumerate(bits):
            names[which].append(bit)
            names[which].sort()
            streams[which] = jnp.stack([streams[which], moved[which]], axis=names[which].index(bit))
    block = jnp.concatenate(streams, axis=-2)
    block = block.reshape(parts // 2, block.shape[-2], LANES)
    moved = swap(block, "dp", near)
    yield [moved]
    return block, moved


class Chain:
    def __init__(self, steps):
        self.steps, self.result, self.pending = steps, None, []

    def step(self):
        if self.result is None:
            try:
                self.pending = next(self.steps)
            except StopIteration as stop:
                self.result = stop.value

    def finish(self):
        while self.result is None:
            self.step()
        return self.result


def unpack_body(names, bases, pieces, filled, id_ref, *refs):
    out_refs = dict(zip(names, refs[2 + filled :]))
    down_ref, small_ref = refs[-2:]
    me = id_ref[0]
    for top in range(2):
        ref = refs[top]
        portions = ref.shape[0]
        for slot in range(portions):
            portion = (slot + top * portions) ^ me
            upper, inner = portion // portions, portion % portions
            for name, layer, first, rows in pieces:
                values = ref[slot, first : first + rows, :]
                if name == "small":
                    small_ref[pl.ds(pl.multiple_of(portion * rows, 8), rows), :] = values
                    continue
                out_ref = out_refs[name]
                layer = layer - bases[name]
                if name == "qkv":
                    width = out_ref.shape[1] // 3
                    unit = math.gcd(rows, width // 2)
                    for k in range(0, rows, unit):
                        flat = inner * rows + k
                        start = (flat // (width // 2)) * width + upper * (width // 2) + flat % (width // 2)
                        out_ref[layer, pl.ds(pl.multiple_of(start, 8), unit), :] = values[k : k + unit]
                elif name == "up":
                    height = out_ref.shape[1]
                    flat = portion * rows
                    tile, start = flat // height, flat % height
                    out_ref[layer, pl.ds(pl.multiple_of(start, 8), rows), pl.ds(pl.multiple_of(tile * LANES, LANES), LANES)] = values
                elif name == "down":
                    down_ref[pl.ds(pl.multiple_of(portion * rows, 8), rows), :] = values
                else:
                    out_ref[layer, pl.ds(pl.multiple_of(portion * rows, 8), rows), :] = values
    if "down" in out_refs:
        for first in range(0, down_ref.shape[0], LANES):
            out_refs["down"][0, first : first + LANES, :] = down_ref[first : first + LANES, :].T
    if "gains" in out_refs:
        layers, wide = out_refs["up_bias"].shape
        row = 0
        for layer in range(layers):
            for name, count in (("gains", 2), ("shifts", 2)):
                out_refs[name][layer] = small_ref[row : row + count, :]
                row += count
            for k in range(wide // LANES):
                out_refs["up_bias"][layer : layer + 1, k * LANES : k * LANES + LANES] = small_ref[row : row + 1, :]
                row += 1
            out_refs["down_bias"][layer : layer + 1, :] = small_ref[row : row + 1, :]
            row += 1


def unpack(ids, pair, pieces, layers, width, hidden, quarters, filled=(), after=()):
    shapes = {"down": (layers, hidden, LANES), "up": (layers, width, hidden // quarters), "out": (layers, width, LANES), "qkv": (layers, 3 * width, LANES)}
    found = {name: [layer for piece, layer, _, _ in pieces if piece == name] for name in shapes}
    names = tuple(name for name in shapes if found[name])
    bases = {name: min(found[name]) for name in names}
    out_specs = [
        pl.BlockSpec((len(found[name]),) + shapes[name][1:], lambda *_, name=name: (bases[name] // len(found[name]), 0, 0)) for name in names
    ]
    out_shape = [jax.ShapeDtypeStruct(shapes[name], F32) for name in names]
    small = [rows for piece, _, _, rows in pieces if piece == "small"]
    if small:
        names += ("gains", "shifts", "up_bias", "down_bias")
        for shape in ((layers, 2, LANES), (layers, 2, LANES), (layers, hidden // quarters), (layers, LANES)):
            out_specs.append(resident(*shape))
            out_shape.append(jax.ShapeDtypeStruct(shape, F32))
    return call(
        functools.partial(unpack_body, names, bases, pieces, len(filled)),
        after,
        grid=(1,),
        prefetch=[ids],
        operands=list(pair) + list(filled),
        in_specs=[constant(*a.shape) for a in pair] + [pl.BlockSpec(memory_space=pl.ANY)] * len(filled),
        out_specs=out_specs,
        scratch=[
            pltpu.VMEM((hidden if found["down"] else 8, LANES), F32),
            pltpu.VMEM((2 * pair[0].shape[0] * small[0] if small else 8, LANES), F32),
        ],
        out_shape=out_shape,
        aliases=[(2 + which, which) for which in range(len(filled))],
        us=4.0,
        name="unpack",
    )


def reverse_bits(value, extent):
    return sum(((value // bit) % 2) * (extent // (2 * bit)) for bit in bits_of(extent))


def per_device(activations_in, gains, shifts, qkv_weights, out_weights, up_weights, up_bias, down_weights, down_bias, feature_maps, lengths, cotangent):
    layers, _, width = gains.shape
    hidden = up_bias.shape[1]
    parts, quarters = lax.axis_size("dp"), lax.axis_size("batch")
    ids = jnp.stack([reverse_bits(lax.axis_index("dp"), parts), lax.axis_index("batch")]).astype(jnp.int32)
    proteins = lengths[0]
    pairs = feature_maps.shape[1] // 2
    half = pairs // 2
    line = Line()
    last = layers - 1
    x, saved = activations_in[0], []
    for layer in range(layers):
        normed_t, *kept, low, low_t = line(attn_fwd, layer, proteins, x, gains, shifts, qkv_weights, feature_maps)
        phi_q, phi_k, uq, uk, v, att, rden = kept
        mid = None
        before = x
        if layer < last:
            x, mid = line(ff_fwd, layer, x, low, out_weights, gains, shifts, up_weights, up_bias, down_weights, down_bias)
        saved.append((before, normed_t, (att, rden, phi_q, phi_k, uq, uk, v), low, low_t, mid))

    smalls = [None] * layers

    def ff_part(layer, grad, top=None, qkv=None):
        _, _, _, low, low_t, mid = saved[layer]
        out, mid_g, att_g, small_two, up_bias_g, sent, kept = line(
            ff_bwd, layer, ids, parts, quarters, grad, low_t, gains, shifts, up_weights, up_bias, down_weights, out_weights, mid=mid, top=top, qkv=qkv
        )
        smalls[layer] = [None, small_two, up_bias_g]
        return out, mid_g, att_g, Chain(scatter(line, sent, kept, parts, quarters))

    def attn_part(layer, att_g, first, count, us):
        return line(attn_bwd, layer, proteins, att_g, *saved[layer][2], feature_maps, first, count, us)

    def input_part(layer, proj_g, mid_g, **rest):
        grad, smalls[layer][0], *ends = line(
            input_bwd, layer, ids, parts, quarters, proj_g, qkv_weights, saved[layer][1], saved[layer][0], gains, mid_g, **rest
        )
        return grad, Chain(scatter(line, *ends, parts, quarters)) if ends else None

    wide = hidden // quarters // LANES
    ff_rows = (hidden // parts, width * wide // parts, width // parts)
    ff_total, qkv_rows = sum(ff_rows), 3 * width // parts
    sizes = (layers, width, hidden, quarters)

    def ff_pieces(layer, base):
        return (("down", layer, base, ff_rows[0]), ("up", layer, base + ff_rows[0], ff_rows[1]), ("out", layer, base + ff_rows[0] + ff_rows[1], ff_rows[2]))

    values, mid_g, att_g, first = ff_part(1, cotangent[0], (x, saved[1][3], down_bias))
    first.step()
    runs = [attn_part(1, att_g, 0, half, 60.0)]
    first.step()
    runs.append(attn_part(1, att_g, half, pairs - half, 1.0))
    grad, _ = input_part(1, runs, mid_g, ends=False)
    first.step()
    _, mid_g, att_g, second = ff_part(0, grad, qkv=(saved[1][1], runs))
    second.step()
    first.step()
    runs = [attn_part(0, att_g, 0, half, 60.0)]
    second.step()
    first.step()
    runs.append(attn_part(0, att_g, half, pairs - half, 1.0))
    spread_one = Chain(spread(line(last_add, [first.finish()]), parts))
    spread_one.step()
    flat = [array for layer in range(layers) for array in smalls[layer]]
    order = []
    for layer in range(layers):
        one, two, bias = (3 * layer + k for k in range(3))
        order += [(one, 0, 0), (two, 0, 0), (one, 1, 0), (two, 1, 0)] + [(bias, 0, k * LANES) for k in range(wide)] + [(two, 2, 0)]
    present = [k for k, array in enumerate(flat) if array is not None]
    order = [(present.index(array) if array in present else -1, row, first_col) for array, row, first_col in order]
    grad, third = input_part(0, runs, mid_g, smalls=[flat[k] for k in present], order=order)
    third.step()
    second.step()
    spread_one.step()
    third.step()
    spread_one.step()
    second.step()
    third.step()
    second.step()
    third.step()
    down, up, out = line(unpack, ids, spread_one.finish(), ff_pieces(1, 0), *sizes)
    pair = Chain(spread(line(last_add, [second.finish(), third.finish()]), parts)).finish()
    pieces = ff_pieces(0, 0) + (("qkv", 1, ff_total, qkv_rows), ("qkv", 0, ff_total + qkv_rows, qkv_rows))
    pieces += (("small", 0, ff_total + 2 * qkv_rows, small_rows_of(len(order), parts)),)
    down, up, out, qkv, gains_g, shifts_g, up_bias_g, down_bias_g = line(unpack, ids, pair, pieces, *sizes, (down, up, out))
    return (
        values[None],
        grad[None],
        gains_g,
        shifts_g,
        qkv.reshape(layers, 3, width, LANES),
        out,
        up,
        up_bias_g,
        down,
        down_bias_g,
    )


def solution(mesh):
    rows = P(("dp", "batch"), None, None)
    return jax.shard_map(
        per_device,
        mesh=mesh,
        in_specs=(rows,) + (P(),) * 9 + (P(("dp", "batch"), None), rows),
        out_specs=(
            rows,
            rows,
            P(None, None, "batch"),
            P(None, None, "batch"),
            P(None, None, None, "batch"),
            P(None, None, "batch"),
            P(None, None, "batch"),
            P(None, "batch"),
            P(None, None, "batch"),
            P(None, "batch"),
        ),
        check_vma=False,
    )
```

```python
import functools
import math

import jax
import jax.numpy as jnp
from jax import lax
from jax.experimental import pallas as pl
from jax.experimental.pallas import tpu as pltpu
from jax.sharding import PartitionSpec as P

BLOCK = 256
BLOCKS = 3
LIVE = BLOCK * BLOCKS
REACH = 160
LANES = 128
NDOC = 6
MIB = 1 << 20
F32 = jnp.float32
BF16 = jnp.bfloat16
LOG2E = 1.4426950408889634
NT = (((1,), (1,)), ((), ()))


def dot(a, b):
    return jnp.dot(a, b, preferred_element_type=F32)


def dot_nt(a, b):
    return lax.dot_general(a, b, NT, preferred_element_type=F32)


def params_for(mib):
    return pltpu.CompilerParams(vmem_limit_bytes=mib * MIB)


def call(body, after, *, grid, in_specs, out_specs, out_shape, prefetch, operands, scratch=(), aliases=(), mib=63, us=3.0, name):
    scalars, count = len(prefetch), len(after)

    def ordered(*refs):
        body(*refs[:scalars], *refs[scalars + count :])

    return pl.pallas_call(
        ordered,
        grid_spec=pltpu.PrefetchScalarGridSpec(
            num_scalar_prefetch=scalars,
            grid=grid,
            in_specs=[pl.BlockSpec(memory_space=pl.ANY)] * count + list(in_specs),
            out_specs=out_specs,
            scratch_shapes=list(scratch),
        ),
        out_shape=out_shape,
        input_output_aliases={scalars + count + operand: output for operand, output in aliases},
        compiler_params=params_for(mib),
        cost_estimate=pl.CostEstimate(flops=int(us * 1.15e9), bytes_accessed=0, transcendentals=0),
        name=name,
    )(*prefetch, *after, *operands)


def constant(*shape):
    return pl.BlockSpec(shape, lambda *_: (0,) * len(shape), pipeline_mode=pl.Buffered(1))


def resident(*shape):
    return pl.BlockSpec(shape, lambda *_: (0,) * len(shape))


def of_layer(layer, array):
    return pl.BlockSpec((None,) + array.shape[1:], lambda *_: (layer,) + (0,) * (array.ndim - 1), pipeline_mode=pl.Buffered(1))


def normalize(values):
    centered = values - jnp.mean(values, axis=-1, keepdims=True)
    rstd = lax.rsqrt(jnp.mean(centered * centered, axis=-1, keepdims=True) + 1e-05)
    return centered * rstd, rstd


def norm_pull(grad, gain, unit, rstd):
    p = grad * gain
    return rstd * (p - jnp.mean(p, axis=-1, keepdims=True) - unit * jnp.mean(p * unit, axis=-1, keepdims=True))


def split_two(values):
    high = values.astype(BF16)
    return high, (values - high.astype(F32)).astype(BF16)


def protein_ids(len_ref, position):
    bound = jnp.int32(0)
    ids = jnp.zeros(position.shape, jnp.int32)
    for j in range(NDOC):
        bound = bound + len_ref[j]
        ids = ids + (position >= bound).astype(jnp.int32)
    return ids


def token_count(len_ref):
    total = jnp.int32(0)
    for j in range(NDOC):
        total = total + len_ref[j]
    return total


def pair_mask(len_ref, shape, first_row, first_col, causal_rows):
    rows = lax.broadcasted_iota(jnp.int32, shape, 0) + first_row
    cols = lax.broadcasted_iota(jnp.int32, shape, 1) + first_col
    same = protein_ids(len_ref, rows) == protein_ids(len_ref, cols)
    ordered = (rows >= cols) if causal_rows else (cols >= rows)
    return jnp.where(same & ordered, 1.0, 0.0).astype(BF16)


def fill_masks(len_ref, own_ref, before_ref, causal_rows):
    for b in range(BLOCKS):
        own_ref[b] = pair_mask(len_ref, (BLOCK, BLOCK), b * BLOCK, b * BLOCK, causal_rows)
    for b in range(1, BLOCKS):
        if causal_rows:
            before_ref[b - 1] = pair_mask(len_ref, (REACH, BLOCK), b * BLOCK, (b - 1) * BLOCK, True)
        else:
            before_ref[b - 1] = pair_mask(len_ref, (REACH, BLOCK), b * BLOCK - REACH, b * BLOCK, False)


def attn_fwd_body(layer, len_ref, x_ref, gain_ref, shift_ref, w_ref, fm_ref, normed_t_ref, phi_q_ref, phi_k_ref, uq_ref, uk_ref,
                  v_ref, att_ref, rden_ref, low_ref, low_t_ref, normed_ref, proj_ref, own_ref, before_ref, num_ref):
    step = pl.program_id(0)

    @pl.when(step == 0)
    def _():
        fill_masks(len_ref, own_ref, before_ref, True)
        for b in range(BLOCKS):
            rows = pl.ds(b * BLOCK, BLOCK)
            unit, _ = normalize(x_ref[rows, :])
            normed = (unit * gain_ref[layer, 0:1, :] + shift_ref[layer, 0:1, :]).astype(BF16)
            normed_ref[rows, :] = normed
            normed_t_ref[:, rows] = normed.T
        for j in range(3):
            for half in range(2):
                got = dot(normed_ref[...], w_ref[j, :, half * 256 : half * 256 + 256])
                proj_ref[j, 2 * half] = got[:, :LANES]
                proj_ref[j, 2 * half + 1] = got[:, LANES:]

    lane = lax.broadcasted_iota(jnp.int32, (BLOCK, LANES), 1) < 64
    uq_ref[0] = proj_ref[0, step]
    uk_ref[0] = proj_ref[1, step]
    v_ref[0] = proj_ref[2, step].astype(BF16)
    first_head = lax.broadcasted_iota(jnp.int32, (LANES, 256), 0) < 64
    minus = [jnp.where(first_head, -1.0, 0.0).astype(BF16), jnp.where(first_head, 0.0, -1.0).astype(BF16)]
    stacked = []
    for head in range(2):
        high, low = split_two(fm_ref[head] * (64.0 ** (-0.25) * LOG2E))
        stacked.append(jnp.concatenate([high, low, high, low, minus[head], minus[head]], axis=0))
    for which, phi_ref in ((0, phi_q_ref), (1, phi_k_ref)):
        for b in range(BLOCKS):
            rows = pl.ds(b * BLOCK, BLOCK)
            u = proj_ref[which, step, rows, :]
            turned = pltpu.roll(u, 64, 1)
            squares = split_two(u * u * (LOG2E / 16.0) + 0.0625)
            for head in range(2):
                twice = jnp.where(lane, u, turned) if head == 0 else jnp.where(lane, turned, u)
                exponent = dot(jnp.concatenate(split_two(twice) + squares, axis=1), stacked[head])
                phi_ref[head, rows, :] = jnp.exp2(exponent).astype(BF16)
    ones = jnp.ones((BLOCK, LANES), BF16)
    for b in range(BLOCKS):
        rows = pl.ds(b * BLOCK, BLOCK)
        v_now = jnp.concatenate([v_ref[0, rows, :], ones], axis=1)
        for head in range(2):
            weights = dot_nt(phi_q_ref[head, rows, :], phi_k_ref[head, rows, :]).astype(BF16) * own_ref[b]
            num_ref[head] = dot(weights, v_now)
            if b > 0:
                earlier = pl.ds((b - 1) * BLOCK, BLOCK)
                v_before = jnp.concatenate([v_ref[0, earlier, :], ones], axis=1)
                weights = dot_nt(phi_q_ref[head, pl.ds(b * BLOCK, REACH), :], phi_k_ref[head, earlier, :])
                num_ref[head, :REACH, :] += dot(weights.astype(BF16) * before_ref[b - 1], v_before)
        rden = 1.0 / jnp.where(lane, num_ref[0, :, LANES:], num_ref[1, :, LANES:])
        attended = jnp.where(lane, num_ref[0, :, :LANES], num_ref[1, :, :LANES]) * rden
        position = lax.broadcasted_iota(jnp.int32, (BLOCK, LANES), 0) + b * BLOCK
        attended = jnp.where(position < token_count(len_ref), attended, 0.0)
        rden_ref[0, rows, :] = rden
        att_ref[0, rows, :] = attended
        low = attended.astype(BF16)
        low_ref[rows, :] = low
        low_t_ref[:, rows] = low.T


def attn_fwd(layer, lengths, x, gains, shifts, w, fm, after=()):
    width = x.shape[1]
    heads = fm.shape[1]
    pairs = heads // 2
    per_pair = pl.BlockSpec((1, LIVE, LANES), lambda p, *_: (p, 0, 0))
    per_head = pl.BlockSpec((2, LIVE, 256), lambda p, *_: (p, 0, 0))
    return call(
        functools.partial(attn_fwd_body, layer),
        after,
        grid=(pairs,),
        prefetch=[lengths],
        operands=[x, gains, shifts, w, fm],
        in_specs=[
            constant(LIVE, width),
            constant(*gains.shape),
            constant(*shifts.shape),
            of_layer(layer, w),
            pl.BlockSpec((None, 2) + fm.shape[2:], lambda p, *_: (layer, p, 0, 0)),
        ],
        out_specs=[resident(width, LIVE), per_head, per_head, per_pair, per_pair, per_pair, per_pair, per_pair,
                   pl.BlockSpec((LIVE, LANES), lambda p, *_: (0, p)), pl.BlockSpec((LANES, LIVE), lambda p, *_: (p, 0))],
        scratch=[
            pltpu.VMEM((LIVE, width), BF16),
            pltpu.VMEM((3, pairs, LIVE, LANES), F32),
            pltpu.VMEM((BLOCKS, BLOCK, BLOCK), BF16),
            pltpu.VMEM((BLOCKS - 1, REACH, BLOCK), BF16),
            pltpu.VMEM((2, BLOCK, 256), F32),
        ],
        out_shape=[
            jax.ShapeDtypeStruct((width, LIVE), BF16),
            jax.ShapeDtypeStruct((heads, LIVE, 256), BF16),
            jax.ShapeDtypeStruct((heads, LIVE, 256), BF16),
            jax.ShapeDtypeStruct((pairs, LIVE, LANES), F32),
            jax.ShapeDtypeStruct((pairs, LIVE, LANES), F32),
            jax.ShapeDtypeStruct((pairs, LIVE, LANES), BF16),
            jax.ShapeDtypeStruct((pairs, LIVE, LANES), F32),
            jax.ShapeDtypeStruct((pairs, LIVE, LANES), F32),
            jax.ShapeDtypeStruct((LIVE, width), BF16),
            jax.ShapeDtypeStruct((width, LIVE), BF16),
        ],
        us=15.0,
        name="attn_forward",
    )


def gelu_terms(pre):
    lifted = 0.5 + 0.5 * lax.erf(pre * math.sqrt(0.5))
    return pre * lifted, lifted + pre * (jnp.exp2(pre * pre * (-0.5 * LOG2E)) * (1.0 / math.sqrt(2.0 * math.pi)))


def ff_fwd_body(layer, x_ref, low_ref, wo_ref, gain_ref, shift_ref, up_ref, up_bias_ref, down_ref, down_bias_ref, out_ref, mid_ref):
    step = pl.program_id(0)
    mid_ref[...] = x_ref[...]

    @pl.when(step < BLOCKS)
    def _():
        mid_ref[...] += dot(low_ref[...], wo_ref[...])

    mid = mid_ref[...]
    unit, _ = normalize(mid)
    normed = (unit * gain_ref[layer, 1:2, :] + shift_ref[layer, 1:2, :]).astype(BF16)
    total = mid + down_bias_ref[layer : layer + 1, :]
    for first in range(0, up_ref.shape[1], 512):
        cols = slice(first, first + 512)
        pre = dot(normed, up_ref[:, cols]) + up_bias_ref[layer : layer + 1, cols]
        act = (pre * (0.5 + 0.5 * lax.erf(pre * math.sqrt(0.5)))).astype(BF16)
        total = total + dot(act, down_ref[cols, :])
    out_ref[...] = total


def ff_fwd(layer, x, low, wo, gains, shifts, up, up_bias, down, down_bias, after=()):
    length, width = x.shape
    rows = pl.BlockSpec((BLOCK, width), lambda i: (i, 0))
    return call(
        functools.partial(ff_fwd_body, layer),
        after,
        grid=(length // BLOCK,),
        prefetch=[],
        operands=[x, low, wo, gains, shifts, up, up_bias, down, down_bias],
        in_specs=[
            rows,
            pl.BlockSpec((BLOCK, width), lambda i: (jnp.minimum(i, BLOCKS - 1), 0)),
            of_layer(layer, wo),
            constant(*gains.shape),
            constant(*shifts.shape),
            of_layer(layer, up),
            constant(*up_bias.shape),
            of_layer(layer, down),
            constant(*down_bias.shape),
        ],
        out_specs=[rows, rows],
        out_shape=[jax.ShapeDtypeStruct((length, width), F32)] * 2,
        us=10.0,
        name="ff_forward",
    )


def attn_bwd_body(len_ref, att_g_ref, att_ref, rden_ref, phi_q_ref, phi_k_ref, uq_ref, uk_ref, v_ref, fm_ref,
                  dq_ref, dk_ref, dv_ref, own_ref, before_ref, own_t_ref, before_t_ref,
                  x_ref, y_ref, dn_ref, d_phi_q, d_phi_k, d_v, raw_ref):
    step = pl.program_id(0)

    @pl.when(step == 0)
    def _():
        fill_masks(len_ref, own_ref, before_ref, True)
        fill_masks(len_ref, own_t_ref, before_t_ref, False)

    lane = lax.broadcasted_iota(jnp.int32, (BLOCK, LANES), 1) < 64
    one = jnp.ones((BLOCK, LANES), BF16)
    for b in range(BLOCKS):
        rows = pl.ds(b * BLOCK, BLOCK)
        position = lax.broadcasted_iota(jnp.int32, (BLOCK, LANES), 0) + b * BLOCK
        dn = jnp.where(position < token_count(len_ref), att_g_ref[rows, :] * rden_ref[0, rows, :], 0.0)
        turned = pltpu.roll(-(dn * att_ref[0, rows, :]), 64, 1)
        dn_ref[rows, :] = dn.astype(BF16)
        v_low = v_ref[0, rows, :]
        for head in range(2):
            first = lane if head == 0 else jnp.logical_not(lane)
            high, low = split_two(jnp.where(first, dn, turned))
            x_ref[head, rows, :] = jnp.concatenate([high, low], axis=1)
            y = jnp.where(first, v_low.astype(F32), 1.0).astype(BF16)
            y_ref[head, rows, :] = jnp.concatenate([y, y], axis=1)
    for head in range(2):
        for b in range(BLOCKS):
            rows = pl.ds(b * BLOCK, BLOCK)
            x, y = x_ref[head, rows, :], y_ref[head, rows, :]
            phi_q, phi_k = phi_q_ref[head, rows, :], phi_k_ref[head, rows, :]
            d_kernel = dot_nt(x, y).astype(BF16) * own_ref[b]
            d_phi_q[rows, :] = dot(d_kernel, phi_k)
            d_kernel_t = dot_nt(y, x).astype(BF16) * own_t_ref[b]
            d_phi_k[rows, :] = dot(d_kernel_t, phi_q)
            kernel_t = dot_nt(phi_k, phi_q).astype(BF16) * own_t_ref[b]
            d_v[head, rows, :] = dot(kernel_t, dn_ref[rows, :])
            if b > 0:
                earlier = pl.ds((b - 1) * BLOCK, BLOCK)
                top = pl.ds(b * BLOCK, REACH)
                bottom = pl.ds(b * BLOCK - REACH, REACH)
                d_kernel = dot_nt(x_ref[head, top, :], y_ref[head, earlier, :]).astype(BF16) * before_ref[b - 1]
                d_phi_q[top, :] += dot(d_kernel, phi_k_ref[head, earlier, :])
                d_kernel_t = dot_nt(y_ref[head, bottom, :], x).astype(BF16) * before_t_ref[b - 1]
                d_phi_k[bottom, :] += dot(d_kernel_t, phi_q)
                kernel_t = dot_nt(phi_k_ref[head, bottom, :], phi_q).astype(BF16) * before_t_ref[b - 1]
                d_v[head, bottom, :] += dot(kernel_t, dn_ref[rows, :])
        high, low = split_two(fm_ref[head])
        stacked = jnp.concatenate([high, low, jnp.ones((LANES, 256), BF16)], axis=0)
        for which, d_phi, phi_ref in ((0, d_phi_q, phi_q_ref), (1, d_phi_k, phi_k_ref)):
            for b in range(BLOCKS):
                rows = pl.ds(b * BLOCK, BLOCK)
                d_projected = (d_phi[rows, :] * phi_ref[head, rows, :].astype(F32)).astype(BF16)
                raw_ref[which, head, rows, :] = dot_nt(d_projected, stacked)
    for b in range(BLOCKS):
        rows = pl.ds(b * BLOCK, BLOCK)
        for which, u_ref, out_ref in ((0, uq_ref, dq_ref), (1, uk_ref, dk_ref)):
            parts = []
            for head in range(2):
                raw = raw_ref[which, head, rows, :LANES]
                parts.append(raw + pltpu.roll(raw, 64, 1))
            along = jnp.where(lane, parts[0], parts[1])
            total = jnp.where(lane, raw_ref[which, 0, rows, LANES:], raw_ref[which, 1, rows, LANES:])
            grad = along * (64.0 ** (-0.25)) - u_ref[0, rows, :] * total * 0.125
            out_ref[rows, :] = grad.astype(BF16)
        dv_ref[rows, :] = jnp.where(lane, d_v[0, rows, :], d_v[1, rows, :]).astype(BF16)


def attn_bwd(layer, lengths, att_g, att, rden, phi_q, phi_k, uq, uk, v, fm, first, count, us, after=()):
    per_pair = pl.BlockSpec((1, LIVE, LANES), lambda p, *_: (first + p, 0, 0))
    per_head = pl.BlockSpec((2, LIVE, 256), lambda p, *_: (first + p, 0, 0))
    return call(
        attn_bwd_body,
        after,
        grid=(count,),
        prefetch=[lengths],
        operands=[att_g, att, rden, phi_q, phi_k, uq, uk, v, fm],
        in_specs=[pl.BlockSpec((LIVE, LANES), lambda p, *_: (0, first + p)), per_pair, per_pair, per_head, per_head, per_pair, per_pair, per_pair,
                  pl.BlockSpec((None, 2) + fm.shape[2:], lambda p, *_: (layer, first + p, 0, 0))],
        out_specs=[pl.BlockSpec((LIVE, LANES), lambda p, *_: (0, p))] * 3,
        scratch=[
            pltpu.VMEM((BLOCKS, BLOCK, BLOCK), BF16),
            pltpu.VMEM((BLOCKS - 1, REACH, BLOCK), BF16),
            pltpu.VMEM((BLOCKS, BLOCK, BLOCK), BF16),
            pltpu.VMEM((BLOCKS - 1, REACH, BLOCK), BF16),
            pltpu.VMEM((2, LIVE, 256), BF16),
            pltpu.VMEM((2, LIVE, 256), BF16),
            pltpu.VMEM((LIVE, LANES), BF16),
            pltpu.VMEM((LIVE, 256), F32),
            pltpu.VMEM((LIVE, 256), F32),
            pltpu.VMEM((2, LIVE, LANES), F32),
            pltpu.VMEM((2, 2, LIVE, 256), F32),
        ],
        out_shape=[jax.ShapeDtypeStruct((LIVE, count * LANES), BF16)] * 3,
        us=us,
        name="attn_backward",
    )


GROUPS = 4


def put(out_ref, ids, values, quarter, base):
    me, here = ids
    count = out_ref.shape[0]
    rows = values.shape[0] // count
    for portion in range(count):
        out_ref[portion ^ me, quarter ^ here, base : base + rows, :] = values[portion * rows : portion * rows + rows]


def columns(values, which):
    return values[:, which * LANES : which * LANES + LANES]


def group_of_qkv(half, group, refs):
    normed_t_ref, lefts = refs[0], refs[1:]
    runs = len(lefts) // 3
    tall = normed_t_ref.shape[0] // 2
    height = 3 * tall // GROUPS
    parts = []
    first = group * height
    while first < (group + 1) * height:
        j, start = divmod(first, tall)
        rows = min(tall - start, (group + 1) * height - first)
        normed_t = normed_t_ref[pl.ds(pl.multiple_of(half * tall + start, 16), rows), :]
        parts.append(jnp.concatenate([dot(normed_t, lefts[3 * run + j][...]) for run in range(runs)], axis=1))
        first += rows
    return jnp.concatenate(parts, axis=0) if len(parts) > 1 else parts[0]


def ff_bwd_body(layer, top, runs, parts, id_ref, *refs):
    extra_refs, refs = refs[: 3 * runs + (runs > 0)], refs[3 * runs + (runs > 0) :]
    if top:
        (x_ref, low_ref, g_ref, low_t_ref, gain_ref, shift_ref, up_ref, up_bias_ref, down_ref, down_bias_ref, wo_ref,
         out_ref, mid_g_ref, att_g_ref, small_ref, up_bias_g_ref, kept_ref,
         act_ref, pre_ref, g_t_ref, normed_t_ref, mid_low_ref, mid_ref) = refs
    else:
        (mid_ref, g_ref, low_t_ref, gain_ref, shift_ref, up_ref, up_bias_ref, down_ref, wo_ref,
         mid_g_ref, att_g_ref, small_ref, up_bias_g_ref, sent_ref, kept_ref,
         act_ref, pre_ref, g_t_ref, normed_t_ref, mid_low_ref) = refs
    step = pl.program_id(0)
    hidden = up_ref.shape[1]
    quarters = kept_ref.shape[1]
    length = g_t_ref.shape[1]
    tiles = length // BLOCK
    share = hidden // quarters

    @pl.when(step == 0)
    def _():
        small_ref[...] = jnp.zeros_like(small_ref)
        up_bias_g_ref[...] = jnp.zeros_like(up_bias_g_ref)

    @pl.when(step < tiles)
    def _():
        if top:
            mid_ref[...] = x_ref[...]

            @pl.when(step < BLOCKS)
            def _():
                mid_ref[...] += dot(low_ref[...], wo_ref[...])

        rows = pl.ds(pl.multiple_of(step * BLOCK, BLOCK), BLOCK)
        mid = mid_ref[...]
        unit, rstd = normalize(mid)
        normed = (unit * gain_ref[layer, 1:2, :] + shift_ref[layer, 1:2, :]).astype(BF16)
        normed_t_ref[:, rows] = normed.T
        grad = g_ref[...]
        g_low = grad.astype(BF16)
        g_t_ref[:, rows] = g_low.T
        if top:
            total = mid + down_bias_ref[layer : layer + 1, :]
        back = jnp.zeros(grad.shape, F32)
        for quarter in range(quarters):
            cols = slice(quarter * share, quarter * share + share)
            pre = dot(normed, up_ref[:, cols]) + up_bias_ref[layer : layer + 1, cols]
            act, slope = gelu_terms(pre)
            act = act.astype(BF16)
            per_half = quarters // 2
            act_ref[quarter // per_half, rows, (quarter % per_half) * share : (quarter % per_half) * share + share] = act
            if top:
                total = total + dot(act, down_ref[cols, :])
            pre_low = (dot_nt(g_low, down_ref[cols, :]) * slope).astype(BF16)
            for which in range(share // LANES):
                pre_ref[which, rows, quarter * LANES : quarter * LANES + LANES] = columns(pre_low, which)
            up_bias_g_ref[:, cols] += jnp.sum(pre_low.astype(F32), axis=0, keepdims=True)
            back = back + dot_nt(pre_low, up_ref[:, cols])
        if top:
            out_ref[...] = total
        mid_g = grad + norm_pull(back, gain_ref[layer, 1:2, :], unit, rstd)
        mid_g_ref[...] = mid_g
        mid_low = mid_g.astype(BF16)
        small_ref[0:1, :] += jnp.sum(back * unit, axis=0, keepdims=True)
        small_ref[1:2, :] += jnp.sum(back, axis=0, keepdims=True)
        small_ref[2:3, :] += jnp.sum(g_low.astype(F32), axis=0, keepdims=True)

        @pl.when(step < BLOCKS)
        def _():
            mid_low_ref[rows, :] = mid_low
            att_g_ref[...] = dot_nt(mid_low, wo_ref[...])

    count = kept_ref.shape[0]
    if top:
        ids = (0, 0)
        halves = ((tiles, 0, kept_ref), (tiles + GROUPS, 1, kept_ref))
    else:
        ids = (id_ref[0] & (count - 1), id_ref[1])
        own = id_ref[0] // (parts // 2)
        halves = ((tiles, own ^ 1, sent_ref), (tiles + GROUPS, own, kept_ref))
    for first, half, end_ref in halves:
        for group in range(GROUPS):

            @pl.when(step == first + group)
            def _(half=half, group=group, end_ref=end_ref):
                wide = act_ref.shape[2] // GROUPS
                down = dot(g_t_ref[...], act_ref[half, :, group * wide : group * wide + wide])
                height = normed_t_ref.shape[0] * (share // LANES // 2) // GROUPS
                per_tile = normed_t_ref.shape[0] // height
                part = group % per_tile
                up = dot(normed_t_ref[part * height : part * height + height, :], pre_ref[half * (share // LANES // 2) + group // per_tile])
                tall = low_t_ref.shape[0] // 2 // GROUPS
                low_rows = pl.ds(pl.multiple_of(half * (low_t_ref.shape[0] // 2) + group * tall, tall), tall)
                out = dot(low_t_ref[low_rows, :], mid_low_ref[...])
                if runs:
                    extra = group_of_qkv(half, group, extra_refs)
                for quarter in range(quarters):
                    rows = slice(quarter * LANES, quarter * LANES + LANES)
                    pieces = [
                        jnp.concatenate([columns(down[rows], which) for which in range(wide // LANES)], axis=0),
                        columns(up, quarter),
                        columns(out, quarter),
                    ]
                    if runs:
                        pieces.append(columns(extra, quarter))
                    base = 0
                    for piece in pieces:
                        put(end_ref, ids, piece, quarter, base)
                        base += piece.shape[0] // count


def ff_bwd(layer, ids, parts, quarters, grad, low_t, gains, shifts, up, up_bias, down, wo, mid=None, top=None, qkv=None, after=()):
    length, width = grad.shape
    hidden = up.shape[2]
    tiles = length // BLOCK
    portions = parts // 2
    group = portions // GROUPS
    rows = pl.BlockSpec((BLOCK, width), lambda i, ids: (jnp.minimum(i, tiles - 1), 0))
    live = pl.BlockSpec((BLOCK, width), lambda i, ids: (jnp.minimum(i, BLOCKS - 1), 0))
    weights = [gains, shifts, up, up_bias, down] + ([top[2]] if top else []) + [wo]
    weight_specs = [constant(*gains.shape), constant(*shifts.shape), of_layer(layer, up), constant(*up_bias.shape), of_layer(layer, down)]
    weight_specs += ([constant(*top[2].shape)] if top else []) + [of_layer(layer, wo)]
    piece_rows = hidden // parts + width * (hidden // quarters // LANES) // parts + width // parts + (3 * width // parts if qkv else 0)
    extra = [qkv[0]] + [part for run in qkv[1] for part in run] if qkv else []
    end = (portions, quarters, piece_rows, LANES)

    def end_spec(first):
        return pl.BlockSpec((group,) + end[1:], lambda i, ids: (jnp.clip(i - first, 0, GROUPS - 1) ^ ((ids[0] & (portions - 1)) // group), 0, 0, 0))

    if top:
        ends = [pl.BlockSpec((group,) + end[1:], lambda i, ids: (jnp.clip(i - tiles, 0, 2 * GROUPS - 1), 0, 0, 0))]
        end_shapes = [(parts,) + end[1:]]
    else:
        ends = [end_spec(tiles), end_spec(tiles + GROUPS)]
        end_shapes = [end, end]
    got = call(
        functools.partial(ff_bwd_body, layer, bool(top), len(extra) // 3, parts),
        after,
        grid=(tiles + 2 * GROUPS,),
        prefetch=[ids],
        operands=extra + ([top[0], top[1]] if top else [mid]) + [grad, low_t] + weights,
        in_specs=[constant(*a.shape) for a in extra] + ([rows, live] if top else [rows]) + [rows, constant(*low_t.shape)] + weight_specs,
        out_specs=([rows] if top else []) + [rows, live, resident(8, width), resident(1, hidden)] + ends,
        scratch=[
            pltpu.VMEM((2, length, hidden // 2), BF16),
            pltpu.VMEM((hidden // quarters // LANES, length, quarters * LANES), BF16),
            pltpu.VMEM((width, length), BF16),
            pltpu.VMEM((width, length), BF16),
            pltpu.VMEM((LIVE, width), BF16),
        ] + ([pltpu.VMEM((BLOCK, width), F32)] if top else []),
        out_shape=([jax.ShapeDtypeStruct((length, width), F32)] if top else [])
        + [
            jax.ShapeDtypeStruct((length, width), F32),
            jax.ShapeDtypeStruct((LIVE, width), F32),
            jax.ShapeDtypeStruct((8, width), F32),
            jax.ShapeDtypeStruct((1, hidden), F32),
        ]
        + [jax.ShapeDtypeStruct(shape, F32) for shape in end_shapes],
        us=18.0,
        name="ff_backward",
    )
    return got if top else [None] + list(got)


def input_bwd_body(layer, runs, parts, order, ends, id_ref, *refs):
    left_refs = refs[: 3 * runs]
    w_ref, normed_t_ref, x_ref, gain_ref, mid_g_ref = refs[3 * runs : 3 * runs + 5]
    small_refs = refs[3 * runs + 5 : -4]
    if ends:
        out_ref, small_ref, sent_ref, kept_ref = refs[-4:]
    else:
        out_ref, small_ref = refs[-2:]
    step = pl.program_id(0)
    tiles = pl.num_programs(0) - (2 if ends else 0)

    @pl.when(step == 0)
    def _():
        small_ref[...] = jnp.zeros_like(small_ref)

    @pl.when(step < BLOCKS)
    def _():
        rows = pl.ds(pl.multiple_of(step * BLOCK, BLOCK), BLOCK)
        back = jnp.zeros(x_ref.shape, F32)
        for run in range(runs):
            for j in range(3):
                left = left_refs[3 * run + j]
                wide = left.shape[1]
                back = back + dot_nt(left[rows, :], w_ref[j, :, run * wide : run * wide + wide])
        unit, rstd = normalize(x_ref[...])
        out_ref[...] = mid_g_ref[...] + norm_pull(back, gain_ref[layer, 0:1, :], unit, rstd)
        small_ref[0:1, :] += jnp.sum(back * unit, axis=0, keepdims=True)
        small_ref[1:2, :] += jnp.sum(back, axis=0, keepdims=True)

    @pl.when((step >= BLOCKS) & (step < tiles))
    def _():
        out_ref[...] = mid_g_ref[...]

    if not ends:
        return
    count, quarters = sent_ref.shape[:2]
    ids = (id_ref[0] & (count - 1), id_ref[1])
    for when, flip, end_ref in ((tiles, 1, sent_ref), (tiles + 1, 0, kept_ref)):
        half = (id_ref[0] // (parts // 2)) ^ flip

        @pl.when(step == when)
        def _(half=half, end_ref=end_ref):
            tall = normed_t_ref.shape[0] // 2
            normed_t = normed_t_ref[pl.ds(pl.multiple_of(half * tall, tall), tall), :]
            totals = [jnp.concatenate([dot(normed_t, left_refs[3 * run + j][...]) for run in range(runs)], axis=1) for j in range(3)]
            for quarter in range(quarters):
                put(end_ref, ids, jnp.concatenate([columns(total, quarter) for total in totals], axis=0), quarter, 0)
            base = 3 * tall // count
            if order:
                room = end_ref.shape[2] - base
                end_ref[:, :, base:, :] = jnp.zeros((count, quarters, room, LANES), F32)

                @pl.when(half == 0)
                def _():
                    for at, (array, row, first) in enumerate(order):
                        portion, offset = divmod(at, room)
                        source = small_ref if array < 0 else small_refs[array]
                        per = source.shape[1] // quarters
                        for quarter in range(quarters):
                            start = quarter * per + first
                            end_ref[portion ^ ids[0], quarter ^ ids[1], base + offset : base + offset + 1, :] = source[row : row + 1, start : start + LANES]


def input_bwd(layer, ids, parts, quarters, proj_g, w, normed_t, x, gains, mid_g, smalls=(), order=(), ends=True, after=()):
    length, width = x.shape
    tiles = length // BLOCK
    rows = pl.BlockSpec((BLOCK, width), lambda i, ids: (jnp.minimum(i, tiles - 1), 0))
    lefts = [part for run in proj_g for part in run]
    small_rows = small_rows_of(len(order), parts)
    end = (parts // 2, quarters, 3 * width // parts + small_rows, LANES)
    return call(
        functools.partial(input_bwd_body, layer, len(proj_g), parts, tuple(order), ends),
        after,
        grid=(tiles + (2 if ends else 0),),
        prefetch=[ids],
        operands=lefts + [w, normed_t, x, gains, mid_g] + list(smalls),
        in_specs=[constant(*a.shape) for a in lefts]
        + [of_layer(layer, w), constant(*normed_t.shape), rows, constant(*gains.shape), rows]
        + [constant(*a.shape) for a in smalls],
        out_specs=[rows, resident(8, width)] + [resident(*end)] * (2 if ends else 0),
        out_shape=[jax.ShapeDtypeStruct((length, width), F32), jax.ShapeDtypeStruct((8, width), F32)] + [jax.ShapeDtypeStruct(end, F32)] * (2 if ends else 0),
        us=1.0,
        name="input_backward",
    )


def small_rows_of(count, parts):
    return -(-count // (8 * parts)) * 8


def cut_of(rows):
    return rows // 16 * 8 if rows >= 16 else rows // 2


def fork_body(kept_ref, got_ref, *ends):
    portions = kept_ref.shape[0]
    cut = ends[0].shape[2]
    for slot in range(portions):
        upper, lower = ends[slot // (portions // 2)], ends[2 + slot % 2]
        upper[slot % (portions // 2)] = kept_ref[slot, :, :cut] + got_ref[slot, :, :cut]
        lower[slot // 2] = kept_ref[slot, :, cut:] + got_ref[slot, :, cut:]


def fork(kept, got, after):
    portions, quarters, rows, _ = kept.shape
    cut = cut_of(rows)
    ends = [(portions // 2, quarters, n, LANES) for n in (cut, cut, rows - cut, rows - cut)]
    by_quarter = lambda shape: pl.BlockSpec((shape[0], 1) + shape[2:], lambda i: (0, i, 0, 0))
    return call(
        fork_body,
        after,
        grid=(quarters,),
        prefetch=[],
        operands=[kept, got],
        in_specs=[by_quarter(kept.shape)] * 2,
        out_specs=[by_quarter(end) for end in ends],
        out_shape=[jax.ShapeDtypeStruct(end, F32) for end in ends],
        us=3.0,
        name="fork_terms",
    )


def add_body(count, *refs):
    outs = refs[2 * count :]
    for which in range(count):
        for side in range(2):
            outs[2 * which + side][...] = refs[2 * which][:, side] + refs[2 * which + 1][:, side]


def add_streams(streams, wheres, after):
    operands, shapes = [], []
    for pair, where in zip(streams, wheres):
        shape = pair[0].shape
        flat = (math.prod(shape[:where]), 2, math.prod(shape[where + 1 : -2])) + shape[-2:]
        operands += [part.reshape(flat) for part in pair]
        shapes.append((flat[0],) + flat[2:])
    outs = [shape for shape in shapes for _ in range(2)]
    got = call(
        functools.partial(add_body, len(streams)),
        after,
        grid=(1,),
        prefetch=[],
        operands=operands,
        in_specs=[constant(*a.shape) for a in operands],
        out_specs=[resident(*shape) for shape in outs],
        out_shape=[jax.ShapeDtypeStruct(shape, F32) for shape in outs],
        us=1.5,
        name="add_terms",
    )
    results = []
    for which in range(len(got) // 2):
        shape, where = streams[which][0].shape, wheres[which]
        lead = shape[:where] + shape[where + 1 : -2]
        results.append(tuple(part.reshape(lead + part.shape[-2:]) for part in got[2 * which : 2 * which + 2]))
    return results


def pairs_body(count, *refs):
    kept_ref, sent_ref = refs[2 * count :]
    first = 0
    for which in range(count):
        one, two = refs[2 * which], refs[2 * which + 1]
        rows = one.shape[-2]
        for out_ref, side in ((kept_ref, 0), (sent_ref, 1)):
            out_ref[:, first : first + rows, :] = one[:, side] + two[:, side]
        first += rows


def add_pairs(streams, after):
    operands = [part.reshape((part.shape[0] // 2, 2) + part.shape[1:]) for pair in streams for part in pair]
    shape = (operands[0].shape[0], sum(pair[0].shape[1] for pair in streams), LANES)
    return call(
        functools.partial(pairs_body, len(streams)),
        after,
        grid=(1,),
        prefetch=[],
        operands=operands,
        in_specs=[constant(*a.shape) for a in operands],
        out_specs=[resident(*shape)] * 2,
        out_shape=[jax.ShapeDtypeStruct(shape, F32)] * 2,
        us=1.5,
        name="add_pairs",
    )


def last_add_body(counts, *refs):
    upper_ref, lower_ref = refs[-2:]
    cut = upper_ref.shape[0]
    first, base = 0, 0
    for count in counts:
        total = sum(ref[...] for ref in refs[first : first + count])
        first += count
        rows = total.shape[0]
        split = min(max(cut - base, 0), rows)
        if split:
            upper_ref[base : base + split, :] = total[:split]
        if split < rows:
            lower_ref[base + split - cut : base + rows - cut, :] = total[split:]
        base += rows


def last_add(runs, after):
    operands = [term for run in runs for term in run]
    rows = sum(run[0].shape[0] for run in runs)
    cut = cut_of(rows)
    return call(
        functools.partial(last_add_body, tuple(len(run) for run in runs)),
        after,
        grid=(1,),
        prefetch=[],
        operands=operands,
        in_specs=[constant(*a.shape) for a in operands],
        out_specs=[resident(cut, LANES), resident(rows - cut, LANES)],
        out_shape=[jax.ShapeDtypeStruct((cut, LANES), F32), jax.ShapeDtypeStruct((rows - cut, LANES), F32)],
        us=1.5,
        name="last_terms",
    )


def hold_body(*refs):
    del refs


def hold(block, after):
    return call(
        hold_body,
        after,
        grid=(1,),
        prefetch=[],
        operands=[block],
        in_specs=[pl.BlockSpec(memory_space=pl.ANY)],
        out_specs=pl.BlockSpec(memory_space=pl.ANY),
        out_shape=jax.ShapeDtypeStruct(block.shape, block.dtype),
        aliases=[(0, 0)],
        us=1.0,
        name="hold",
    )


def swap(block, axis_name, bit):
    return lax.ppermute(block, axis_name, [(i, i ^ bit) for i in range(lax.axis_size(axis_name))])


def bits_of(extent):
    return [1 << i for i in range(extent.bit_length() - 1)]


class Line:
    def __init__(self):
        self.last = []

    def __call__(self, function, *args, **kwargs):
        made = function(*args, after=self.last, **kwargs)
        leaves = jax.tree.leaves(made)
        self.last = [min(leaves, key=lambda a: a.size)]
        return made

    def wait(self, *chains):
        self.last = self.last + [array for chain in chains for array in chain.pending]


def scatter(line, sent, kept, parts, quarters):
    dp_bits, batch_bits = bits_of(parts), bits_of(quarters)
    near, far = dp_bits[0], dp_bits[1:]
    got = swap(sent, "dp", near)
    yield [got]
    ends = line(fork, kept, got)
    names = [("dp", bit) for bit in far] + [("batch", bit) for bit in batch_bits[::-1]]
    streams, left = [], []
    for which, order in enumerate((far, far[::-1])):
        kept, sent = ends[2 * which : 2 * which + 2]
        left.append([name for name in names if name != ("dp", order[0])])
        kept, sent = (part.reshape((2,) * len(left[-1]) + part.shape[2:]) for part in (kept, sent))
        streams.append((kept, swap(sent, "dp", order[0])))
    yield [got for _, got in streams]
    for bits in zip(far[1:], far[::-1][1:]):
        wheres = [names_left.index(("dp", bit)) for names_left, bit in zip(left, bits)]
        results = line(add_streams, streams, wheres)
        for which, bit in enumerate(bits):
            left[which].remove(("dp", bit))
            streams[which] = (results[which][0], swap(results[which][1], "dp", bit))
        yield [got for _, got in streams]
    streams = [tuple(part.reshape((quarters,) + part.shape[-2:]) for part in pair) for pair in streams]
    for bit in batch_bits:
        kept, sent = line(add_pairs, streams)
        streams = [(kept, swap(sent, "batch", bit))]
        yield [streams[0][1]]
    return [part[0] for part in streams[0]]


def spread(halves, parts):
    dp_bits = bits_of(parts)
    near, far = dp_bits[0], dp_bits[1:]
    streams = list(halves)
    names = [[], []]
    for bits in zip(far[::-1], far):
        moved = [swap(stream, "dp", bit) for stream, bit in zip(streams, bits)]
        yield moved
        for which, bit in enumerate(bits):
            names[which].append(bit)
            names[which].sort()
            streams[which] = jnp.stack([streams[which], moved[which]], axis=names[which].index(bit))
    block = jnp.concatenate(streams, axis=-2)
    block = block.reshape(parts // 2, block.shape[-2], LANES)
    moved = swap(block, "dp", near)
    yield [moved]
    return block, moved


class Chain:
    def __init__(self, steps):
        self.steps, self.result, self.pending = steps, None, []

    def step(self):
        if self.result is None:
            try:
                self.pending = next(self.steps)
            except StopIteration as stop:
                self.result = stop.value

    def finish(self):
        while self.result is None:
            self.step()
        return self.result


def unpack_body(names, bases, pieces, inputs, filled, id_ref, *refs):
    out_refs = dict(zip(names, refs[inputs + filled :]))
    down_ref, small_ref = refs[-2:]
    me = id_ref[0] if inputs == 2 else 0
    for top in range(inputs):
        ref = refs[top]
        portions = ref.shape[0]
        for slot in range(portions):
            portion = (slot + top * portions) ^ me
            half = portions * inputs // 2
            upper, inner = portion // half, portion % half
            for name, layer, first, rows in pieces:
                values = ref[slot, first : first + rows, :]
                if name == "small":
                    small_ref[pl.ds(pl.multiple_of(portion * rows, 8), rows), :] = values
                    continue
                out_ref = out_refs[name]
                layer = layer - bases[name]
                if name == "qkv":
                    width = out_ref.shape[1] // 3
                    unit = math.gcd(rows, width // 2)
                    for k in range(0, rows, unit):
                        flat = inner * rows + k
                        start = (flat // (width // 2)) * width + upper * (width // 2) + flat % (width // 2)
                        out_ref[layer, pl.ds(pl.multiple_of(start, 8), unit), :] = values[k : k + unit]
                elif name == "up":
                    height = out_ref.shape[1]
                    flat = portion * rows
                    tile, start = flat // height, flat % height
                    out_ref[layer, pl.ds(pl.multiple_of(start, 8), rows), pl.ds(pl.multiple_of(tile * LANES, LANES), LANES)] = values
                elif name == "down":
                    down_ref[pl.ds(pl.multiple_of(portion * rows, 8), rows), :] = values
                else:
                    out_ref[layer, pl.ds(pl.multiple_of(portion * rows, 8), rows), :] = values
    if "down" in out_refs:
        for first in range(0, down_ref.shape[0], LANES):
            out_refs["down"][0, first : first + LANES, :] = down_ref[first : first + LANES, :].T
    if "gains" in out_refs:
        layers, wide = out_refs["up_bias"].shape
        row = 0
        for layer in range(layers):
            for name, count in (("gains", 2), ("shifts", 2)):
                out_refs[name][layer] = small_ref[row : row + count, :]
                row += count
            for k in range(wide // LANES):
                out_refs["up_bias"][layer : layer + 1, k * LANES : k * LANES + LANES] = small_ref[row : row + 1, :]
                row += 1
            out_refs["down_bias"][layer : layer + 1, :] = small_ref[row : row + 1, :]
            row += 1


def unpack(ids, pair, pieces, layers, width, hidden, quarters, filled=(), after=()):
    shapes = {"down": (layers, hidden, LANES), "up": (layers, width, hidden // quarters), "out": (layers, width, LANES), "qkv": (layers, 3 * width, LANES)}
    found = {name: [layer for piece, layer, _, _ in pieces if piece == name] for name in shapes}
    names = tuple(name for name in shapes if found[name])
    bases = {name: min(found[name]) for name in names}
    out_specs = [
        pl.BlockSpec((len(found[name]),) + shapes[name][1:], lambda *_, name=name: (bases[name] // len(found[name]), 0, 0)) for name in names
    ]
    out_shape = [jax.ShapeDtypeStruct(shapes[name], F32) for name in names]
    small = [rows for piece, _, _, rows in pieces if piece == "small"]
    if small:
        names += ("gains", "shifts", "up_bias", "down_bias")
        for shape in ((layers, 2, LANES), (layers, 2, LANES), (layers, hidden // quarters), (layers, LANES)):
            out_specs.append(resident(*shape))
            out_shape.append(jax.ShapeDtypeStruct(shape, F32))
    return call(
        functools.partial(unpack_body, names, bases, pieces, len(pair), len(filled)),
        after,
        grid=(1,),
        prefetch=[ids],
        operands=list(pair) + list(filled),
        in_specs=[constant(*a.shape) for a in pair] + [pl.BlockSpec(memory_space=pl.ANY)] * len(filled),
        out_specs=out_specs,
        scratch=[
            pltpu.VMEM((hidden if found["down"] else 8, LANES), F32),
            pltpu.VMEM((len(pair) * pair[0].shape[0] * small[0] if small else 8, LANES), F32),
        ],
        out_shape=out_shape,
        aliases=[(len(pair) + which, which) for which in range(len(filled))],
        us=4.0,
        name="unpack",
    )


def reverse_bits(value, extent):
    return sum(((value // bit) % 2) * (extent // (2 * bit)) for bit in bits_of(extent))


def per_device(activations_in, gains, shifts, qkv_weights, out_weights, up_weights, up_bias, down_weights, down_bias, feature_maps, lengths, cotangent):
    layers, _, width = gains.shape
    hidden = up_bias.shape[1]
    parts, quarters = lax.axis_size("dp"), lax.axis_size("batch")
    ids = jnp.stack([reverse_bits(lax.axis_index("dp"), parts), lax.axis_index("batch")]).astype(jnp.int32)
    proteins = lengths[0]
    pairs = feature_maps.shape[1] // 2
    half = pairs // 2
    line = Line()
    last = layers - 1
    x, saved = activations_in[0], []
    for layer in range(layers):
        normed_t, *kept, low, low_t = line(attn_fwd, layer, proteins, x, gains, shifts, qkv_weights, feature_maps)
        phi_q, phi_k, uq, uk, v, att, rden = kept
        mid = None
        before = x
        if layer < last:
            x, mid = line(ff_fwd, layer, x, low, out_weights, gains, shifts, up_weights, up_bias, down_weights, down_bias)
        saved.append((before, normed_t, (att, rden, phi_q, phi_k, uq, uk, v), low, low_t, mid))

    smalls = [None] * layers

    def ff_part(layer, grad, top=None, qkv=None):
        _, _, _, low, low_t, mid = saved[layer]
        out, mid_g, att_g, small_two, up_bias_g, *ends = line(
            ff_bwd, layer, ids, parts, quarters, grad, low_t, gains, shifts, up_weights, up_bias, down_weights, out_weights, mid=mid, top=top, qkv=qkv
        )
        smalls[layer] = [None, small_two, up_bias_g]
        return out, mid_g, att_g, ends[0] if top else Chain(scatter(line, *ends, parts, quarters))

    def attn_part(layer, att_g, first, count, us):
        return line(attn_bwd, layer, proteins, att_g, *saved[layer][2], feature_maps, first, count, us)

    def input_part(layer, proj_g, mid_g, **rest):
        grad, smalls[layer][0], *ends = line(
            input_bwd, layer, ids, parts, quarters, proj_g, qkv_weights, saved[layer][1], saved[layer][0], gains, mid_g, **rest
        )
        return grad, Chain(scatter(line, *ends, parts, quarters)) if ends else None

    wide = hidden // quarters // LANES
    ff_rows = (hidden // parts, width * wide // parts, width // parts)
    ff_total, qkv_rows = sum(ff_rows), 3 * width // parts
    sizes = (layers, width, hidden, quarters)

    def ff_pieces(layer, base):
        return (("down", layer, base, ff_rows[0]), ("up", layer, base + ff_rows[0], ff_rows[1]), ("out", layer, base + ff_rows[0] + ff_rows[1], ff_rows[2]))

    values, mid_g, att_g, first = ff_part(1, cotangent[0], (x, saved[1][3], down_bias))
    first = lax.psum_scatter(first.reshape(-1, LANES), "dp", scatter_dimension=0, tiled=True)
    runs = [attn_part(1, att_g, 0, pairs, 1.0)]
    grad, _ = input_part(1, runs, mid_g, ends=False)
    _, mid_g, att_g, second = ff_part(0, grad, qkv=(saved[1][1], runs))
    second.step()
    runs = [attn_part(0, att_g, 0, half, 60.0)]
    second.step()
    first = lax.psum_scatter(line(hold, first), "batch", scatter_dimension=0, tiled=True)
    runs.append(attn_part(0, att_g, half, pairs - half, 1.0))
    flat = [array for layer in range(layers) for array in smalls[layer]]
    order = []
    for layer in range(layers):
        one, two, bias = (3 * layer + k for k in range(3))
        order += [(one, 0, 0), (two, 0, 0), (one, 1, 0), (two, 1, 0)] + [(bias, 0, k * LANES) for k in range(wide)] + [(two, 2, 0)]
    present = [k for k, array in enumerate(flat) if array is not None]
    order = [(present.index(array) if array in present else -1, row, first_col) for array, row, first_col in order]
    grad, third = input_part(0, runs, mid_g, smalls=[flat[k] for k in present], order=order)
    third.step()
    second.step()
    second.step()
    third.step()
    first = lax.all_gather(line(hold, first), "dp", tiled=True).reshape(parts, -1, LANES)
    third.step()
    second.step()
    third.step()
    third.step()
    down, up, out = line(unpack, ids, [first], ff_pieces(1, 0), *sizes)
    pair = Chain(spread(line(last_add, [second.finish(), third.finish()]), parts)).finish()
    pieces = ff_pieces(0, 0) + (("qkv", 1, ff_total, qkv_rows), ("qkv", 0, ff_total + qkv_rows, qkv_rows))
    pieces += (("small", 0, ff_total + 2 * qkv_rows, small_rows_of(len(order), parts)),)
    down, up, out, qkv, gains_g, shifts_g, up_bias_g, down_bias_g = line(unpack, ids, pair, pieces, *sizes, (down, up, out))
    return (
        values[None],
        grad[None],
        gains_g,
        shifts_g,
        qkv.reshape(layers, 3, width, LANES),
        out,
        up,
        up_bias_g,
        down,
        down_bias_g,
    )


def solution(mesh):
    rows = P(("dp", "batch"), None, None)
    return jax.shard_map(
        per_device,
        mesh=mesh,
        in_specs=(rows,) + (P(),) * 9 + (P(("dp", "batch"), None), rows),
        out_specs=(
            rows,
            rows,
            P(None, None, "batch"),
            P(None, None, "batch"),
            P(None, None, None, "batch"),
            P(None, None, "batch"),
            P(None, None, "batch"),
            P(None, "batch"),
            P(None, None, "batch"),
            P(None, "batch"),
        ),
        check_vma=False,
    )
```

```python
import functools
import math

import jax
import jax.numpy as jnp
from jax import lax
from jax.experimental import pallas as pl
from jax.experimental.pallas import tpu as pltpu
from jax.sharding import PartitionSpec as P

BLOCK = 256
BLOCKS = 3
LIVE = BLOCK * BLOCKS
REACH = 160
LANES = 128
NDOC = 6
MIB = 1 << 20
F32 = jnp.float32
BF16 = jnp.bfloat16
LOG2E = 1.4426950408889634
NT = (((1,), (1,)), ((), ()))


def dot(a, b):
    return jnp.dot(a, b, preferred_element_type=F32)


def dot_nt(a, b):
    return lax.dot_general(a, b, NT, preferred_element_type=F32)


def params_for(mib):
    return pltpu.CompilerParams(vmem_limit_bytes=mib * MIB)


def call(body, after, *, grid, in_specs, out_specs, out_shape, prefetch, operands, scratch=(), aliases=(), mib=63, us=3.0, name):
    scalars, count = len(prefetch), len(after)

    def ordered(*refs):
        body(*refs[:scalars], *refs[scalars + count :])

    return pl.pallas_call(
        ordered,
        grid_spec=pltpu.PrefetchScalarGridSpec(
            num_scalar_prefetch=scalars,
            grid=grid,
            in_specs=[pl.BlockSpec(memory_space=pl.ANY)] * count + list(in_specs),
            out_specs=out_specs,
            scratch_shapes=list(scratch),
        ),
        out_shape=out_shape,
        input_output_aliases={scalars + count + operand: output for operand, output in aliases},
        compiler_params=params_for(mib),
        cost_estimate=pl.CostEstimate(flops=int(us * 1.15e9), bytes_accessed=0, transcendentals=0),
        name=name,
    )(*prefetch, *after, *operands)


def constant(*shape):
    return pl.BlockSpec(shape, lambda *_: (0,) * len(shape), pipeline_mode=pl.Buffered(1))


def resident(*shape):
    return pl.BlockSpec(shape, lambda *_: (0,) * len(shape))


def of_layer(layer, array):
    return pl.BlockSpec((None,) + array.shape[1:], lambda *_: (layer,) + (0,) * (array.ndim - 1), pipeline_mode=pl.Buffered(1))


def anywhere():
    return pl.BlockSpec(memory_space=pl.ANY)


def fetch(step, begin, end, sources, targets, sems):
    copies = [pltpu.make_async_copy(source, target, sems.at[k]) for k, (source, target) in enumerate(zip(sources, targets))]

    @pl.when(step == begin)
    def _():
        for copy in copies:
            copy.start()

    @pl.when(step == end)
    def _():
        for copy in copies:
            copy.wait()


def normalize(values):
    centered = values - jnp.mean(values, axis=-1, keepdims=True)
    rstd = lax.rsqrt(jnp.mean(centered * centered, axis=-1, keepdims=True) + 1e-05)
    return centered * rstd, rstd


def norm_pull(grad, gain, unit, rstd):
    p = grad * gain
    return rstd * (p - jnp.mean(p, axis=-1, keepdims=True) - unit * jnp.mean(p * unit, axis=-1, keepdims=True))


def split_two(values):
    high = values.astype(BF16)
    return high, (values - high.astype(F32)).astype(BF16)


def protein_ids(len_ref, position):
    bound = jnp.int32(0)
    ids = jnp.zeros(position.shape, jnp.int32)
    for j in range(NDOC):
        bound = bound + len_ref[j]
        ids = ids + (position >= bound).astype(jnp.int32)
    return ids


def token_count(len_ref):
    total = jnp.int32(0)
    for j in range(NDOC):
        total = total + len_ref[j]
    return total


def pair_mask(len_ref, shape, first_row, first_col, causal_rows):
    rows = lax.broadcasted_iota(jnp.int32, shape, 0) + first_row
    cols = lax.broadcasted_iota(jnp.int32, shape, 1) + first_col
    same = protein_ids(len_ref, rows) == protein_ids(len_ref, cols)
    ordered = (rows >= cols) if causal_rows else (cols >= rows)
    return jnp.where(same & ordered, 1.0, 0.0).astype(BF16)


def fill_masks(len_ref, own_ref, before_ref, causal_rows):
    for b in range(BLOCKS):
        own_ref[b] = pair_mask(len_ref, (BLOCK, BLOCK), b * BLOCK, b * BLOCK, causal_rows)
    for b in range(1, BLOCKS):
        if causal_rows:
            before_ref[b - 1] = pair_mask(len_ref, (REACH, BLOCK), b * BLOCK, (b - 1) * BLOCK, True)
        else:
            before_ref[b - 1] = pair_mask(len_ref, (REACH, BLOCK), b * BLOCK - REACH, b * BLOCK, False)


def attn_fwd_body(layer, step, low_ref, low_t_ref, len_ref, x_ref, gain_ref, shift_ref, w_ref, fm_ref, normed_t_ref, phi_q_ref, phi_k_ref, uq_ref, uk_ref,
                  v_ref, att_ref, rden_ref, normed_ref, proj_ref, own_ref, before_ref, num_ref):
    columns_here = pl.ds(pl.multiple_of(step * LANES, LANES), LANES)

    @pl.when(step == 0)
    def _():
        fill_masks(len_ref, own_ref, before_ref, True)
        for b in range(BLOCKS):
            rows = pl.ds(b * BLOCK, BLOCK)
            unit, _ = normalize(x_ref[rows, :])
            normed = (unit * gain_ref[layer, 0:1, :] + shift_ref[layer, 0:1, :]).astype(BF16)
            normed_ref[rows, :] = normed
            normed_t_ref[:, rows] = normed.T
        for j in range(3):
            for half in range(2):
                got = dot(normed_ref[...], w_ref[j, :, half * 256 : half * 256 + 256])
                proj_ref[j, 2 * half] = got[:, :LANES]
                proj_ref[j, 2 * half + 1] = got[:, LANES:]

    lane = lax.broadcasted_iota(jnp.int32, (BLOCK, LANES), 1) < 64
    uq_ref[0] = proj_ref[0, step]
    uk_ref[0] = proj_ref[1, step]
    v_ref[0] = proj_ref[2, step].astype(BF16)
    first_head = lax.broadcasted_iota(jnp.int32, (LANES, 256), 0) < 64
    minus = [jnp.where(first_head, -1.0, 0.0).astype(BF16), jnp.where(first_head, 0.0, -1.0).astype(BF16)]
    stacked = []
    for head in range(2):
        high, low = split_two(fm_ref[head] * (64.0 ** (-0.25) * LOG2E))
        stacked.append(jnp.concatenate([high, low, high, low, minus[head], minus[head]], axis=0))
    for which, phi_ref in ((0, phi_q_ref), (1, phi_k_ref)):
        for b in range(BLOCKS):
            rows = pl.ds(b * BLOCK, BLOCK)
            u = proj_ref[which, step, rows, :]
            turned = pltpu.roll(u, 64, 1)
            squares = split_two(u * u * (LOG2E / 16.0) + 0.0625)
            for head in range(2):
                twice = jnp.where(lane, u, turned) if head == 0 else jnp.where(lane, turned, u)
                exponent = dot(jnp.concatenate(split_two(twice) + squares, axis=1), stacked[head])
                phi_ref[head, rows, :] = jnp.exp2(exponent).astype(BF16)
    ones = jnp.ones((BLOCK, LANES), BF16)
    for b in range(BLOCKS):
        rows = pl.ds(b * BLOCK, BLOCK)
        v_now = jnp.concatenate([v_ref[0, rows, :], ones], axis=1)
        for head in range(2):
            weights = dot_nt(phi_q_ref[head, rows, :], phi_k_ref[head, rows, :]).astype(BF16) * own_ref[b]
            num_ref[head] = dot(weights, v_now)
            if b > 0:
                earlier = pl.ds((b - 1) * BLOCK, BLOCK)
                v_before = jnp.concatenate([v_ref[0, earlier, :], ones], axis=1)
                weights = dot_nt(phi_q_ref[head, pl.ds(b * BLOCK, REACH), :], phi_k_ref[head, earlier, :])
                num_ref[head, :REACH, :] += dot(weights.astype(BF16) * before_ref[b - 1], v_before)
        rden = 1.0 / jnp.where(lane, num_ref[0, :, LANES:], num_ref[1, :, LANES:])
        attended = jnp.where(lane, num_ref[0, :, :LANES], num_ref[1, :, :LANES]) * rden
        position = lax.broadcasted_iota(jnp.int32, (BLOCK, LANES), 0) + b * BLOCK
        attended = jnp.where(position < token_count(len_ref), attended, 0.0)
        rden_ref[0, rows, :] = rden
        att_ref[0, rows, :] = attended
        low = attended.astype(BF16)
        low_ref[rows, columns_here] = low
        low_t_ref[columns_here, rows] = low.T


def gelu_terms(pre):
    lifted = 0.5 + 0.5 * lax.erf(pre * math.sqrt(0.5))
    return pre * lifted, lifted + pre * (jnp.exp2(pre * pre * (-0.5 * LOG2E)) * (1.0 / math.sqrt(2.0 * math.pi)))


def ff_fwd_body(layer, step, x_ref, low_ref, wo_ref, gain_ref, shift_ref, up_ref, up_bias_ref, down_ref, down_bias_ref, out_ref, mid_ref):
    mid_ref[...] = x_ref[...]

    @pl.when(step < BLOCKS)
    def _():
        mid_ref[...] += dot(low_ref[...], wo_ref[...])

    mid = mid_ref[...]
    unit, _ = normalize(mid)
    normed = (unit * gain_ref[layer, 1:2, :] + shift_ref[layer, 1:2, :]).astype(BF16)
    total = mid + down_bias_ref[layer : layer + 1, :]
    for first in range(0, up_ref.shape[1], 512):
        cols = slice(first, first + 512)
        pre = dot(normed, up_ref[:, cols]) + up_bias_ref[layer : layer + 1, cols]
        act = (pre * (0.5 + 0.5 * lax.erf(pre * math.sqrt(0.5)))).astype(BF16)
        total = total + dot(act, down_ref[cols, :])
    out_ref[...] = total


def attn_bwd_body(len_ref, att_g_ref, att_ref, rden_ref, phi_q_ref, phi_k_ref, uq_ref, uk_ref, v_ref, fm_ref,
                  dq_ref, dk_ref, dv_ref, own_ref, before_ref, own_t_ref, before_t_ref,
                  x_ref, y_ref, dn_ref, d_phi_q, d_phi_k, d_v, raw_ref):
    step = pl.program_id(0)

    @pl.when(step == 0)
    def _():
        fill_masks(len_ref, own_ref, before_ref, True)
        fill_masks(len_ref, own_t_ref, before_t_ref, False)

    lane = lax.broadcasted_iota(jnp.int32, (BLOCK, LANES), 1) < 64
    one = jnp.ones((BLOCK, LANES), BF16)
    for b in range(BLOCKS):
        rows = pl.ds(b * BLOCK, BLOCK)
        position = lax.broadcasted_iota(jnp.int32, (BLOCK, LANES), 0) + b * BLOCK
        dn = jnp.where(position < token_count(len_ref), att_g_ref[rows, :] * rden_ref[0, rows, :], 0.0)
        turned = pltpu.roll(-(dn * att_ref[0, rows, :]), 64, 1)
        dn_ref[rows, :] = dn.astype(BF16)
        v_low = v_ref[0, rows, :]
        for head in range(2):
            first = lane if head == 0 else jnp.logical_not(lane)
            high, low = split_two(jnp.where(first, dn, turned))
            x_ref[head, rows, :] = jnp.concatenate([high, low], axis=1)
            y = jnp.where(first, v_low.astype(F32), 1.0).astype(BF16)
            y_ref[head, rows, :] = jnp.concatenate([y, y], axis=1)
    for head in range(2):
        for b in range(BLOCKS):
            rows = pl.ds(b * BLOCK, BLOCK)
            x, y = x_ref[head, rows, :], y_ref[head, rows, :]
            phi_q, phi_k = phi_q_ref[head, rows, :], phi_k_ref[head, rows, :]
            d_kernel = dot_nt(x, y).astype(BF16) * own_ref[b]
            d_phi_q[rows, :] = dot(d_kernel, phi_k)
            d_kernel_t = dot_nt(y, x).astype(BF16) * own_t_ref[b]
            d_phi_k[rows, :] = dot(d_kernel_t, phi_q)
            kernel_t = dot_nt(phi_k, phi_q).astype(BF16) * own_t_ref[b]
            d_v[head, rows, :] = dot(kernel_t, dn_ref[rows, :])
            if b > 0:
                earlier = pl.ds((b - 1) * BLOCK, BLOCK)
                top = pl.ds(b * BLOCK, REACH)
                bottom = pl.ds(b * BLOCK - REACH, REACH)
                d_kernel = dot_nt(x_ref[head, top, :], y_ref[head, earlier, :]).astype(BF16) * before_ref[b - 1]
                d_phi_q[top, :] += dot(d_kernel, phi_k_ref[head, earlier, :])
                d_kernel_t = dot_nt(y_ref[head, bottom, :], x).astype(BF16) * before_t_ref[b - 1]
                d_phi_k[bottom, :] += dot(d_kernel_t, phi_q)
                kernel_t = dot_nt(phi_k_ref[head, bottom, :], phi_q).astype(BF16) * before_t_ref[b - 1]
                d_v[head, bottom, :] += dot(kernel_t, dn_ref[rows, :])
        high, low = split_two(fm_ref[head])
        stacked = jnp.concatenate([high, low, jnp.ones((LANES, 256), BF16)], axis=0)
        for which, d_phi, phi_ref in ((0, d_phi_q, phi_q_ref), (1, d_phi_k, phi_k_ref)):
            for b in range(BLOCKS):
                rows = pl.ds(b * BLOCK, BLOCK)
                d_projected = (d_phi[rows, :] * phi_ref[head, rows, :].astype(F32)).astype(BF16)
                raw_ref[which, head, rows, :] = dot_nt(d_projected, stacked)
    for b in range(BLOCKS):
        rows = pl.ds(b * BLOCK, BLOCK)
        for which, u_ref, out_ref in ((0, uq_ref, dq_ref), (1, uk_ref, dk_ref)):
            parts = []
            for head in range(2):
                raw = raw_ref[which, head, rows, :LANES]
                parts.append(raw + pltpu.roll(raw, 64, 1))
            along = jnp.where(lane, parts[0], parts[1])
            total = jnp.where(lane, raw_ref[which, 0, rows, LANES:], raw_ref[which, 1, rows, LANES:])
            grad = along * (64.0 ** (-0.25)) - u_ref[0, rows, :] * total * 0.125
            out_ref[rows, :] = grad.astype(BF16)
        dv_ref[rows, :] = jnp.where(lane, d_v[0, rows, :], d_v[1, rows, :]).astype(BF16)


def attn_bwd(layer, lengths, att_g, att, rden, phi_q, phi_k, uq, uk, v, fm, first, count, us, after=()):
    per_pair = pl.BlockSpec((1, LIVE, LANES), lambda p, *_: (first + p, 0, 0))
    per_head = pl.BlockSpec((2, LIVE, 256), lambda p, *_: (first + p, 0, 0))
    return call(
        attn_bwd_body,
        after,
        grid=(count,),
        prefetch=[lengths],
        operands=[att_g, att, rden, phi_q, phi_k, uq, uk, v, fm],
        in_specs=[pl.BlockSpec((LIVE, LANES), lambda p, *_: (0, first + p)), per_pair, per_pair, per_head, per_head, per_pair, per_pair, per_pair,
                  pl.BlockSpec((None, 2) + fm.shape[2:], lambda p, *_: (layer, first + p, 0, 0))],
        out_specs=[pl.BlockSpec((LIVE, LANES), lambda p, *_: (0, p))] * 3,
        scratch=[
            pltpu.VMEM((BLOCKS, BLOCK, BLOCK), BF16),
            pltpu.VMEM((BLOCKS - 1, REACH, BLOCK), BF16),
            pltpu.VMEM((BLOCKS, BLOCK, BLOCK), BF16),
            pltpu.VMEM((BLOCKS - 1, REACH, BLOCK), BF16),
            pltpu.VMEM((2, LIVE, 256), BF16),
            pltpu.VMEM((2, LIVE, 256), BF16),
            pltpu.VMEM((LIVE, LANES), BF16),
            pltpu.VMEM((LIVE, 256), F32),
            pltpu.VMEM((LIVE, 256), F32),
            pltpu.VMEM((2, LIVE, LANES), F32),
            pltpu.VMEM((2, 2, LIVE, 256), F32),
        ],
        out_shape=[jax.ShapeDtypeStruct((LIVE, count * LANES), BF16)] * 3,
        us=us,
        name="attn_backward",
    )


GROUPS = 4


def put(out_ref, ids, values, quarter, base):
    me, here = ids
    count = out_ref.shape[0]
    rows = values.shape[0] // count
    for portion in range(count):
        out_ref[portion ^ me, quarter ^ here, base : base + rows, :] = values[portion * rows : portion * rows + rows]


def columns(values, which):
    return values[:, which * LANES : which * LANES + LANES]


def group_of_qkv(half, group, refs):
    normed_t_ref, lefts = refs[0], refs[1:]
    runs = len(lefts) // 3
    tall = normed_t_ref.shape[0] // 2
    height = 3 * tall // GROUPS
    parts = []
    first = group * height
    while first < (group + 1) * height:
        j, start = divmod(first, tall)
        rows = min(tall - start, (group + 1) * height - first)
        normed_t = normed_t_ref[pl.ds(pl.multiple_of(half * tall + start, 16), rows), :]
        parts.append(jnp.concatenate([dot(normed_t, lefts[3 * run + j][...]) for run in range(runs)], axis=1))
        first += rows
    return jnp.concatenate(parts, axis=0) if len(parts) > 1 else parts[0]


def ff_bwd_body(layer, top, runs, parts, step, id_ref, *refs):
    extra_refs, refs = refs[: 3 * runs + (runs > 0)], refs[3 * runs + (runs > 0) :]
    if top:
        (x_ref, low_ref, g_ref, low_t_ref, gain_ref, shift_ref, up_ref, up_bias_ref, down_ref, down_bias_ref, wo_ref,
         out_ref, mid_g_ref, att_g_ref, small_ref, up_bias_g_ref, kept_ref,
         act_ref, pre_ref, g_t_ref, normed_t_ref, mid_low_ref, mid_ref) = refs
    else:
        (mid_ref, g_ref, low_t_ref, gain_ref, shift_ref, up_ref, up_bias_ref, down_ref, wo_ref,
         mid_g_ref, att_g_ref, small_ref, up_bias_g_ref, sent_ref, kept_ref,
         act_ref, pre_ref, g_t_ref, normed_t_ref, mid_low_ref) = refs
    hidden = up_ref.shape[1]
    quarters = kept_ref.shape[1]
    length = g_t_ref.shape[1]
    tiles = length // BLOCK
    share = hidden // quarters

    @pl.when(step == 0)
    def _():
        small_ref[...] = jnp.zeros_like(small_ref)
        up_bias_g_ref[...] = jnp.zeros_like(up_bias_g_ref)

    @pl.when(step < tiles)
    def _():
        if top:
            mid_ref[...] = x_ref[...]

            @pl.when(step < BLOCKS)
            def _():
                mid_ref[...] += dot(low_ref[...], wo_ref[...])

        rows = pl.ds(pl.multiple_of(step * BLOCK, BLOCK), BLOCK)
        mid = mid_ref[...]
        unit, rstd = normalize(mid)
        normed = (unit * gain_ref[layer, 1:2, :] + shift_ref[layer, 1:2, :]).astype(BF16)
        normed_t_ref[:, rows] = normed.T
        grad = g_ref[...]
        g_low = grad.astype(BF16)
        g_t_ref[:, rows] = g_low.T
        if top:
            total = mid + down_bias_ref[layer : layer + 1, :]
        back = jnp.zeros(grad.shape, F32)
        for quarter in range(quarters):
            cols = slice(quarter * share, quarter * share + share)
            pre = dot(normed, up_ref[:, cols]) + up_bias_ref[layer : layer + 1, cols]
            act, slope = gelu_terms(pre)
            act = act.astype(BF16)
            per_half = quarters // 2
            act_ref[quarter // per_half, rows, (quarter % per_half) * share : (quarter % per_half) * share + share] = act
            if top:
                total = total + dot(act, down_ref[cols, :])
            pre_low = (dot_nt(g_low, down_ref[cols, :]) * slope).astype(BF16)
            for which in range(share // LANES):
                pre_ref[which, rows, quarter * LANES : quarter * LANES + LANES] = columns(pre_low, which)
            up_bias_g_ref[:, cols] += jnp.sum(pre_low.astype(F32), axis=0, keepdims=True)
            back = back + dot_nt(pre_low, up_ref[:, cols])
        if top:
            out_ref[...] = total
        mid_g = grad + norm_pull(back, gain_ref[layer, 1:2, :], unit, rstd)
        mid_g_ref[...] = mid_g
        mid_low = mid_g.astype(BF16)
        small_ref[0:1, :] += jnp.sum(back * unit, axis=0, keepdims=True)
        small_ref[1:2, :] += jnp.sum(back, axis=0, keepdims=True)
        small_ref[2:3, :] += jnp.sum(g_low.astype(F32), axis=0, keepdims=True)

        @pl.when(step < BLOCKS)
        def _():
            mid_low_ref[rows, :] = mid_low
            att_g_ref[...] = dot_nt(mid_low, wo_ref[...])

    count = kept_ref.shape[0]
    if top:
        ids = (0, 0)
        halves = ((tiles, 0, kept_ref), (tiles + GROUPS, 1, kept_ref))
    else:
        ids = (id_ref[0] & (count - 1), id_ref[1])
        own = id_ref[0] // (parts // 2)
        halves = ((tiles, own ^ 1, sent_ref), (tiles + GROUPS, own, kept_ref))
    for first, half, end_ref in halves:
        for group in range(GROUPS):

            @pl.when(step == first + group)
            def _(half=half, group=group, end_ref=end_ref):
                wide = act_ref.shape[2] // GROUPS
                down = dot(g_t_ref[...], act_ref[half, :, group * wide : group * wide + wide])
                height = normed_t_ref.shape[0] * (share // LANES // 2) // GROUPS
                per_tile = normed_t_ref.shape[0] // height
                part = group % per_tile
                up = dot(normed_t_ref[part * height : part * height + height, :], pre_ref[half * (share // LANES // 2) + group // per_tile])
                tall = low_t_ref.shape[0] // 2 // GROUPS
                low_rows = pl.ds(pl.multiple_of(half * (low_t_ref.shape[0] // 2) + group * tall, tall), tall)
                out = dot(low_t_ref[low_rows, :], mid_low_ref[...])
                if runs:
                    extra = group_of_qkv(half, group, extra_refs)
                for quarter in range(quarters):
                    rows = slice(quarter * LANES, quarter * LANES + LANES)
                    pieces = [
                        jnp.concatenate([columns(down[rows], which) for which in range(wide // LANES)], axis=0),
                        columns(up, quarter),
                        columns(out, quarter),
                    ]
                    if runs:
                        pieces.append(columns(extra, quarter))
                    base = 0
                    for piece in pieces:
                        put(end_ref, ids, piece, quarter, base)
                        base += piece.shape[0] // count


def piece_shapes(parts, quarters, width, hidden):
    rows = hidden // parts + width * (hidden // quarters // LANES) // parts + width // parts
    return (parts // 2, quarters, rows, LANES)


def lower_body(layer, runs, parts, id_ref, *refs):
    extra = 3 * runs + 1
    step = pl.program_id(0)
    *refs, sems = refs
    late = refs[len(refs) - extra - 1 :]
    refs = refs[: len(refs) - extra - 1]
    low_t = extra + 2
    fetch(step, 0, pl.num_programs(0) - 2 * GROUPS, list(refs[:extra]) + [refs[low_t]], late, sems)
    ff_bwd_body(layer, False, runs, parts, step, id_ref, *late[:extra], *refs[extra:low_t], late[extra], *refs[low_t + 1 :])


def ff_bwd(layer, ids, parts, quarters, grad, low_t, gains, shifts, up, up_bias, down, wo, mid, qkv, after=()):
    length, width = grad.shape
    hidden = up.shape[2]
    tiles = length // BLOCK
    portions = parts // 2
    group = portions // GROUPS
    rows = pl.BlockSpec((BLOCK, width), lambda i, ids: (jnp.minimum(i, tiles - 1), 0))
    live = pl.BlockSpec((BLOCK, width), lambda i, ids: (jnp.minimum(i, BLOCKS - 1), 0))
    extra = [qkv[0]] + [part for run in qkv[1] for part in run]
    end = piece_shapes(parts, quarters, width, hidden)
    end = end[:2] + (end[2] + 3 * width // parts, LANES)

    def end_spec(first):
        return pl.BlockSpec((group,) + end[1:], lambda i, ids: (jnp.clip(i - first, 0, GROUPS - 1) ^ ((ids[0] & (portions - 1)) // group), 0, 0, 0))

    return call(
        functools.partial(lower_body, layer, len(extra) // 3, parts),
        after,
        grid=(tiles + 2 * GROUPS,),
        prefetch=[ids],
        operands=extra + [mid, grad, low_t, gains, shifts, up, up_bias, down, wo],
        in_specs=[anywhere() for _ in extra]
        + [rows, rows, anywhere(), constant(*gains.shape), constant(*shifts.shape), of_layer(layer, up), constant(*up_bias.shape)]
        + [of_layer(layer, down), of_layer(layer, wo)],
        out_specs=[rows, live, resident(8, width), resident(1, hidden), end_spec(tiles), end_spec(tiles + GROUPS)],
        scratch=ff_bwd_scratch(length, width, hidden, quarters)
        + [pltpu.VMEM(array.shape, array.dtype) for array in extra + [low_t]]
        + [pltpu.SemaphoreType.DMA((len(extra) + 1,))],
        out_shape=[
            jax.ShapeDtypeStruct((length, width), F32),
            jax.ShapeDtypeStruct((LIVE, width), F32),
            jax.ShapeDtypeStruct((8, width), F32),
            jax.ShapeDtypeStruct((1, hidden), F32),
            jax.ShapeDtypeStruct(end, F32),
            jax.ShapeDtypeStruct(end, F32),
        ],
        us=18.0,
        name="ff_backward",
    )


def ff_bwd_scratch(length, width, hidden, quarters):
    return [
        pltpu.VMEM((2, length, hidden // 2), BF16),
        pltpu.VMEM((hidden // quarters // LANES, length, quarters * LANES), BF16),
        pltpu.VMEM((width, length), BF16),
        pltpu.VMEM((width, length), BF16),
        pltpu.VMEM((LIVE, width), BF16),
    ]


def layer_body(layer, top, pairs, parts, len_ref, id_ref, *refs):
    x_ref, gain_ref, shift_ref, w_ref, fm_ref, wo_ref, up_ref, up_bias_ref, down_ref, down_bias_ref = refs[:10]
    refs = refs[10:]
    *refs, wo_late, up_late, down_late, sems = refs
    step = pl.program_id(0)
    fetch(step, 0, pairs, [ref.at[layer] for ref in (wo_ref, up_ref, down_ref)], [wo_late, up_late, down_late], sems)
    wo_ref, up_ref, down_ref = wo_late, up_late, down_late
    refs = tuple(refs)
    if top:
        (g_ref, *outs) = refs[:9]
        out_ref, mid_g_ref, att_g_ref, small_ref, up_bias_g_ref, kept_ref, low_t_ref = refs[9:15] + refs[21:22]
        attn_scratch, low_ref = refs[15:20], refs[20]
        ff_scratch = refs[22:]
    else:
        outs = refs[:8]
        low_t_ref, out_ref, mid_ref = refs[8:11]
        attn_scratch, low_ref = refs[11:16], refs[16]

    @pl.when(step < pairs)
    def _():
        attn_fwd_body(layer, step, low_ref, low_t_ref, len_ref, x_ref, gain_ref, shift_ref, w_ref, fm_ref, *outs, *attn_scratch)

    @pl.when(step >= pairs)
    def _():
        tile = step - pairs
        x_tile = x_ref.at[pl.ds(pl.multiple_of(jnp.minimum(tile, x_ref.shape[0] // BLOCK - 1) * BLOCK, BLOCK), BLOCK)]
        low_tile = low_ref.at[pl.ds(pl.multiple_of(jnp.minimum(tile, BLOCKS - 1) * BLOCK, BLOCK), BLOCK)]
        weight_refs = (gain_ref, shift_ref, up_ref, up_bias_ref, down_ref, down_bias_ref)
        if top:
            ff_bwd_body(layer, True, 0, parts, tile, id_ref, x_tile, low_tile, g_ref, low_t_ref, *weight_refs, wo_ref,
                        out_ref, mid_g_ref, att_g_ref, small_ref, up_bias_g_ref, kept_ref, *ff_scratch)
        else:
            ff_fwd_body(layer, tile, x_tile, low_tile, wo_ref, *weight_refs, out_ref, mid_ref)


def layer_forward(layer, lengths, ids, parts, quarters, x, gains, shifts, w, fm, wo, up, up_bias, down, down_bias, grad=None, after=()):
    length, width = x.shape
    hidden = up.shape[2]
    pairs = fm.shape[1] // 2
    heads = 2 * pairs
    tiles = length // BLOCK
    top = grad is not None
    pair = lambda i: jnp.minimum(i, pairs - 1)
    tile = lambda i: jnp.clip(i - pairs, 0, tiles - 1)
    per_pair = pl.BlockSpec((1, LIVE, LANES), lambda i, *_: (pair(i), 0, 0))
    per_head = pl.BlockSpec((2, LIVE, 256), lambda i, *_: (pair(i), 0, 0))
    rows = pl.BlockSpec((BLOCK, width), lambda i, *_: (tile(i), 0))
    live = pl.BlockSpec((BLOCK, width), lambda i, *_: (jnp.minimum(tile(i), BLOCKS - 1), 0))
    out_specs = [resident(width, LIVE), per_head, per_head] + [per_pair] * 5
    out_shape = [jax.ShapeDtypeStruct((width, LIVE), BF16)] + [jax.ShapeDtypeStruct((heads, LIVE, 256), BF16)] * 2
    out_shape += [jax.ShapeDtypeStruct((pairs, LIVE, LANES), dtype) for dtype in (F32, F32, BF16, F32, F32)]
    scratch = [
        pltpu.VMEM((LIVE, width), BF16),
        pltpu.VMEM((3, pairs, LIVE, LANES), F32),
        pltpu.VMEM((BLOCKS, BLOCK, BLOCK), BF16),
        pltpu.VMEM((BLOCKS - 1, REACH, BLOCK), BF16),
        pltpu.VMEM((2, BLOCK, 256), F32),
        pltpu.VMEM((LIVE, width), BF16),
    ]
    if top:
        end = piece_shapes(parts, quarters, width, hidden)
        group = end[0] // GROUPS
        out_specs += [rows, rows, live, resident(8, width), resident(1, hidden)]
        out_specs.append(pl.BlockSpec((group,) + end[1:], lambda i, *_: (jnp.clip(i - pairs - tiles, 0, 2 * GROUPS - 1), 0, 0, 0)))
        out_shape += [jax.ShapeDtypeStruct(shape, F32) for shape in ((length, width), (length, width), (LIVE, width), (8, width), (1, hidden), (parts,) + end[1:])]
        scratch += [pltpu.VMEM((width, LIVE), BF16)] + ff_bwd_scratch(length, width, hidden, quarters) + [pltpu.VMEM((BLOCK, width), F32)]
    else:
        out_specs += [resident(width, LIVE), rows, rows]
        out_shape += [jax.ShapeDtypeStruct((width, LIVE), BF16)] + [jax.ShapeDtypeStruct((length, width), F32)] * 2
    return call(
        functools.partial(layer_body, layer, top, pairs, parts),
        after,
        grid=(pairs + tiles + (2 * GROUPS if top else 0),),
        prefetch=[lengths, ids],
        operands=[x, gains, shifts, w, fm, wo, up, up_bias, down, down_bias] + ([grad] if top else []),
        in_specs=[
            constant(*x.shape),
            constant(*gains.shape),
            constant(*shifts.shape),
            of_layer(layer, w),
            pl.BlockSpec((None, 2) + fm.shape[2:], lambda i, *_: (layer, pair(i), 0, 0)),
            anywhere(),
            anywhere(),
            constant(*up_bias.shape),
            anywhere(),
            constant(*down_bias.shape),
        ]
        + ([rows] if top else []),
        out_specs=out_specs,
        scratch=scratch + [pltpu.VMEM(array.shape[1:], array.dtype) for array in (wo, up, down)] + [pltpu.SemaphoreType.DMA((3,))],
        out_shape=out_shape,
        us=20.0,
        name="layer_top" if top else "layer_forward",
    )


def input_bwd_body(layer, runs, parts, order, ends, id_ref, *refs):
    left_refs = refs[: 3 * runs]
    w_ref, normed_t_ref, x_ref, gain_ref, mid_g_ref = refs[3 * runs : 3 * runs + 5]
    small_refs = refs[3 * runs + 5 : -4]
    if ends:
        out_ref, small_ref, sent_ref, kept_ref = refs[-4:]
    else:
        out_ref, small_ref = refs[-2:]
    step = pl.program_id(0)
    tiles = pl.num_programs(0) - (2 if ends else 0)

    @pl.when(step == 0)
    def _():
        small_ref[...] = jnp.zeros_like(small_ref)

    @pl.when(step < BLOCKS)
    def _():
        rows = pl.ds(pl.multiple_of(step * BLOCK, BLOCK), BLOCK)
        back = jnp.zeros(x_ref.shape, F32)
        for run in range(runs):
            for j in range(3):
                left = left_refs[3 * run + j]
                wide = left.shape[1]
                back = back + dot_nt(left[rows, :], w_ref[j, :, run * wide : run * wide + wide])
        unit, rstd = normalize(x_ref[...])
        out_ref[...] = mid_g_ref[...] + norm_pull(back, gain_ref[layer, 0:1, :], unit, rstd)
        small_ref[0:1, :] += jnp.sum(back * unit, axis=0, keepdims=True)
        small_ref[1:2, :] += jnp.sum(back, axis=0, keepdims=True)

    @pl.when((step >= BLOCKS) & (step < tiles))
    def _():
        out_ref[...] = mid_g_ref[...]

    if not ends:
        return
    count, quarters = sent_ref.shape[:2]
    ids = (id_ref[0] & (count - 1), id_ref[1])
    for when, flip, end_ref in ((tiles, 1, sent_ref), (tiles + 1, 0, kept_ref)):
        half = (id_ref[0] // (parts // 2)) ^ flip

        @pl.when(step == when)
        def _(half=half, end_ref=end_ref):
            tall = normed_t_ref.shape[0] // 2
            normed_t = normed_t_ref[pl.ds(pl.multiple_of(half * tall, tall), tall), :]
            totals = [jnp.concatenate([dot(normed_t, left_refs[3 * run + j][...]) for run in range(runs)], axis=1) for j in range(3)]
            for quarter in range(quarters):
                put(end_ref, ids, jnp.concatenate([columns(total, quarter) for total in totals], axis=0), quarter, 0)
            base = 3 * tall // count
            if order:
                room = end_ref.shape[2] - base
                end_ref[:, :, base:, :] = jnp.zeros((count, quarters, room, LANES), F32)

                @pl.when(half == 0)
                def _():
                    for at, (array, row, first) in enumerate(order):
                        portion, offset = divmod(at, room)
                        source = small_ref if array < 0 else small_refs[array]
                        per = source.shape[1] // quarters
                        for quarter in range(quarters):
                            start = quarter * per + first
                            end_ref[portion ^ ids[0], quarter ^ ids[1], base + offset : base + offset + 1, :] = source[row : row + 1, start : start + LANES]


def input_bwd(layer, ids, parts, quarters, proj_g, w, normed_t, x, gains, mid_g, smalls=(), order=(), ends=True, after=()):
    length, width = x.shape
    tiles = length // BLOCK
    rows = pl.BlockSpec((BLOCK, width), lambda i, ids: (jnp.minimum(i, tiles - 1), 0))
    lefts = [part for run in proj_g for part in run]
    small_rows = small_rows_of(len(order), parts)
    end = (parts // 2, quarters, 3 * width // parts + small_rows, LANES)
    return call(
        functools.partial(input_bwd_body, layer, len(proj_g), parts, tuple(order), ends),
        after,
        grid=(tiles + (2 if ends else 0),),
        prefetch=[ids],
        operands=lefts + [w, normed_t, x, gains, mid_g] + list(smalls),
        in_specs=[constant(*a.shape) for a in lefts]
        + [of_layer(layer, w), constant(*normed_t.shape), rows, constant(*gains.shape), rows]
        + [constant(*a.shape) for a in smalls],
        out_specs=[rows, resident(8, width)] + [resident(*end)] * (2 if ends else 0),
        out_shape=[jax.ShapeDtypeStruct((length, width), F32), jax.ShapeDtypeStruct((8, width), F32)] + [jax.ShapeDtypeStruct(end, F32)] * (2 if ends else 0),
        us=1.0,
        name="input_backward",
    )


def small_rows_of(count, parts):
    return -(-count // (8 * parts)) * 8


def cut_of(rows):
    return rows // 16 * 8 if rows >= 16 else rows // 2


def fork_body(kept_ref, got_ref, *ends):
    portions = kept_ref.shape[0]
    cut = ends[0].shape[2]
    for slot in range(portions):
        upper, lower = ends[slot // (portions // 2)], ends[2 + slot % 2]
        upper[slot % (portions // 2)] = kept_ref[slot, :, :cut] + got_ref[slot, :, :cut]
        lower[slot // 2] = kept_ref[slot, :, cut:] + got_ref[slot, :, cut:]


def fork(kept, got, after):
    portions, quarters, rows, _ = kept.shape
    cut = cut_of(rows)
    ends = [(portions // 2, quarters, n, LANES) for n in (cut, cut, rows - cut, rows - cut)]
    by_quarter = lambda shape: pl.BlockSpec((shape[0], 1) + shape[2:], lambda i: (0, i, 0, 0))
    return call(
        fork_body,
        after,
        grid=(quarters,),
        prefetch=[],
        operands=[kept, got],
        in_specs=[by_quarter(kept.shape)] * 2,
        out_specs=[by_quarter(end) for end in ends],
        out_shape=[jax.ShapeDtypeStruct(end, F32) for end in ends],
        us=3.0,
        name="fork_terms",
    )


def add_body(count, *refs):
    outs = refs[2 * count :]
    for which in range(count):
        for side in range(2):
            outs[2 * which + side][...] = refs[2 * which][:, side] + refs[2 * which + 1][:, side]


def add_streams(streams, wheres, after):
    operands, shapes = [], []
    for pair, where in zip(streams, wheres):
        shape = pair[0].shape
        flat = (math.prod(shape[:where]), 2, math.prod(shape[where + 1 : -2])) + shape[-2:]
        operands += [part.reshape(flat) for part in pair]
        shapes.append((flat[0],) + flat[2:])
    outs = [shape for shape in shapes for _ in range(2)]
    got = call(
        functools.partial(add_body, len(streams)),
        after,
        grid=(1,),
        prefetch=[],
        operands=operands,
        in_specs=[constant(*a.shape) for a in operands],
        out_specs=[resident(*shape) for shape in outs],
        out_shape=[jax.ShapeDtypeStruct(shape, F32) for shape in outs],
        us=1.5,
        name="add_terms",
    )
    results = []
    for which in range(len(got) // 2):
        shape, where = streams[which][0].shape, wheres[which]
        lead = shape[:where] + shape[where + 1 : -2]
        results.append(tuple(part.reshape(lead + part.shape[-2:]) for part in got[2 * which : 2 * which + 2]))
    return results


def last_add_body(counts, *refs):
    upper_ref, lower_ref = refs[-2:]
    cut = upper_ref.shape[0]
    first, base = 0, 0
    for count in counts:
        total = sum(ref[...] for ref in refs[first : first + count])
        first += count
        rows = total.shape[0]
        split = min(max(cut - base, 0), rows)
        if split:
            upper_ref[base : base + split, :] = total[:split]
        if split < rows:
            lower_ref[base + split - cut : base + rows - cut, :] = total[split:]
        base += rows


def last_add(runs, after):
    operands = [term for run in runs for term in run]
    rows = sum(run[0].shape[0] for run in runs)
    cut = cut_of(rows)
    return call(
        functools.partial(last_add_body, tuple(len(run) for run in runs)),
        after,
        grid=(1,),
        prefetch=[],
        operands=operands,
        in_specs=[constant(*a.shape) for a in operands],
        out_specs=[resident(cut, LANES), resident(rows - cut, LANES)],
        out_shape=[jax.ShapeDtypeStruct((cut, LANES), F32), jax.ShapeDtypeStruct((rows - cut, LANES), F32)],
        us=1.5,
        name="last_terms",
    )


def hold_body(*refs):
    del refs


def hold(block, after):
    return call(
        hold_body,
        after,
        grid=(1,),
        prefetch=[],
        operands=[block],
        in_specs=[pl.BlockSpec(memory_space=pl.ANY)],
        out_specs=pl.BlockSpec(memory_space=pl.ANY),
        out_shape=jax.ShapeDtypeStruct(block.shape, block.dtype),
        aliases=[(0, 0)],
        us=1.0,
        name="hold",
    )


def swap(block, axis_name, bit):
    return lax.ppermute(block, axis_name, [(i, i ^ bit) for i in range(lax.axis_size(axis_name))])


def bits_of(extent):
    return [1 << i for i in range(extent.bit_length() - 1)]


class Line:
    def __init__(self):
        self.last = []

    def __call__(self, function, *args, **kwargs):
        made = function(*args, after=self.last, **kwargs)
        leaves = jax.tree.leaves(made)
        self.last = [min(leaves, key=lambda a: a.size)]
        return made

    def wait(self, *chains):
        self.last = self.last + [array for chain in chains for array in chain.pending]


def scatter(line, sent, kept, parts, quarters):
    dp_bits, batch_bits = bits_of(parts), bits_of(quarters)
    near, far = dp_bits[0], dp_bits[1:]
    got = swap(sent, "dp", near)
    yield [got]
    ends = line(fork, kept, got)
    names = [("dp", bit) for bit in far] + [("batch", bit) for bit in batch_bits[::-1]]
    streams, left = [], []
    for which, order in enumerate((far, far[::-1])):
        kept, sent = ends[2 * which : 2 * which + 2]
        left.append([name for name in names if name != ("dp", order[0])])
        kept, sent = (part.reshape((2,) * len(left[-1]) + part.shape[2:]) for part in (kept, sent))
        streams.append((kept, swap(sent, "dp", order[0])))
    yield [got for _, got in streams]
    orders = (far[1:], far[::-1][1:])
    orders = [[("dp", bit) for bit in order] + [("batch", bit) for bit in last] for order, last in zip(orders, (batch_bits, batch_bits[::-1]))]
    for steps in zip(*orders):
        wheres = [names_left.index(step) for names_left, step in zip(left, steps)]
        results = line(add_streams, streams, wheres)
        for which, step in enumerate(steps):
            left[which].remove(step)
            streams[which] = (results[which][0], swap(results[which][1], *step))
        yield [got for _, got in streams]
    return streams


def spread(halves, parts):
    dp_bits = bits_of(parts)
    near, far = dp_bits[0], dp_bits[1:]
    streams = list(halves)
    names = [[], []]
    for bits in zip(far[::-1], far):
        moved = [swap(stream, "dp", bit) for stream, bit in zip(streams, bits)]
        yield moved
        for which, bit in enumerate(bits):
            names[which].append(bit)
            names[which].sort()
            streams[which] = jnp.stack([streams[which], moved[which]], axis=names[which].index(bit))
    block = jnp.concatenate(streams, axis=-2)
    block = block.reshape(parts // 2, block.shape[-2], LANES)
    moved = swap(block, "dp", near)
    yield [moved]
    return block, moved


class Chain:
    def __init__(self, steps):
        self.steps, self.result, self.pending = steps, None, []

    def step(self):
        if self.result is None:
            try:
                self.pending = next(self.steps)
            except StopIteration as stop:
                self.result = stop.value

    def finish(self):
        while self.result is None:
            self.step()
        return self.result


def unpack_body(names, bases, pieces, inputs, filled, id_ref, *refs):
    out_refs = dict(zip(names, refs[inputs + filled :]))
    down_ref, small_ref = refs[-2:]
    me = id_ref[0] if inputs == 2 else 0
    for top in range(inputs):
        ref = refs[top]
        portions = ref.shape[0]
        for slot in range(portions):
            portion = (slot + top * portions) ^ me
            half = portions * inputs // 2
            upper, inner = portion // half, portion % half
            for name, layer, first, rows in pieces:
                values = ref[slot, first : first + rows, :]
                if name == "small":
                    small_ref[pl.ds(pl.multiple_of(portion * rows, 8), rows), :] = values
                    continue
                out_ref = out_refs[name]
                layer = layer - bases[name]
                if name == "qkv":
                    width = out_ref.shape[1] // 3
                    unit = math.gcd(rows, width // 2)
                    for k in range(0, rows, unit):
                        flat = inner * rows + k
                        start = (flat // (width // 2)) * width + upper * (width // 2) + flat % (width // 2)
                        out_ref[layer, pl.ds(pl.multiple_of(start, 8), unit), :] = values[k : k + unit]
                elif name == "up":
                    height = out_ref.shape[1]
                    flat = portion * rows
                    tile, start = flat // height, flat % height
                    out_ref[layer, pl.ds(pl.multiple_of(start, 8), rows), pl.ds(pl.multiple_of(tile * LANES, LANES), LANES)] = values
                elif name == "down":
                    down_ref[pl.ds(pl.multiple_of(portion * rows, 8), rows), :] = values
                else:
                    out_ref[layer, pl.ds(pl.multiple_of(portion * rows, 8), rows), :] = values
    if "down" in out_refs:
        for first in range(0, down_ref.shape[0], LANES):
            out_refs["down"][0, first : first + LANES, :] = down_ref[first : first + LANES, :].T
    if "gains" in out_refs:
        layers, wide = out_refs["up_bias"].shape
        row = 0
        for layer in range(layers):
            for name, count in (("gains", 2), ("shifts", 2)):
                out_refs[name][layer] = small_ref[row : row + count, :]
                row += count
            for k in range(wide // LANES):
                out_refs["up_bias"][layer : layer + 1, k * LANES : k * LANES + LANES] = small_ref[row : row + 1, :]
                row += 1
            out_refs["down_bias"][layer : layer + 1, :] = small_ref[row : row + 1, :]
            row += 1


def unpack(ids, pair, pieces, layers, width, hidden, quarters, filled=(), after=()):
    shapes = {"down": (layers, hidden, LANES), "up": (layers, width, hidden // quarters), "out": (layers, width, LANES), "qkv": (layers, 3 * width, LANES)}
    found = {name: [layer for piece, layer, _, _ in pieces if piece == name] for name in shapes}
    names = tuple(name for name in shapes if found[name])
    bases = {name: min(found[name]) for name in names}
    out_specs = [
        pl.BlockSpec((len(found[name]),) + shapes[name][1:], lambda *_, name=name: (bases[name] // len(found[name]), 0, 0)) for name in names
    ]
    out_shape = [jax.ShapeDtypeStruct(shapes[name], F32) for name in names]
    small = [rows for piece, _, _, rows in pieces if piece == "small"]
    if small:
        names += ("gains", "shifts", "up_bias", "down_bias")
        for shape in ((layers, 2, LANES), (layers, 2, LANES), (layers, hidden // quarters), (layers, LANES)):
            out_specs.append(resident(*shape))
            out_shape.append(jax.ShapeDtypeStruct(shape, F32))
    return call(
        functools.partial(unpack_body, names, bases, pieces, len(pair), len(filled)),
        after,
        grid=(1,),
        prefetch=[ids],
        operands=list(pair) + list(filled),
        in_specs=[constant(*a.shape) for a in pair] + [pl.BlockSpec(memory_space=pl.ANY)] * len(filled),
        out_specs=out_specs,
        scratch=[
            pltpu.VMEM((hidden if found["down"] else 8, LANES), F32),
            pltpu.VMEM((len(pair) * pair[0].shape[0] * small[0] if small else 8, LANES), F32),
        ],
        out_shape=out_shape,
        aliases=[(len(pair) + which, which) for which in range(len(filled))],
        us=4.0,
        name="unpack",
    )


def reverse_bits(value, extent):
    return sum(((value // bit) % 2) * (extent // (2 * bit)) for bit in bits_of(extent))


def per_device(activations_in, gains, shifts, qkv_weights, out_weights, up_weights, up_bias, down_weights, down_bias, feature_maps, lengths, cotangent):
    layers, _, width = gains.shape
    hidden = up_bias.shape[1]
    parts, quarters = lax.axis_size("dp"), lax.axis_size("batch")
    ids = jnp.stack([reverse_bits(lax.axis_index("dp"), parts), lax.axis_index("batch")]).astype(jnp.int32)
    proteins = lengths[0]
    pairs = feature_maps.shape[1] // 2
    half = pairs // 2
    line = Line()
    last = layers - 1
    weights = (gains, shifts, qkv_weights, feature_maps, out_weights, up_weights, up_bias, down_weights, down_bias)
    x_one = activations_in[0]
    normed_zero_t, *kept_zero, low_t, x_two, mid = layer_forward(0, proteins, ids, parts, quarters, x_one, *weights)
    normed_one_t, *kept_one, values, mid_g, att_g, small_two, up_bias_g, first = layer_forward(1, proteins, ids, parts, quarters, x_two, *weights, grad=cotangent[0])
    line.last = [up_bias_g]
    smalls = [[None, None, None], [None, small_two, up_bias_g]]
    saved = ((x_one, normed_zero_t, kept_zero), (x_two, normed_one_t, kept_one))

    def attn_part(layer, att_g, first, count, us):
        phi_q, phi_k, uq, uk, v, att, rden = saved[layer][2]
        return line(attn_bwd, layer, proteins, att_g, att, rden, phi_q, phi_k, uq, uk, v, feature_maps, first, count, us)

    def input_part(layer, proj_g, mid_g, **rest):
        grad, smalls[layer][0], *ends = line(
            input_bwd, layer, ids, parts, quarters, proj_g, qkv_weights, saved[layer][1], saved[layer][0], gains, mid_g, **rest
        )
        return grad, Chain(scatter(line, *ends, parts, quarters)) if ends else None

    wide = hidden // quarters // LANES
    ff_rows = (hidden // parts, width * wide // parts, width // parts)
    ff_total, qkv_rows = sum(ff_rows), 3 * width // parts
    sizes = (layers, width, hidden, quarters)

    def ff_pieces(layer, base):
        return (("down", layer, base, ff_rows[0]), ("up", layer, base + ff_rows[0], ff_rows[1]), ("out", layer, base + ff_rows[0] + ff_rows[1], ff_rows[2]))

    first = lax.psum_scatter(first.reshape(-1, LANES), "dp", scatter_dimension=0, tiled=True)
    runs = [attn_part(1, att_g, 0, pairs, 1.0)]
    grad, _ = input_part(1, runs, mid_g, ends=False)
    mid_g, att_g, smalls[0][1], smalls[0][2], sent, kept = line(
        ff_bwd, 0, ids, parts, quarters, grad, low_t, gains, shifts, up_weights, up_bias, down_weights, out_weights, mid, (normed_one_t, runs)
    )
    second = Chain(scatter(line, sent, kept, parts, quarters))
    second.step()
    runs = [attn_part(0, att_g, 0, half, 60.0)]
    second.step()
    first = lax.psum_scatter(line(hold, first), "batch", scatter_dimension=0, tiled=True)
    runs.append(attn_part(0, att_g, half, pairs - half, 1.0))
    flat = [array for layer in range(layers) for array in smalls[layer]]
    order = []
    for layer in range(layers):
        one, two, bias = (3 * layer + k for k in range(3))
        order += [(one, 0, 0), (two, 0, 0), (one, 1, 0), (two, 1, 0)] + [(bias, 0, k * LANES) for k in range(wide)] + [(two, 2, 0)]
    present = [k for k, array in enumerate(flat) if array is not None]
    order = [(present.index(array) if array in present else -1, row, first_col) for array, row, first_col in order]
    grad, third = input_part(0, runs, mid_g, smalls=[flat[k] for k in present], order=order)
    third.step()
    second.step()
    third.step()
    second.step()
    first = lax.all_gather(line(hold, first), "dp", tiled=True).reshape(parts, -1, LANES)
    third.step()
    third.step()
    second.step()
    third.step()
    down, up, out = line(unpack, ids, [first], ff_pieces(1, 0), *sizes)
    pair = Chain(spread(line(last_add, second.finish() + third.finish()), parts)).finish()
    pieces = ff_pieces(0, 0) + (("qkv", 1, ff_total, qkv_rows), ("qkv", 0, ff_total + qkv_rows, qkv_rows))
    pieces += (("small", 0, ff_total + 2 * qkv_rows, small_rows_of(len(order), parts)),)
    down, up, out, qkv, gains_g, shifts_g, up_bias_g, down_bias_g = line(unpack, ids, pair, pieces, *sizes, (down, up, out))
    return (
        values[None],
        grad[None],
        gains_g,
        shifts_g,
        qkv.reshape(layers, 3, width, LANES),
        out,
        up,
        up_bias_g,
        down,
        down_bias_g,
    )


def solution(mesh):
    rows = P(("dp", "batch"), None, None)
    return jax.shard_map(
        per_device,
        mesh=mesh,
        in_specs=(rows,) + (P(),) * 9 + (P(("dp", "batch"), None), rows),
        out_specs=(
            rows,
            rows,
            P(None, None, "batch"),
            P(None, None, "batch"),
            P(None, None, None, "batch"),
            P(None, None, "batch"),
            P(None, None, "batch"),
            P(None, "batch"),
            P(None, None, "batch"),
            P(None, "batch"),
        ),
        check_vma=False,
    )
```

```python
import functools
import math

import jax
import jax.numpy as jnp
from jax import lax
from jax.experimental import pallas as pl
from jax.experimental.pallas import tpu as pltpu
from jax.sharding import PartitionSpec as P

BLOCK = 256
BLOCKS = 3
LIVE = BLOCK * BLOCKS
REACH = 160
LANES = 128
NDOC = 6
MIB = 1 << 20
F32 = jnp.float32
BF16 = jnp.bfloat16
LOG2E = 1.4426950408889634
NT = (((1,), (1,)), ((), ()))


def dot(a, b):
    return jnp.dot(a, b, preferred_element_type=F32)


def dot_nt(a, b):
    return lax.dot_general(a, b, NT, preferred_element_type=F32)


def params_for(mib):
    return pltpu.CompilerParams(vmem_limit_bytes=mib * MIB)


def call(body, after, *, grid, in_specs, out_specs, out_shape, prefetch, operands, scratch=(), aliases=(), mib=63, us=3.0, name):
    scalars, count = len(prefetch), len(after)

    def ordered(*refs):
        body(*refs[:scalars], *refs[scalars + count :])

    return pl.pallas_call(
        ordered,
        grid_spec=pltpu.PrefetchScalarGridSpec(
            num_scalar_prefetch=scalars,
            grid=grid,
            in_specs=[pl.BlockSpec(memory_space=pl.ANY)] * count + list(in_specs),
            out_specs=out_specs,
            scratch_shapes=list(scratch),
        ),
        out_shape=out_shape,
        input_output_aliases={scalars + count + operand: output for operand, output in aliases},
        compiler_params=params_for(mib),
        cost_estimate=pl.CostEstimate(flops=int(us * 1.15e9), bytes_accessed=0, transcendentals=0),
        name=name,
    )(*prefetch, *after, *operands)


def constant(*shape):
    return pl.BlockSpec(shape, lambda *_: (0,) * len(shape), pipeline_mode=pl.Buffered(1))


def resident(*shape):
    return pl.BlockSpec(shape, lambda *_: (0,) * len(shape))


def of_layer(layer, array):
    return pl.BlockSpec((None,) + array.shape[1:], lambda *_: (layer,) + (0,) * (array.ndim - 1), pipeline_mode=pl.Buffered(1))


def anywhere():
    return pl.BlockSpec(memory_space=pl.ANY)


def fetch(step, begin, end, sources, targets, sems):
    copies = [pltpu.make_async_copy(source, target, sems.at[k]) for k, (source, target) in enumerate(zip(sources, targets))]

    @pl.when(step == begin)
    def _():
        for copy in copies:
            copy.start()

    @pl.when(step == end)
    def _():
        for copy in copies:
            copy.wait()


def normalize(values):
    centered = values - jnp.mean(values, axis=-1, keepdims=True)
    rstd = lax.rsqrt(jnp.mean(centered * centered, axis=-1, keepdims=True) + 1e-05)
    return centered * rstd, rstd


def norm_pull(grad, gain, unit, rstd):
    p = grad * gain
    return rstd * (p - jnp.mean(p, axis=-1, keepdims=True) - unit * jnp.mean(p * unit, axis=-1, keepdims=True))


def split_two(values):
    high = values.astype(BF16)
    return high, (values - high.astype(F32)).astype(BF16)


def protein_ids(len_ref, position):
    bound = jnp.int32(0)
    ids = jnp.zeros(position.shape, jnp.int32)
    for j in range(NDOC):
        bound = bound + len_ref[j]
        ids = ids + (position >= bound).astype(jnp.int32)
    return ids


def token_count(len_ref):
    total = jnp.int32(0)
    for j in range(NDOC):
        total = total + len_ref[j]
    return total


def pair_mask(len_ref, shape, first_row, first_col, causal_rows):
    rows = lax.broadcasted_iota(jnp.int32, shape, 0) + first_row
    cols = lax.broadcasted_iota(jnp.int32, shape, 1) + first_col
    same = protein_ids(len_ref, rows) == protein_ids(len_ref, cols)
    ordered = (rows >= cols) if causal_rows else (cols >= rows)
    return jnp.where(same & ordered, 1.0, 0.0).astype(BF16)


def fill_masks(len_ref, own_ref, before_ref, causal_rows):
    for b in range(BLOCKS):
        own_ref[b] = pair_mask(len_ref, (BLOCK, BLOCK), b * BLOCK, b * BLOCK, causal_rows)
    for b in range(1, BLOCKS):
        if causal_rows:
            before_ref[b - 1] = pair_mask(len_ref, (REACH, BLOCK), b * BLOCK, (b - 1) * BLOCK, True)
        else:
            before_ref[b - 1] = pair_mask(len_ref, (REACH, BLOCK), b * BLOCK - REACH, b * BLOCK, False)


def attn_fwd_body(layer, step, low_ref, low_t_ref, len_ref, x_ref, gain_ref, shift_ref, w_ref, fm_ref, normed_t_ref, phi_q_ref, phi_k_ref, uq_ref, uk_ref,
                  v_ref, att_ref, rden_ref, normed_ref, proj_ref, own_ref, before_ref, num_ref):
    columns_here = pl.ds(pl.multiple_of(step * LANES, LANES), LANES)

    @pl.when(step == 0)
    def _():
        fill_masks(len_ref, own_ref, before_ref, True)
        for b in range(BLOCKS):
            rows = pl.ds(b * BLOCK, BLOCK)
            unit, _ = normalize(x_ref[rows, :])
            normed = (unit * gain_ref[layer, 0:1, :] + shift_ref[layer, 0:1, :]).astype(BF16)
            normed_ref[rows, :] = normed
            normed_t_ref[:, rows] = normed.T
        for j in range(3):
            for half in range(2):
                got = dot(normed_ref[...], w_ref[j, :, half * 256 : half * 256 + 256])
                proj_ref[j, 2 * half] = got[:, :LANES]
                proj_ref[j, 2 * half + 1] = got[:, LANES:]

    lane = lax.broadcasted_iota(jnp.int32, (BLOCK, LANES), 1) < 64
    uq_ref[0] = proj_ref[0, step]
    uk_ref[0] = proj_ref[1, step]
    v_ref[0] = proj_ref[2, step].astype(BF16)
    first_head = lax.broadcasted_iota(jnp.int32, (LANES, 256), 0) < 64
    minus = [jnp.where(first_head, -1.0, 0.0).astype(BF16), jnp.where(first_head, 0.0, -1.0).astype(BF16)]
    stacked = []
    for head in range(2):
        high, low = split_two(fm_ref[head] * (64.0 ** (-0.25) * LOG2E))
        stacked.append(jnp.concatenate([high, low, high, low, minus[head], minus[head]], axis=0))
    for which, phi_ref in ((0, phi_q_ref), (1, phi_k_ref)):
        for b in range(BLOCKS):
            rows = pl.ds(b * BLOCK, BLOCK)
            u = proj_ref[which, step, rows, :]
            turned = pltpu.roll(u, 64, 1)
            squares = split_two(u * u * (LOG2E / 16.0) + 0.0625)
            for head in range(2):
                twice = jnp.where(lane, u, turned) if head == 0 else jnp.where(lane, turned, u)
                exponent = dot(jnp.concatenate(split_two(twice) + squares, axis=1), stacked[head])
                phi_ref[head, rows, :] = jnp.exp2(exponent).astype(BF16)
    ones = jnp.ones((BLOCK, LANES), BF16)
    for b in range(BLOCKS):
        rows = pl.ds(b * BLOCK, BLOCK)
        v_now = jnp.concatenate([v_ref[0, rows, :], ones], axis=1)
        for head in range(2):
            weights = dot_nt(phi_q_ref[head, rows, :], phi_k_ref[head, rows, :]).astype(BF16) * own_ref[b]
            num_ref[head] = dot(weights, v_now)
            if b > 0:
                earlier = pl.ds((b - 1) * BLOCK, BLOCK)
                v_before = jnp.concatenate([v_ref[0, earlier, :], ones], axis=1)
                weights = dot_nt(phi_q_ref[head, pl.ds(b * BLOCK, REACH), :], phi_k_ref[head, earlier, :])
                num_ref[head, :REACH, :] += dot(weights.astype(BF16) * before_ref[b - 1], v_before)
        rden = 1.0 / jnp.where(lane, num_ref[0, :, LANES:], num_ref[1, :, LANES:])
        attended = jnp.where(lane, num_ref[0, :, :LANES], num_ref[1, :, :LANES]) * rden
        position = lax.broadcasted_iota(jnp.int32, (BLOCK, LANES), 0) + b * BLOCK
        attended = jnp.where(position < token_count(len_ref), attended, 0.0)
        rden_ref[0, rows, :] = rden
        att_ref[0, rows, :] = attended
        low = attended.astype(BF16)
        low_ref[rows, columns_here] = low
        low_t_ref[columns_here, rows] = low.T


def gelu_terms(pre):
    lifted = 0.5 + 0.5 * lax.erf(pre * math.sqrt(0.5))
    return pre * lifted, lifted + pre * (jnp.exp2(pre * pre * (-0.5 * LOG2E)) * (1.0 / math.sqrt(2.0 * math.pi)))


def ff_fwd_body(layer, step, x_ref, low_ref, wo_ref, gain_ref, shift_ref, up_ref, up_bias_ref, down_ref, down_bias_ref, out_ref, mid_ref):
    mid_ref[...] = x_ref[...]

    @pl.when(step < BLOCKS)
    def _():
        mid_ref[...] += dot(low_ref[...], wo_ref[...])

    mid = mid_ref[...]
    unit, _ = normalize(mid)
    normed = (unit * gain_ref[layer, 1:2, :] + shift_ref[layer, 1:2, :]).astype(BF16)
    total = mid + down_bias_ref[layer : layer + 1, :]
    for first in range(0, up_ref.shape[1], 512):
        cols = slice(first, first + 512)
        pre = dot(normed, up_ref[:, cols]) + up_bias_ref[layer : layer + 1, cols]
        act = (pre * (0.5 + 0.5 * lax.erf(pre * math.sqrt(0.5)))).astype(BF16)
        total = total + dot(act, down_ref[cols, :])
    out_ref[...] = total


def attn_bwd_body(len_ref, att_g_ref, att_ref, rden_ref, phi_q_ref, phi_k_ref, uq_ref, uk_ref, v_ref, fm_ref,
                  dq_ref, dk_ref, dv_ref, own_ref, before_ref, own_t_ref, before_t_ref,
                  x_ref, y_ref, dn_ref, d_phi_q, d_phi_k, d_v, raw_ref):
    step = pl.program_id(0)

    @pl.when(step == 0)
    def _():
        fill_masks(len_ref, own_ref, before_ref, True)
        fill_masks(len_ref, own_t_ref, before_t_ref, False)

    lane = lax.broadcasted_iota(jnp.int32, (BLOCK, LANES), 1) < 64
    one = jnp.ones((BLOCK, LANES), BF16)
    for b in range(BLOCKS):
        rows = pl.ds(b * BLOCK, BLOCK)
        position = lax.broadcasted_iota(jnp.int32, (BLOCK, LANES), 0) + b * BLOCK
        dn = jnp.where(position < token_count(len_ref), att_g_ref[rows, :] * rden_ref[0, rows, :], 0.0)
        turned = pltpu.roll(-(dn * att_ref[0, rows, :]), 64, 1)
        dn_ref[rows, :] = dn.astype(BF16)
        v_low = v_ref[0, rows, :]
        for head in range(2):
            first = lane if head == 0 else jnp.logical_not(lane)
            high, low = split_two(jnp.where(first, dn, turned))
            x_ref[head, rows, :] = jnp.concatenate([high, low], axis=1)
            y = jnp.where(first, v_low.astype(F32), 1.0).astype(BF16)
            y_ref[head, rows, :] = jnp.concatenate([y, y], axis=1)
    for head in range(2):
        for b in range(BLOCKS):
            rows = pl.ds(b * BLOCK, BLOCK)
            x, y = x_ref[head, rows, :], y_ref[head, rows, :]
            phi_q, phi_k = phi_q_ref[head, rows, :], phi_k_ref[head, rows, :]
            d_kernel = dot_nt(x, y).astype(BF16) * own_ref[b]
            d_phi_q[rows, :] = dot(d_kernel, phi_k)
            d_kernel_t = dot_nt(y, x).astype(BF16) * own_t_ref[b]
            d_phi_k[rows, :] = dot(d_kernel_t, phi_q)
            kernel_t = dot_nt(phi_k, phi_q).astype(BF16) * own_t_ref[b]
            d_v[head, rows, :] = dot(kernel_t, dn_ref[rows, :])
            if b > 0:
                earlier = pl.ds((b - 1) * BLOCK, BLOCK)
                top = pl.ds(b * BLOCK, REACH)
                bottom = pl.ds(b * BLOCK - REACH, REACH)
                d_kernel = dot_nt(x_ref[head, top, :], y_ref[head, earlier, :]).astype(BF16) * before_ref[b - 1]
                d_phi_q[top, :] += dot(d_kernel, phi_k_ref[head, earlier, :])
                d_kernel_t = dot_nt(y_ref[head, bottom, :], x).astype(BF16) * before_t_ref[b - 1]
                d_phi_k[bottom, :] += dot(d_kernel_t, phi_q)
                kernel_t = dot_nt(phi_k_ref[head, bottom, :], phi_q).astype(BF16) * before_t_ref[b - 1]
                d_v[head, bottom, :] += dot(kernel_t, dn_ref[rows, :])
        high, low = split_two(fm_ref[head])
        stacked = jnp.concatenate([high, low, jnp.ones((LANES, 256), BF16)], axis=0)
        for which, d_phi, phi_ref in ((0, d_phi_q, phi_q_ref), (1, d_phi_k, phi_k_ref)):
            for b in range(BLOCKS):
                rows = pl.ds(b * BLOCK, BLOCK)
                d_projected = (d_phi[rows, :] * phi_ref[head, rows, :].astype(F32)).astype(BF16)
                raw_ref[which, head, rows, :] = dot_nt(d_projected, stacked)
    for b in range(BLOCKS):
        rows = pl.ds(b * BLOCK, BLOCK)
        for which, u_ref, out_ref in ((0, uq_ref, dq_ref), (1, uk_ref, dk_ref)):
            parts = []
            for head in range(2):
                raw = raw_ref[which, head, rows, :LANES]
                parts.append(raw + pltpu.roll(raw, 64, 1))
            along = jnp.where(lane, parts[0], parts[1])
            total = jnp.where(lane, raw_ref[which, 0, rows, LANES:], raw_ref[which, 1, rows, LANES:])
            grad = along * (64.0 ** (-0.25)) - u_ref[0, rows, :] * total * 0.125
            out_ref[rows, :] = grad.astype(BF16)
        dv_ref[rows, :] = jnp.where(lane, d_v[0, rows, :], d_v[1, rows, :]).astype(BF16)


def attn_bwd(layer, lengths, att_g, att, rden, phi_q, phi_k, uq, uk, v, fm, first, count, us, after=()):
    per_pair = pl.BlockSpec((1, LIVE, LANES), lambda p, *_: (first + p, 0, 0))
    per_head = pl.BlockSpec((2, LIVE, 256), lambda p, *_: (first + p, 0, 0))
    return call(
        attn_bwd_body,
        after,
        grid=(count,),
        prefetch=[lengths],
        operands=[att_g, att, rden, phi_q, phi_k, uq, uk, v, fm],
        in_specs=[pl.BlockSpec((LIVE, LANES), lambda p, *_: (0, first + p)), per_pair, per_pair, per_head, per_head, per_pair, per_pair, per_pair,
                  pl.BlockSpec((None, 2) + fm.shape[2:], lambda p, *_: (layer, first + p, 0, 0))],
        out_specs=[pl.BlockSpec((LIVE, LANES), lambda p, *_: (0, p))] * 3,
        scratch=[
            pltpu.VMEM((BLOCKS, BLOCK, BLOCK), BF16),
            pltpu.VMEM((BLOCKS - 1, REACH, BLOCK), BF16),
            pltpu.VMEM((BLOCKS, BLOCK, BLOCK), BF16),
            pltpu.VMEM((BLOCKS - 1, REACH, BLOCK), BF16),
            pltpu.VMEM((2, LIVE, 256), BF16),
            pltpu.VMEM((2, LIVE, 256), BF16),
            pltpu.VMEM((LIVE, LANES), BF16),
            pltpu.VMEM((LIVE, 256), F32),
            pltpu.VMEM((LIVE, 256), F32),
            pltpu.VMEM((2, LIVE, LANES), F32),
            pltpu.VMEM((2, 2, LIVE, 256), F32),
        ],
        out_shape=[jax.ShapeDtypeStruct((LIVE, count * LANES), BF16)] * 3,
        us=us,
        name="attn_backward",
    )


GROUPS = 2


def put(out_ref, ids, values, quarter, base):
    me, here = ids
    count = out_ref.shape[0]
    rows = values.shape[0] // count
    for portion in range(count):
        out_ref[portion ^ me, quarter ^ here, base : base + rows, :] = values[portion * rows : portion * rows + rows]


def columns(values, which):
    return values[:, which * LANES : which * LANES + LANES]


def group_of_qkv(half, group, refs):
    normed_t_ref, lefts = refs[0], refs[1:]
    runs = len(lefts) // 3
    tall = normed_t_ref.shape[0] // 2
    height = 3 * tall // GROUPS
    parts = []
    first = group * height
    while first < (group + 1) * height:
        j, start = divmod(first, tall)
        rows = min(tall - start, (group + 1) * height - first)
        normed_t = normed_t_ref[pl.ds(pl.multiple_of(half * tall + start, 16), rows), :]
        parts.append(jnp.concatenate([dot(normed_t, lefts[3 * run + j][...]) for run in range(runs)], axis=1))
        first += rows
    return jnp.concatenate(parts, axis=0) if len(parts) > 1 else parts[0]


def ff_bwd_body(layer, top, runs, parts, step, id_ref, *refs):
    extra_refs, refs = refs[: 3 * runs + (runs > 0)], refs[3 * runs + (runs > 0) :]
    if top:
        (x_ref, low_ref, g_ref, low_t_ref, gain_ref, shift_ref, up_ref, up_bias_ref, down_ref, down_bias_ref, wo_ref,
         out_ref, mid_g_ref, att_g_ref, small_ref, up_bias_g_ref, kept_ref,
         act_ref, pre_ref, g_t_ref, normed_t_ref, mid_low_ref, mid_ref) = refs
    else:
        (mid_ref, g_ref, low_t_ref, gain_ref, shift_ref, up_ref, up_bias_ref, down_ref, wo_ref,
         mid_g_ref, att_g_ref, small_ref, up_bias_g_ref, sent_ref, kept_ref,
         act_ref, pre_ref, g_t_ref, normed_t_ref, mid_low_ref) = refs
    hidden = up_ref.shape[1]
    quarters = kept_ref.shape[1]
    length = g_t_ref.shape[1]
    tiles = length // BLOCK
    share = hidden // quarters

    @pl.when(step == 0)
    def _():
        small_ref[...] = jnp.zeros_like(small_ref)
        up_bias_g_ref[...] = jnp.zeros_like(up_bias_g_ref)

    @pl.when(step < tiles)
    def _():
        if top:
            mid_ref[...] = x_ref[...]

            @pl.when(step < BLOCKS)
            def _():
                mid_ref[...] += dot(low_ref[...], wo_ref[...])

        rows = pl.ds(pl.multiple_of(step * BLOCK, BLOCK), BLOCK)
        mid = mid_ref[...]
        unit, rstd = normalize(mid)
        normed = (unit * gain_ref[layer, 1:2, :] + shift_ref[layer, 1:2, :]).astype(BF16)
        normed_t_ref[:, rows] = normed.T
        grad = g_ref[...]
        g_low = grad.astype(BF16)
        g_t_ref[:, rows] = g_low.T
        if top:
            total = mid + down_bias_ref[layer : layer + 1, :]
        back = jnp.zeros(grad.shape, F32)
        for quarter in range(quarters):
            cols = slice(quarter * share, quarter * share + share)
            pre = dot(normed, up_ref[:, cols]) + up_bias_ref[layer : layer + 1, cols]
            act, slope = gelu_terms(pre)
            act = act.astype(BF16)
            per_half = quarters // 2
            act_ref[quarter // per_half, rows, (quarter % per_half) * share : (quarter % per_half) * share + share] = act
            if top:
                total = total + dot(act, down_ref[cols, :])
            pre_low = (dot_nt(g_low, down_ref[cols, :]) * slope).astype(BF16)
            for which in range(share // LANES):
                pre_ref[which, rows, quarter * LANES : quarter * LANES + LANES] = columns(pre_low, which)
            up_bias_g_ref[:, cols] += jnp.sum(pre_low.astype(F32), axis=0, keepdims=True)
            back = back + dot_nt(pre_low, up_ref[:, cols])
        if top:
            out_ref[...] = total
        mid_g = grad + norm_pull(back, gain_ref[layer, 1:2, :], unit, rstd)
        mid_g_ref[...] = mid_g
        mid_low = mid_g.astype(BF16)
        small_ref[0:1, :] += jnp.sum(back * unit, axis=0, keepdims=True)
        small_ref[1:2, :] += jnp.sum(back, axis=0, keepdims=True)
        small_ref[2:3, :] += jnp.sum(g_low.astype(F32), axis=0, keepdims=True)

        @pl.when(step < BLOCKS)
        def _():
            mid_low_ref[rows, :] = mid_low
            att_g_ref[...] = dot_nt(mid_low, wo_ref[...])

    count = kept_ref.shape[0]
    if top:
        ids = (0, 0)
        halves = ((tiles, 0, kept_ref), (tiles + GROUPS, 1, kept_ref))
    else:
        ids = (id_ref[0] & (count - 1), id_ref[1])
        own = id_ref[0] // (parts // 2)
        halves = ((tiles, own ^ 1, sent_ref), (tiles + GROUPS, own, kept_ref))
    for first, half, end_ref in halves:
        for group in range(GROUPS):

            @pl.when(step == first + group)
            def _(half=half, group=group, end_ref=end_ref):
                wide = act_ref.shape[2] // GROUPS
                down = dot(g_t_ref[...], act_ref[half, :, group * wide : group * wide + wide])
                height = normed_t_ref.shape[0] * (share // LANES // 2) // GROUPS
                per_tile = normed_t_ref.shape[0] // height
                part = group % per_tile
                up = dot(normed_t_ref[part * height : part * height + height, :], pre_ref[half * (share // LANES // 2) + group // per_tile])
                tall = low_t_ref.shape[0] // 2 // GROUPS
                low_rows = pl.ds(pl.multiple_of(half * (low_t_ref.shape[0] // 2) + group * tall, tall), tall)
                out = dot(low_t_ref[low_rows, :], mid_low_ref[...])
                if runs:
                    extra = group_of_qkv(half, group, extra_refs)
                for quarter in range(quarters):
                    rows = slice(quarter * LANES, quarter * LANES + LANES)
                    pieces = [
                        jnp.concatenate([columns(down[rows], which) for which in range(wide // LANES)], axis=0),
                        columns(up, quarter),
                        columns(out, quarter),
                    ]
                    if runs:
                        pieces.append(columns(extra, quarter))
                    base = 0
                    for piece in pieces:
                        put(end_ref, ids, piece, quarter, base)
                        base += piece.shape[0] // count


def piece_shapes(parts, quarters, width, hidden):
    rows = hidden // parts + width * (hidden // quarters // LANES) // parts + width // parts
    return (parts // 2, quarters, rows, LANES)


def lower_body(layer, runs, parts, id_ref, *refs):
    extra = 3 * runs + 1
    step = pl.program_id(0)
    *refs, sems = refs
    late = refs[len(refs) - extra - 1 :]
    refs = refs[: len(refs) - extra - 1]
    low_t = extra + 2
    fetch(step, 0, pl.num_programs(0) - 2 * GROUPS, list(refs[:extra]) + [refs[low_t]], late, sems)
    ff_bwd_body(layer, False, runs, parts, step, id_ref, *late[:extra], *refs[extra:low_t], late[extra], *refs[low_t + 1 :])


def ff_bwd(layer, ids, parts, quarters, grad, low_t, gains, shifts, up, up_bias, down, wo, mid, qkv, after=()):
    length, width = grad.shape
    hidden = up.shape[2]
    tiles = length // BLOCK
    portions = parts // 2
    group = portions // GROUPS
    rows = pl.BlockSpec((BLOCK, width), lambda i, ids: (jnp.minimum(i, tiles - 1), 0))
    live = pl.BlockSpec((BLOCK, width), lambda i, ids: (jnp.minimum(i, BLOCKS - 1), 0))
    extra = [qkv[0]] + [part for run in qkv[1] for part in run]
    end = piece_shapes(parts, quarters, width, hidden)
    end = end[:2] + (end[2] + 3 * width // parts, LANES)

    def end_spec(first):
        return pl.BlockSpec((group,) + end[1:], lambda i, ids: (jnp.clip(i - first, 0, GROUPS - 1) ^ ((ids[0] & (portions - 1)) // group), 0, 0, 0))

    return call(
        functools.partial(lower_body, layer, len(extra) // 3, parts),
        after,
        grid=(tiles + 2 * GROUPS,),
        prefetch=[ids],
        operands=extra + [mid, grad, low_t, gains, shifts, up, up_bias, down, wo],
        in_specs=[anywhere() for _ in extra]
        + [rows, rows, anywhere(), constant(*gains.shape), constant(*shifts.shape), of_layer(layer, up), constant(*up_bias.shape)]
        + [of_layer(layer, down), of_layer(layer, wo)],
        out_specs=[rows, live, resident(8, width), resident(1, hidden), end_spec(tiles), end_spec(tiles + GROUPS)],
        scratch=ff_bwd_scratch(length, width, hidden, quarters)
        + [pltpu.VMEM(array.shape, array.dtype) for array in extra + [low_t]]
        + [pltpu.SemaphoreType.DMA((len(extra) + 1,))],
        out_shape=[
            jax.ShapeDtypeStruct((length, width), F32),
            jax.ShapeDtypeStruct((LIVE, width), F32),
            jax.ShapeDtypeStruct((8, width), F32),
            jax.ShapeDtypeStruct((1, hidden), F32),
            jax.ShapeDtypeStruct(end, F32),
            jax.ShapeDtypeStruct(end, F32),
        ],
        us=18.0,
        name="ff_backward",
    )


def ff_bwd_scratch(length, width, hidden, quarters):
    return [
        pltpu.VMEM((2, length, hidden // 2), BF16),
        pltpu.VMEM((hidden // quarters // LANES, length, quarters * LANES), BF16),
        pltpu.VMEM((width, length), BF16),
        pltpu.VMEM((width, length), BF16),
        pltpu.VMEM((LIVE, width), BF16),
    ]


def layer_body(layer, top, pairs, parts, len_ref, id_ref, *refs):
    x_ref, gain_ref, shift_ref, w_ref, fm_ref, wo_ref, up_ref, up_bias_ref, down_ref, down_bias_ref = refs[:10]
    refs = refs[10:]
    *refs, wo_late, up_late, down_late, sems = refs
    step = pl.program_id(0)
    fetch(step, 0, pairs, [ref.at[layer] for ref in (wo_ref, up_ref, down_ref)], [wo_late, up_late, down_late], sems)
    wo_ref, up_ref, down_ref = wo_late, up_late, down_late
    refs = tuple(refs)
    if top:
        (g_ref, *outs) = refs[:9]
        out_ref, mid_g_ref, att_g_ref, small_ref, up_bias_g_ref, kept_ref, low_t_ref = refs[9:15] + refs[21:22]
        attn_scratch, low_ref = refs[15:20], refs[20]
        ff_scratch = refs[22:]
    else:
        outs = refs[:8]
        low_t_ref, out_ref, mid_ref = refs[8:11]
        attn_scratch, low_ref = refs[11:16], refs[16]

    @pl.when(step < pairs)
    def _():
        attn_fwd_body(layer, step, low_ref, low_t_ref, len_ref, x_ref, gain_ref, shift_ref, w_ref, fm_ref, *outs, *attn_scratch)

    @pl.when(step >= pairs)
    def _():
        tile = step - pairs
        x_tile = x_ref.at[pl.ds(pl.multiple_of(jnp.minimum(tile, x_ref.shape[0] // BLOCK - 1) * BLOCK, BLOCK), BLOCK)]
        low_tile = low_ref.at[pl.ds(pl.multiple_of(jnp.minimum(tile, BLOCKS - 1) * BLOCK, BLOCK), BLOCK)]
        weight_refs = (gain_ref, shift_ref, up_ref, up_bias_ref, down_ref, down_bias_ref)
        if top:
            ff_bwd_body(layer, True, 0, parts, tile, id_ref, x_tile, low_tile, g_ref, low_t_ref, *weight_refs, wo_ref,
                        out_ref, mid_g_ref, att_g_ref, small_ref, up_bias_g_ref, kept_ref, *ff_scratch)
        else:
            ff_fwd_body(layer, tile, x_tile, low_tile, wo_ref, *weight_refs, out_ref, mid_ref)


def layer_forward(layer, lengths, ids, parts, quarters, x, gains, shifts, w, fm, wo, up, up_bias, down, down_bias, grad=None, after=()):
    length, width = x.shape
    hidden = up.shape[2]
    pairs = fm.shape[1] // 2
    heads = 2 * pairs
    tiles = length // BLOCK
    top = grad is not None
    pair = lambda i: jnp.minimum(i, pairs - 1)
    tile = lambda i: jnp.clip(i - pairs, 0, tiles - 1)
    per_pair = pl.BlockSpec((1, LIVE, LANES), lambda i, *_: (pair(i), 0, 0))
    per_head = pl.BlockSpec((2, LIVE, 256), lambda i, *_: (pair(i), 0, 0))
    rows = pl.BlockSpec((BLOCK, width), lambda i, *_: (tile(i), 0))
    live = pl.BlockSpec((BLOCK, width), lambda i, *_: (jnp.minimum(tile(i), BLOCKS - 1), 0))
    out_specs = [resident(width, LIVE), per_head, per_head] + [per_pair] * 5
    out_shape = [jax.ShapeDtypeStruct((width, LIVE), BF16)] + [jax.ShapeDtypeStruct((heads, LIVE, 256), BF16)] * 2
    out_shape += [jax.ShapeDtypeStruct((pairs, LIVE, LANES), dtype) for dtype in (F32, F32, BF16, F32, F32)]
    scratch = [
        pltpu.VMEM((LIVE, width), BF16),
        pltpu.VMEM((3, pairs, LIVE, LANES), F32),
        pltpu.VMEM((BLOCKS, BLOCK, BLOCK), BF16),
        pltpu.VMEM((BLOCKS - 1, REACH, BLOCK), BF16),
        pltpu.VMEM((2, BLOCK, 256), F32),
        pltpu.VMEM((LIVE, width), BF16),
    ]
    if top:
        end = piece_shapes(parts, quarters, width, hidden)
        group = end[0] // GROUPS
        out_specs += [rows, rows, live, resident(8, width), resident(1, hidden)]
        out_specs.append(pl.BlockSpec((group,) + end[1:], lambda i, *_: (jnp.clip(i - pairs - tiles, 0, 2 * GROUPS - 1), 0, 0, 0)))
        out_shape += [jax.ShapeDtypeStruct(shape, F32) for shape in ((length, width), (length, width), (LIVE, width), (8, width), (1, hidden), (parts,) + end[1:])]
        scratch += [pltpu.VMEM((width, LIVE), BF16)] + ff_bwd_scratch(length, width, hidden, quarters) + [pltpu.VMEM((BLOCK, width), F32)]
    else:
        out_specs += [resident(width, LIVE), rows, rows]
        out_shape += [jax.ShapeDtypeStruct((width, LIVE), BF16)] + [jax.ShapeDtypeStruct((length, width), F32)] * 2
    return call(
        functools.partial(layer_body, layer, top, pairs, parts),
        after,
        grid=(pairs + tiles + (2 * GROUPS if top else 0),),
        prefetch=[lengths, ids],
        operands=[x, gains, shifts, w, fm, wo, up, up_bias, down, down_bias] + ([grad] if top else []),
        in_specs=[
            constant(*x.shape),
            constant(*gains.shape),
            constant(*shifts.shape),
            of_layer(layer, w),
            pl.BlockSpec((None, 2) + fm.shape[2:], lambda i, *_: (layer, pair(i), 0, 0)),
            anywhere(),
            anywhere(),
            constant(*up_bias.shape),
            anywhere(),
            constant(*down_bias.shape),
        ]
        + ([rows] if top else []),
        out_specs=out_specs,
        scratch=scratch + [pltpu.VMEM(array.shape[1:], array.dtype) for array in (wo, up, down)] + [pltpu.SemaphoreType.DMA((3,))],
        out_shape=out_shape,
        us=20.0,
        name="layer_top" if top else "layer_forward",
    )


def input_bwd_body(layer, runs, parts, order, ends, id_ref, *refs):
    left_refs = refs[: 3 * runs]
    w_ref, normed_t_ref, x_ref, gain_ref, mid_g_ref = refs[3 * runs : 3 * runs + 5]
    small_refs = refs[3 * runs + 5 : -4]
    if ends:
        out_ref, small_ref, sent_ref, kept_ref = refs[-4:]
    else:
        out_ref, small_ref = refs[-2:]
    step = pl.program_id(0)
    tiles = pl.num_programs(0) - (2 if ends else 0)

    @pl.when(step == 0)
    def _():
        small_ref[...] = jnp.zeros_like(small_ref)

    @pl.when(step < BLOCKS)
    def _():
        rows = pl.ds(pl.multiple_of(step * BLOCK, BLOCK), BLOCK)
        back = jnp.zeros(x_ref.shape, F32)
        for run in range(runs):
            for j in range(3):
                left = left_refs[3 * run + j]
                wide = left.shape[1]
                back = back + dot_nt(left[rows, :], w_ref[j, :, run * wide : run * wide + wide])
        unit, rstd = normalize(x_ref[...])
        out_ref[...] = mid_g_ref[...] + norm_pull(back, gain_ref[layer, 0:1, :], unit, rstd)
        small_ref[0:1, :] += jnp.sum(back * unit, axis=0, keepdims=True)
        small_ref[1:2, :] += jnp.sum(back, axis=0, keepdims=True)

    @pl.when((step >= BLOCKS) & (step < tiles))
    def _():
        out_ref[...] = mid_g_ref[...]

    if not ends:
        return
    count, quarters = sent_ref.shape[:2]
    ids = (id_ref[0] & (count - 1), id_ref[1])
    for when, flip, end_ref in ((tiles, 1, sent_ref), (tiles + 1, 0, kept_ref)):
        half = (id_ref[0] // (parts // 2)) ^ flip

        @pl.when(step == when)
        def _(half=half, end_ref=end_ref):
            tall = normed_t_ref.shape[0] // 2
            normed_t = normed_t_ref[pl.ds(pl.multiple_of(half * tall, tall), tall), :]
            totals = [jnp.concatenate([dot(normed_t, left_refs[3 * run + j][...]) for run in range(runs)], axis=1) for j in range(3)]
            for quarter in range(quarters):
                put(end_ref, ids, jnp.concatenate([columns(total, quarter) for total in totals], axis=0), quarter, 0)
            base = 3 * tall // count
            if order:
                room = end_ref.shape[2] - base
                end_ref[:, :, base:, :] = jnp.zeros((count, quarters, room, LANES), F32)

                @pl.when(half == 0)
                def _():
                    for at, (array, row, first) in enumerate(order):
                        portion, offset = divmod(at, room)
                        source = small_ref if array < 0 else small_refs[array]
                        per = source.shape[1] // quarters
                        for quarter in range(quarters):
                            start = quarter * per + first
                            end_ref[portion ^ ids[0], quarter ^ ids[1], base + offset : base + offset + 1, :] = source[row : row + 1, start : start + LANES]


def input_bwd(layer, ids, parts, quarters, proj_g, w, normed_t, x, gains, mid_g, smalls=(), order=(), ends=True, after=()):
    length, width = x.shape
    tiles = length // BLOCK
    rows = pl.BlockSpec((BLOCK, width), lambda i, ids: (jnp.minimum(i, tiles - 1), 0))
    lefts = [part for run in proj_g for part in run]
    small_rows = small_rows_of(len(order), parts, 3 * width // parts)
    end = (parts // 2, quarters, 3 * width // parts + small_rows, LANES)
    return call(
        functools.partial(input_bwd_body, layer, len(proj_g), parts, tuple(order), ends),
        after,
        grid=(tiles + (2 if ends else 0),),
        prefetch=[ids],
        operands=lefts + [w, normed_t, x, gains, mid_g] + list(smalls),
        in_specs=[constant(*a.shape) for a in lefts]
        + [of_layer(layer, w), constant(*normed_t.shape), rows, constant(*gains.shape), rows]
        + [constant(*a.shape) for a in smalls],
        out_specs=[rows, resident(8, width)] + [resident(*end)] * (2 if ends else 0),
        out_shape=[jax.ShapeDtypeStruct((length, width), F32), jax.ShapeDtypeStruct((8, width), F32)] + [jax.ShapeDtypeStruct(end, F32)] * (2 if ends else 0),
        us=1.0,
        name="input_backward",
    )


def small_rows_of(count, parts, others):
    least = -(-count // (8 * parts)) * 8
    return least + (others + least) % 16


class Share:
    def __init__(self, terms, names, rows):
        self.terms, self.names, self.rows, self.done = terms, names, rows, ()

    def operands(self, step, over):
        specs = []
        for _, names, which in self.terms:
            at = [0 if name in self.done else 1 if name == step else None for name in names]
            block = [2 if index is None and name not in over else None for name, index in zip(names, at)]

            def index_map(*grid, names=names, at=at, which=which):
                free = [grid[over.index(name)] if name in over else 0 for name in names]
                return tuple(one if index is None else index for one, index in zip(free, at)) + (which, 0)

            specs.append(pl.BlockSpec(tuple(block) + (self.rows, LANES), index_map))
        return [array for array, _, _ in self.terms], specs

    def left(self, step):
        return [name for name in self.names if name not in self.done and name != step]

    def take(self, step, array):
        self.terms.append((array, tuple(self.left(step)), 0))
        self.done += (step,)


def sums_body(counts, *refs):
    outs = refs[len(refs) - len(counts) :]
    first = 0
    for count, out in zip(counts, outs):
        out[...] = sum(ref[...] for ref in refs[first : first + count])
        first += count


def sums_to_send(shares, steps, over, after):
    operands, in_specs, out_specs, out_shape = [], [], [], []
    for part, step in zip(shares, steps):
        arrays, specs = part.operands(step, over)
        operands += arrays
        in_specs += specs
        left = part.left(step)
        out_shape.append(jax.ShapeDtypeStruct((2,) * len(left) + (part.rows, LANES), F32))
        block = tuple(None if name in over else 2 for name in left) + (part.rows, LANES)
        out_specs.append(pl.BlockSpec(block, lambda *grid, left=left: tuple(grid[over.index(n)] if n in over else 0 for n in left) + (0, 0)))
    return call(
        functools.partial(sums_body, tuple(len(part.terms) for part in shares)),
        after,
        grid=(2,) * len(over) if over else (1,),
        prefetch=[],
        operands=operands,
        in_specs=in_specs,
        out_specs=out_specs,
        out_shape=out_shape,
        us=2.0,
        name="sums_to_send",
    )


def last_add_body(counts, *refs):
    upper_ref, lower_ref = refs[-2:]
    cut = upper_ref.shape[0]
    first, base = 0, 0
    for count in counts:
        total = sum(ref[...] for ref in refs[first : first + count])
        first += count
        rows = total.shape[0]
        split = min(max(cut - base, 0), rows)
        if split:
            upper_ref[base : base + split, :] = total[:split]
        if split < rows:
            lower_ref[base + split - cut : base + rows - cut, :] = total[split:]
        base += rows


def last_add(shares, after):
    rows = sum(part.rows for part in shares)
    cut = rows // 2
    operands, in_specs = [], []
    for part in shares:
        arrays, specs = part.operands(None, ())
        operands += arrays
        in_specs += specs
    return call(
        functools.partial(last_add_body, tuple(len(part.terms) for part in shares)),
        after,
        grid=(1,),
        prefetch=[],
        operands=operands,
        in_specs=in_specs,
        out_specs=[resident(cut, LANES), resident(rows - cut, LANES)],
        out_shape=[jax.ShapeDtypeStruct((cut, LANES), F32), jax.ShapeDtypeStruct((rows - cut, LANES), F32)],
        us=1.5,
        name="last_terms",
    )


def hold_body(*refs):
    del refs


def hold(block, after):
    return call(
        hold_body,
        after,
        grid=(1,),
        prefetch=[],
        operands=[block],
        in_specs=[pl.BlockSpec(memory_space=pl.ANY)],
        out_specs=pl.BlockSpec(memory_space=pl.ANY),
        out_shape=jax.ShapeDtypeStruct(block.shape, block.dtype),
        aliases=[(0, 0)],
        us=1.0,
        name="hold",
    )


def swap(block, axis_name, bit):
    return lax.ppermute(block, axis_name, [(i, i ^ bit) for i in range(lax.axis_size(axis_name))])


def bits_of(extent):
    return [1 << i for i in range(extent.bit_length() - 1)]


class Line:
    def __init__(self):
        self.last = []

    def __call__(self, function, *args, **kwargs):
        made = function(*args, after=self.last, **kwargs)
        leaves = jax.tree.leaves(made)
        self.last = [min(leaves, key=lambda a: a.size)]
        return made

    def wait(self, *chains):
        self.last = self.last + [array for chain in chains for array in chain.pending]


def scatter(line, sent, kept, parts, quarters):
    dp_bits, batch_bits = bits_of(parts), bits_of(quarters)
    near, far = dp_bits[0], dp_bits[1:]
    got = swap(sent, "dp", near)
    yield [got]
    batch_names = [("batch", bit) for bit in batch_bits[::-1]]
    names = tuple([("dp", bit) for bit in far] + batch_names)
    rows = kept.shape[2] // 2
    whole = [part.reshape((2,) * len(names) + part.shape[2:]) for part in (kept, got)]
    shares = [Share([(part, names, which) for part in whole], names, rows) for which in range(2)]
    orders = [[("dp", bit) for bit in order] + [("batch", bit) for bit in last] for order, last in ((far, batch_bits), (far[::-1], batch_bits[::-1]))]
    for count, steps in enumerate(zip(*orders)):
        large = rows * 2 ** (len(names) - count) > 2**12
        sums = line(sums_to_send, shares, steps, tuple(batch_names) if large and steps[0][0] == "dp" else ())
        moved = [swap(block, *step) for block, step in zip(sums, steps)]
        for part, step, block in zip(shares, steps, moved):
            part.take(step, block)
        yield moved
    return shares


def spread(halves, parts):
    dp_bits = bits_of(parts)
    near, far = dp_bits[0], dp_bits[1:]
    streams = list(halves)
    names = [[], []]
    for bits in zip(far[::-1], far):
        moved = [swap(stream, "dp", bit) for stream, bit in zip(streams, bits)]
        yield moved
        for which, bit in enumerate(bits):
            names[which].append(bit)
            names[which].sort()
            streams[which] = jnp.stack([streams[which], moved[which]], axis=names[which].index(bit))
    block = jnp.concatenate(streams, axis=-2)
    block = block.reshape(parts // 2, block.shape[-2], LANES)
    moved = swap(block, "dp", near)
    yield [moved]
    return block, moved


class Chain:
    def __init__(self, steps):
        self.steps, self.result, self.pending = steps, None, []

    def step(self):
        if self.result is None:
            try:
                self.pending = next(self.steps)
            except StopIteration as stop:
                self.result = stop.value

    def finish(self):
        while self.result is None:
            self.step()
        return self.result


def unpack_body(names, bases, pieces, inputs, filled, id_ref, *refs):
    out_refs = dict(zip(names, refs[inputs + filled :]))
    down_ref, small_ref = refs[-2:]
    me = id_ref[0] if inputs == 2 else 0
    for top in range(inputs):
        ref = refs[top]
        portions = ref.shape[0]
        for slot in range(portions):
            portion = (slot + top * portions) ^ me
            half = portions * inputs // 2
            upper, inner = portion // half, portion % half
            for name, layer, first, rows in pieces:
                values = ref[slot, first : first + rows, :]
                if name == "small":
                    small_ref[pl.ds(pl.multiple_of(portion * rows, 8), rows), :] = values
                    continue
                out_ref = out_refs[name]
                layer = layer - bases[name]
                if name == "qkv":
                    width = out_ref.shape[1] // 3
                    unit = math.gcd(rows, width // 2)
                    for k in range(0, rows, unit):
                        flat = inner * rows + k
                        start = (flat // (width // 2)) * width + upper * (width // 2) + flat % (width // 2)
                        out_ref[layer, pl.ds(pl.multiple_of(start, 8), unit), :] = values[k : k + unit]
                elif name == "up":
                    height = out_ref.shape[1]
                    flat = portion * rows
                    tile, start = flat // height, flat % height
                    out_ref[layer, pl.ds(pl.multiple_of(start, 8), rows), pl.ds(pl.multiple_of(tile * LANES, LANES), LANES)] = values
                elif name == "down":
                    down_ref[pl.ds(pl.multiple_of(portion * rows, 8), rows), :] = values
                else:
                    out_ref[layer, pl.ds(pl.multiple_of(portion * rows, 8), rows), :] = values
    if "down" in out_refs:
        for first in range(0, down_ref.shape[0], LANES):
            out_refs["down"][0, first : first + LANES, :] = down_ref[first : first + LANES, :].T
    if "gains" in out_refs:
        layers, wide = out_refs["up_bias"].shape
        row = 0
        for layer in range(layers):
            for name, count in (("gains", 2), ("shifts", 2)):
                out_refs[name][layer] = small_ref[row : row + count, :]
                row += count
            for k in range(wide // LANES):
                out_refs["up_bias"][layer : layer + 1, k * LANES : k * LANES + LANES] = small_ref[row : row + 1, :]
                row += 1
            out_refs["down_bias"][layer : layer + 1, :] = small_ref[row : row + 1, :]
            row += 1


def unpack(ids, pair, pieces, layers, width, hidden, quarters, filled=(), after=()):
    shapes = {"down": (layers, hidden, LANES), "up": (layers, width, hidden // quarters), "out": (layers, width, LANES), "qkv": (layers, 3 * width, LANES)}
    found = {name: [layer for piece, layer, _, _ in pieces if piece == name] for name in shapes}
    names = tuple(name for name in shapes if found[name])
    bases = {name: min(found[name]) for name in names}
    out_specs = [
        pl.BlockSpec((len(found[name]),) + shapes[name][1:], lambda *_, name=name: (bases[name] // len(found[name]), 0, 0)) for name in names
    ]
    out_shape = [jax.ShapeDtypeStruct(shapes[name], F32) for name in names]
    small = [rows for piece, _, _, rows in pieces if piece == "small"]
    if small:
        names += ("gains", "shifts", "up_bias", "down_bias")
        for shape in ((layers, 2, LANES), (layers, 2, LANES), (layers, hidden // quarters), (layers, LANES)):
            out_specs.append(resident(*shape))
            out_shape.append(jax.ShapeDtypeStruct(shape, F32))
    return call(
        functools.partial(unpack_body, names, bases, pieces, len(pair), len(filled)),
        after,
        grid=(1,),
        prefetch=[ids],
        operands=list(pair) + list(filled),
        in_specs=[constant(*a.shape) for a in pair] + [pl.BlockSpec(memory_space=pl.ANY)] * len(filled),
        out_specs=out_specs,
        scratch=[
            pltpu.VMEM((hidden if found["down"] else 8, LANES), F32),
            pltpu.VMEM((len(pair) * pair[0].shape[0] * small[0] if small else 8, LANES), F32),
        ],
        out_shape=out_shape,
        aliases=[(len(pair) + which, which) for which in range(len(filled))],
        mib=32,
        us=4.0,
        name="unpack",
    )


def reverse_bits(value, extent):
    return sum(((value // bit) % 2) * (extent // (2 * bit)) for bit in bits_of(extent))


def per_device(activations_in, gains, shifts, qkv_weights, out_weights, up_weights, up_bias, down_weights, down_bias, feature_maps, lengths, cotangent):
    layers, _, width = gains.shape
    hidden = up_bias.shape[1]
    parts, quarters = lax.axis_size("dp"), lax.axis_size("batch")
    ids = jnp.stack([reverse_bits(lax.axis_index("dp"), parts), lax.axis_index("batch")]).astype(jnp.int32)
    proteins = lengths[0]
    pairs = feature_maps.shape[1] // 2
    half = pairs // 2
    line = Line()
    last = layers - 1
    weights = (gains, shifts, qkv_weights, feature_maps, out_weights, up_weights, up_bias, down_weights, down_bias)
    x_one = activations_in[0]
    normed_zero_t, *kept_zero, low_t, x_two, mid = layer_forward(0, proteins, ids, parts, quarters, x_one, *weights)
    normed_one_t, *kept_one, values, mid_g, att_g, small_two, up_bias_g, first = layer_forward(1, proteins, ids, parts, quarters, x_two, *weights, grad=cotangent[0])
    line.last = [up_bias_g]
    smalls = [[None, None, None], [None, small_two, up_bias_g]]
    saved = ((x_one, normed_zero_t, kept_zero), (x_two, normed_one_t, kept_one))

    def attn_part(layer, att_g, first, count, us):
        phi_q, phi_k, uq, uk, v, att, rden = saved[layer][2]
        return line(attn_bwd, layer, proteins, att_g, att, rden, phi_q, phi_k, uq, uk, v, feature_maps, first, count, us)

    def input_part(layer, proj_g, mid_g, **rest):
        grad, smalls[layer][0], *ends = line(
            input_bwd, layer, ids, parts, quarters, proj_g, qkv_weights, saved[layer][1], saved[layer][0], gains, mid_g, **rest
        )
        return grad, Chain(scatter(line, *ends, parts, quarters)) if ends else None

    wide = hidden // quarters // LANES
    ff_rows = (hidden // parts, width * wide // parts, width // parts)
    ff_total, qkv_rows = sum(ff_rows), 3 * width // parts
    sizes = (layers, width, hidden, quarters)

    def ff_pieces(layer, base):
        return (("down", layer, base, ff_rows[0]), ("up", layer, base + ff_rows[0], ff_rows[1]), ("out", layer, base + ff_rows[0] + ff_rows[1], ff_rows[2]))

    first = lax.psum_scatter(first.reshape(-1, LANES), "dp", scatter_dimension=0, tiled=True)
    runs = [attn_part(1, att_g, 0, pairs, 1.0)]
    grad, _ = input_part(1, runs, mid_g, ends=False)
    mid_g, att_g, smalls[0][1], smalls[0][2], sent, kept = line(
        ff_bwd, 0, ids, parts, quarters, grad, low_t, gains, shifts, up_weights, up_bias, down_weights, out_weights, mid, (normed_one_t, runs)
    )
    second = Chain(scatter(line, sent, kept, parts, quarters))
    second.step()
    runs = [attn_part(0, att_g, 0, half, 60.0)]
    second.step()
    first = lax.psum_scatter(line(hold, first), "batch", scatter_dimension=0, tiled=True)
    runs.append(attn_part(0, att_g, half, pairs - half, 1.0))
    flat = [array for layer in range(layers) for array in smalls[layer]]
    order = []
    for layer in range(layers):
        one, two, bias = (3 * layer + k for k in range(3))
        order += [(one, 0, 0), (two, 0, 0), (one, 1, 0), (two, 1, 0)] + [(bias, 0, k * LANES) for k in range(wide)] + [(two, 2, 0)]
    present = [k for k, array in enumerate(flat) if array is not None]
    order = [(present.index(array) if array in present else -1, row, first_col) for array, row, first_col in order]
    grad, third = input_part(0, runs, mid_g, smalls=[flat[k] for k in present], order=order)
    third.step()
    second.step()
    third.step()
    second.step()
    first = lax.all_gather(line(hold, first), "dp", tiled=True).reshape(parts, -1, LANES)
    third.step()
    third.step()
    second.step()
    third.step()
    down, up, out = line(unpack, ids, [first], ff_pieces(1, 0), *sizes)
    pair = Chain(spread(line(last_add, second.finish() + third.finish()), parts)).finish()
    pieces = ff_pieces(0, 0) + (("qkv", 1, ff_total, qkv_rows), ("qkv", 0, ff_total + qkv_rows, qkv_rows))
    pieces += (("small", 0, ff_total + 2 * qkv_rows, small_rows_of(len(order), parts, qkv_rows)),)
    down, up, out, qkv, gains_g, shifts_g, up_bias_g, down_bias_g = line(unpack, ids, pair, pieces, *sizes, (down, up, out))
    return (
        values[None],
        grad[None],
        gains_g,
        shifts_g,
        qkv.reshape(layers, 3, width, LANES),
        out,
        up,
        up_bias_g,
        down,
        down_bias_g,
    )


def solution(mesh):
    rows = P(("dp", "batch"), None, None)
    return jax.shard_map(
        per_device,
        mesh=mesh,
        in_specs=(rows,) + (P(),) * 9 + (P(("dp", "batch"), None), rows),
        out_specs=(
            rows,
            rows,
            P(None, None, "batch"),
            P(None, None, "batch"),
            P(None, None, None, "batch"),
            P(None, None, "batch"),
            P(None, None, "batch"),
            P(None, "batch"),
            P(None, None, "batch"),
            P(None, "batch"),
        ),
        check_vma=False,
    )
```

```python
import functools
import math

import jax
import jax.numpy as jnp
from jax import lax
from jax.experimental import pallas as pl
from jax.experimental.pallas import tpu as pltpu
from jax.sharding import PartitionSpec as P

BLOCK = 256
BLOCKS = 3
LIVE = BLOCK * BLOCKS
REACH = 160
LANES = 128
NDOC = 6
MIB = 1 << 20
F32 = jnp.float32
BF16 = jnp.bfloat16
LOG2E = 1.4426950408889634
NT = (((1,), (1,)), ((), ()))


def dot(a, b):
    return jnp.dot(a, b, preferred_element_type=F32)


def dot_nt(a, b):
    return lax.dot_general(a, b, NT, preferred_element_type=F32)


def params_for(mib):
    return pltpu.CompilerParams(vmem_limit_bytes=mib * MIB)


def call(body, after, *, grid, in_specs, out_specs, out_shape, prefetch, operands, scratch=(), aliases=(), mib=63, us=3.0, name):
    scalars, count = len(prefetch), len(after)

    def ordered(*refs):
        body(*refs[:scalars], *refs[scalars + count :])

    return pl.pallas_call(
        ordered,
        grid_spec=pltpu.PrefetchScalarGridSpec(
            num_scalar_prefetch=scalars,
            grid=grid,
            in_specs=[pl.BlockSpec(memory_space=pl.ANY)] * count + list(in_specs),
            out_specs=out_specs,
            scratch_shapes=list(scratch),
        ),
        out_shape=out_shape,
        input_output_aliases={scalars + count + operand: output for operand, output in aliases},
        compiler_params=params_for(mib),
        cost_estimate=pl.CostEstimate(flops=int(us * 1.15e9), bytes_accessed=0, transcendentals=0),
        name=name,
    )(*prefetch, *after, *operands)


def constant(*shape):
    return pl.BlockSpec(shape, lambda *_: (0,) * len(shape), pipeline_mode=pl.Buffered(1))


def resident(*shape):
    return pl.BlockSpec(shape, lambda *_: (0,) * len(shape))


def of_layer(layer, array):
    return pl.BlockSpec((None,) + array.shape[1:], lambda *_: (layer,) + (0,) * (array.ndim - 1), pipeline_mode=pl.Buffered(1))


def anywhere():
    return pl.BlockSpec(memory_space=pl.ANY)


def fetch(step, begin, end, sources, targets, sems):
    copies = [pltpu.make_async_copy(source, target, sems.at[k]) for k, (source, target) in enumerate(zip(sources, targets))]

    @pl.when(step == begin)
    def _():
        for copy in copies:
            copy.start()

    @pl.when(step == end)
    def _():
        for copy in copies:
            copy.wait()


def normalize(values):
    centered = values - jnp.mean(values, axis=-1, keepdims=True)
    rstd = lax.rsqrt(jnp.mean(centered * centered, axis=-1, keepdims=True) + 1e-05)
    return centered * rstd, rstd


def norm_pull(grad, gain, unit, rstd):
    p = grad * gain
    return rstd * (p - jnp.mean(p, axis=-1, keepdims=True) - unit * jnp.mean(p * unit, axis=-1, keepdims=True))


def split_two(values):
    high = values.astype(BF16)
    return high, (values - high.astype(F32)).astype(BF16)


def protein_ids(len_ref, position):
    bound = jnp.int32(0)
    ids = jnp.zeros(position.shape, jnp.int32)
    for j in range(NDOC):
        bound = bound + len_ref[j]
        ids = ids + (position >= bound).astype(jnp.int32)
    return ids


def token_count(len_ref):
    total = jnp.int32(0)
    for j in range(NDOC):
        total = total + len_ref[j]
    return total


def pair_mask(len_ref, shape, first_row, first_col, causal_rows):
    rows = lax.broadcasted_iota(jnp.int32, shape, 0) + first_row
    cols = lax.broadcasted_iota(jnp.int32, shape, 1) + first_col
    same = protein_ids(len_ref, rows) == protein_ids(len_ref, cols)
    ordered = (rows >= cols) if causal_rows else (cols >= rows)
    return jnp.where(same & ordered, 1.0, 0.0).astype(BF16)


def fill_masks(len_ref, own_ref, before_ref, causal_rows):
    for b in range(BLOCKS):
        own_ref[b] = pair_mask(len_ref, (BLOCK, BLOCK), b * BLOCK, b * BLOCK, causal_rows)
    for b in range(1, BLOCKS):
        if causal_rows:
            before_ref[b - 1] = pair_mask(len_ref, (REACH, BLOCK), b * BLOCK, (b - 1) * BLOCK, True)
        else:
            before_ref[b - 1] = pair_mask(len_ref, (REACH, BLOCK), b * BLOCK - REACH, b * BLOCK, False)


def attn_fwd_body(layer, step, low_ref, low_t_ref, len_ref, x_ref, gain_ref, shift_ref, w_ref, fm_ref, normed_t_ref, phi_q_ref, phi_k_ref, uq_ref, uk_ref,
                  v_ref, att_ref, rden_ref, normed_ref, proj_ref, own_ref, before_ref, num_ref):
    columns_here = pl.ds(pl.multiple_of(step * LANES, LANES), LANES)

    @pl.when(step == 0)
    def _():
        fill_masks(len_ref, own_ref, before_ref, True)
        for b in range(BLOCKS):
            rows = pl.ds(b * BLOCK, BLOCK)
            unit, _ = normalize(x_ref[rows, :])
            normed = (unit * gain_ref[layer, 0:1, :] + shift_ref[layer, 0:1, :]).astype(BF16)
            normed_ref[rows, :] = normed
            normed_t_ref[:, rows] = normed.T
        for j in range(3):
            for half in range(2):
                got = dot(normed_ref[...], w_ref[j, :, half * 256 : half * 256 + 256])
                proj_ref[j, 2 * half] = got[:, :LANES]
                proj_ref[j, 2 * half + 1] = got[:, LANES:]

    lane = lax.broadcasted_iota(jnp.int32, (BLOCK, LANES), 1) < 64
    uq_ref[0] = proj_ref[0, step]
    uk_ref[0] = proj_ref[1, step]
    v_ref[0] = proj_ref[2, step].astype(BF16)
    first_head = lax.broadcasted_iota(jnp.int32, (LANES, 256), 0) < 64
    minus = [jnp.where(first_head, -1.0, 0.0).astype(BF16), jnp.where(first_head, 0.0, -1.0).astype(BF16)]
    stacked = []
    for head in range(2):
        high, low = split_two(fm_ref[head] * (64.0 ** (-0.25) * LOG2E))
        stacked.append(jnp.concatenate([high, low, high, low, minus[head], minus[head]], axis=0))
    for which, phi_ref in ((0, phi_q_ref), (1, phi_k_ref)):
        for b in range(BLOCKS):
            rows = pl.ds(b * BLOCK, BLOCK)
            u = proj_ref[which, step, rows, :]
            turned = pltpu.roll(u, 64, 1)
            squares = split_two(u * u * (LOG2E / 16.0) + 0.0625)
            for head in range(2):
                twice = jnp.where(lane, u, turned) if head == 0 else jnp.where(lane, turned, u)
                exponent = dot(jnp.concatenate(split_two(twice) + squares, axis=1), stacked[head])
                phi_ref[head, rows, :] = jnp.exp2(exponent).astype(BF16)
    ones = jnp.ones((BLOCK, LANES), BF16)
    for b in range(BLOCKS):
        rows = pl.ds(b * BLOCK, BLOCK)
        v_now = jnp.concatenate([v_ref[0, rows, :], ones], axis=1)
        for head in range(2):
            weights = dot_nt(phi_q_ref[head, rows, :], phi_k_ref[head, rows, :]).astype(BF16) * own_ref[b]
            num_ref[head] = dot(weights, v_now)
            if b > 0:
                earlier = pl.ds((b - 1) * BLOCK, BLOCK)
                v_before = jnp.concatenate([v_ref[0, earlier, :], ones], axis=1)
                weights = dot_nt(phi_q_ref[head, pl.ds(b * BLOCK, REACH), :], phi_k_ref[head, earlier, :])
                num_ref[head, :REACH, :] += dot(weights.astype(BF16) * before_ref[b - 1], v_before)
        rden = 1.0 / jnp.where(lane, num_ref[0, :, LANES:], num_ref[1, :, LANES:])
        attended = jnp.where(lane, num_ref[0, :, :LANES], num_ref[1, :, :LANES]) * rden
        position = lax.broadcasted_iota(jnp.int32, (BLOCK, LANES), 0) + b * BLOCK
        attended = jnp.where(position < token_count(len_ref), attended, 0.0)
        rden_ref[0, rows, :] = rden
        att_ref[0, rows, :] = attended
        low = attended.astype(BF16)
        low_ref[rows, columns_here] = low
        low_t_ref[columns_here, rows] = low.T


def gelu_terms(pre):
    lifted = 0.5 + 0.5 * lax.erf(pre * math.sqrt(0.5))
    return pre * lifted, lifted + pre * (jnp.exp2(pre * pre * (-0.5 * LOG2E)) * (1.0 / math.sqrt(2.0 * math.pi)))


def ff_fwd_body(layer, step, x_ref, low_ref, wo_ref, gain_ref, shift_ref, up_ref, up_bias_ref, down_ref, down_bias_ref, out_ref, mid_ref):
    mid_ref[...] = x_ref[...]

    @pl.when(step < BLOCKS)
    def _():
        mid_ref[...] += dot(low_ref[...], wo_ref[...])

    mid = mid_ref[...]
    unit, _ = normalize(mid)
    normed = (unit * gain_ref[layer, 1:2, :] + shift_ref[layer, 1:2, :]).astype(BF16)
    total = mid + down_bias_ref[layer : layer + 1, :]
    for first in range(0, up_ref.shape[1], 512):
        cols = slice(first, first + 512)
        pre = dot(normed, up_ref[:, cols]) + up_bias_ref[layer : layer + 1, cols]
        act = (pre * (0.5 + 0.5 * lax.erf(pre * math.sqrt(0.5)))).astype(BF16)
        total = total + dot(act, down_ref[cols, :])
    out_ref[...] = total


def attn_bwd_body(len_ref, att_g_ref, att_ref, rden_ref, phi_q_ref, phi_k_ref, uq_ref, uk_ref, v_ref, fm_ref,
                  dq_ref, dk_ref, dv_ref, own_ref, before_ref, own_t_ref, before_t_ref,
                  x_ref, y_ref, dn_ref, d_phi_q, d_phi_k, d_v, raw_ref):
    step = pl.program_id(0)

    @pl.when(step == 0)
    def _():
        fill_masks(len_ref, own_ref, before_ref, True)
        fill_masks(len_ref, own_t_ref, before_t_ref, False)

    lane = lax.broadcasted_iota(jnp.int32, (BLOCK, LANES), 1) < 64
    one = jnp.ones((BLOCK, LANES), BF16)
    for b in range(BLOCKS):
        rows = pl.ds(b * BLOCK, BLOCK)
        position = lax.broadcasted_iota(jnp.int32, (BLOCK, LANES), 0) + b * BLOCK
        dn = jnp.where(position < token_count(len_ref), att_g_ref[rows, :] * rden_ref[0, rows, :], 0.0)
        turned = pltpu.roll(-(dn * att_ref[0, rows, :]), 64, 1)
        dn_ref[rows, :] = dn.astype(BF16)
        v_low = v_ref[0, rows, :]
        for head in range(2):
            first = lane if head == 0 else jnp.logical_not(lane)
            high, low = split_two(jnp.where(first, dn, turned))
            x_ref[head, rows, :] = jnp.concatenate([high, low], axis=1)
            y = jnp.where(first, v_low.astype(F32), 1.0).astype(BF16)
            y_ref[head, rows, :] = jnp.concatenate([y, y], axis=1)
    for head in range(2):
        for b in range(BLOCKS):
            rows = pl.ds(b * BLOCK, BLOCK)
            x, y = x_ref[head, rows, :], y_ref[head, rows, :]
            phi_q, phi_k = phi_q_ref[head, rows, :], phi_k_ref[head, rows, :]
            d_kernel = dot_nt(x, y).astype(BF16) * own_ref[b]
            d_phi_q[rows, :] = dot(d_kernel, phi_k)
            d_phi_k[rows, :] = dot(d_kernel.T, phi_q)
            kernel_t = dot_nt(phi_k, phi_q).astype(BF16) * own_t_ref[b]
            d_v[head, rows, :] = dot(kernel_t, dn_ref[rows, :])
            if b > 0:
                earlier = pl.ds((b - 1) * BLOCK, BLOCK)
                top = pl.ds(b * BLOCK, REACH)
                bottom = pl.ds(b * BLOCK - REACH, REACH)
                d_kernel = dot_nt(x_ref[head, top, :], y_ref[head, earlier, :]).astype(BF16) * before_ref[b - 1]
                d_phi_q[top, :] += dot(d_kernel, phi_k_ref[head, earlier, :])
                d_phi_k[bottom, :] += dot(d_kernel.T[BLOCK - REACH :, :], phi_q_ref[head, top, :])
                kernel_t = dot_nt(phi_k_ref[head, bottom, :], phi_q).astype(BF16) * before_t_ref[b - 1]
                d_v[head, bottom, :] += dot(kernel_t, dn_ref[rows, :])
        high, low = split_two(fm_ref[head])
        stacked = jnp.concatenate([high, low, jnp.ones((LANES, 256), BF16)], axis=0)
        for which, d_phi, phi_ref in ((0, d_phi_q, phi_q_ref), (1, d_phi_k, phi_k_ref)):
            for b in range(BLOCKS):
                rows = pl.ds(b * BLOCK, BLOCK)
                d_projected = (d_phi[rows, :] * phi_ref[head, rows, :].astype(F32)).astype(BF16)
                raw_ref[which, head, rows, :] = dot_nt(d_projected, stacked)
    for b in range(BLOCKS):
        rows = pl.ds(b * BLOCK, BLOCK)
        for which, u_ref, out_ref in ((0, uq_ref, dq_ref), (1, uk_ref, dk_ref)):
            parts = []
            for head in range(2):
                raw = raw_ref[which, head, rows, :LANES]
                parts.append(raw + pltpu.roll(raw, 64, 1))
            along = jnp.where(lane, parts[0], parts[1])
            total = jnp.where(lane, raw_ref[which, 0, rows, LANES:], raw_ref[which, 1, rows, LANES:])
            grad = along * (64.0 ** (-0.25)) - u_ref[0, rows, :] * total * 0.125
            out_ref[rows, :] = grad.astype(BF16)
        dv_ref[rows, :] = jnp.where(lane, d_v[0, rows, :], d_v[1, rows, :]).astype(BF16)


def attn_bwd_scratch():
    return [
        pltpu.VMEM((BLOCKS, BLOCK, BLOCK), BF16),
        pltpu.VMEM((BLOCKS - 1, REACH, BLOCK), BF16),
        pltpu.VMEM((BLOCKS, BLOCK, BLOCK), BF16),
        pltpu.VMEM((BLOCKS - 1, REACH, BLOCK), BF16),
        pltpu.VMEM((2, LIVE, 256), BF16),
        pltpu.VMEM((2, LIVE, 256), BF16),
        pltpu.VMEM((LIVE, LANES), BF16),
        pltpu.VMEM((LIVE, 256), F32),
        pltpu.VMEM((LIVE, 256), F32),
        pltpu.VMEM((2, LIVE, LANES), F32),
        pltpu.VMEM((2, 2, LIVE, 256), F32),
    ]


def attn_bwd(layer, lengths, att_g, att, rden, phi_q, phi_k, uq, uk, v, fm, first, count, us, after=()):
    per_pair = pl.BlockSpec((1, LIVE, LANES), lambda p, *_: (first + p, 0, 0))
    per_head = pl.BlockSpec((2, LIVE, 256), lambda p, *_: (first + p, 0, 0))
    return call(
        attn_bwd_body,
        after,
        grid=(count,),
        prefetch=[lengths],
        operands=[att_g, att, rden, phi_q, phi_k, uq, uk, v, fm],
        in_specs=[pl.BlockSpec((LIVE, LANES), lambda p, *_: (0, first + p)), per_pair, per_pair, per_head, per_head, per_pair, per_pair, per_pair,
                  pl.BlockSpec((None, 2) + fm.shape[2:], lambda p, *_: (layer, first + p, 0, 0))],
        out_specs=[pl.BlockSpec((LIVE, LANES), lambda p, *_: (0, p))] * 3,
        scratch=attn_bwd_scratch(),
        out_shape=[jax.ShapeDtypeStruct((LIVE, count * LANES), BF16)] * 3,
        us=us,
        name="attn_backward",
    )


GROUPS = 2


def put(out_ref, ids, values, quarter, base):
    me, here = ids
    count = out_ref.shape[0]
    rows = values.shape[0] // count
    for portion in range(count):
        out_ref[portion ^ me, quarter ^ here, base : base + rows, :] = values[portion * rows : portion * rows + rows]


def columns(values, which):
    return values[:, which * LANES : which * LANES + LANES]


def group_of_qkv(half, group, refs):
    normed_t_ref, lefts = refs[0], refs[1:]
    runs = len(lefts) // 3
    tall = normed_t_ref.shape[0] // 2
    height = 3 * tall // GROUPS
    parts = []
    first = group * height
    while first < (group + 1) * height:
        j, start = divmod(first, tall)
        rows = min(tall - start, (group + 1) * height - first)
        normed_t = normed_t_ref[pl.ds(pl.multiple_of(half * tall + start, 16), rows), :]
        parts.append(jnp.concatenate([dot(normed_t, lefts[3 * run + j][...]) for run in range(runs)], axis=1))
        first += rows
    return jnp.concatenate(parts, axis=0) if len(parts) > 1 else parts[0]


def ff_bwd_body(layer, top, runs, parts, step, id_ref, *refs):
    extra_refs, refs = refs[: 3 * runs + (runs > 0)], refs[3 * runs + (runs > 0) :]
    if top:
        (x_ref, low_ref, g_ref, low_t_ref, gain_ref, shift_ref, up_ref, up_bias_ref, down_ref, down_bias_ref, wo_ref,
         out_ref, mid_g_ref, att_g_ref, small_ref, up_bias_g_ref, kept_ref,
         act_ref, pre_ref, g_t_ref, normed_t_ref, mid_low_ref, mid_ref) = refs
    else:
        (mid_ref, g_ref, low_t_ref, gain_ref, shift_ref, up_ref, up_bias_ref, down_ref, wo_ref,
         mid_g_ref, att_g_ref, small_ref, up_bias_g_ref, sent_ref, kept_ref,
         act_ref, pre_ref, g_t_ref, normed_t_ref, mid_low_ref) = refs
    hidden = up_ref.shape[1]
    quarters = kept_ref.shape[1]
    length = g_t_ref.shape[1]
    tiles = length // BLOCK
    share = hidden // quarters

    @pl.when(step == 0)
    def _():
        small_ref[...] = jnp.zeros_like(small_ref)
        up_bias_g_ref[...] = jnp.zeros_like(up_bias_g_ref)

    @pl.when(step < tiles)
    def _():
        if top:
            mid_ref[...] = x_ref[...]

            @pl.when(step < BLOCKS)
            def _():
                mid_ref[...] += dot(low_ref[...], wo_ref[...])

        rows = pl.ds(pl.multiple_of(step * BLOCK, BLOCK), BLOCK)
        mid = mid_ref[...]
        unit, rstd = normalize(mid)
        normed = (unit * gain_ref[layer, 1:2, :] + shift_ref[layer, 1:2, :]).astype(BF16)
        normed_t_ref[:, rows] = normed.T
        grad = g_ref[...]
        g_low = grad.astype(BF16)
        g_t_ref[:, rows] = g_low.T
        if top:
            total = mid + down_bias_ref[layer : layer + 1, :]
        back = jnp.zeros(grad.shape, F32)
        for quarter in range(quarters):
            cols = slice(quarter * share, quarter * share + share)
            pre = dot(normed, up_ref[:, cols]) + up_bias_ref[layer : layer + 1, cols]
            act, slope = gelu_terms(pre)
            act = act.astype(BF16)
            per_half = quarters // 2
            act_ref[quarter // per_half, rows, (quarter % per_half) * share : (quarter % per_half) * share + share] = act
            if top:
                total = total + dot(act, down_ref[cols, :])
            pre_low = (dot_nt(g_low, down_ref[cols, :]) * slope).astype(BF16)
            for which in range(share // LANES):
                pre_ref[which, rows, quarter * LANES : quarter * LANES + LANES] = columns(pre_low, which)
            up_bias_g_ref[:, cols] += jnp.sum(pre_low.astype(F32), axis=0, keepdims=True)
            back = back + dot_nt(pre_low, up_ref[:, cols])
        if top:
            out_ref[...] = total
        mid_g = grad + norm_pull(back, gain_ref[layer, 1:2, :], unit, rstd)
        mid_g_ref[...] = mid_g
        mid_low = mid_g.astype(BF16)
        small_ref[0:1, :] += jnp.sum(back * unit, axis=0, keepdims=True)
        small_ref[1:2, :] += jnp.sum(back, axis=0, keepdims=True)
        small_ref[2:3, :] += jnp.sum(g_low.astype(F32), axis=0, keepdims=True)

        @pl.when(step < BLOCKS)
        def _():
            mid_low_ref[rows, :] = mid_low
            att_g_ref[...] = dot_nt(mid_low, wo_ref[...])

    count = kept_ref.shape[0]
    if top:
        ids = (0, 0)
        halves = ((tiles, 0, kept_ref), (tiles + GROUPS, 1, kept_ref))
    else:
        ids = (id_ref[0] & (count - 1), id_ref[1])
        own = id_ref[0] // (parts // 2)
        halves = ((tiles, own ^ 1, sent_ref), (tiles + GROUPS, own, kept_ref))
    for first, half, end_ref in halves:
        for group in range(GROUPS):

            @pl.when(step == first + group)
            def _(half=half, group=group, end_ref=end_ref):
                wide = act_ref.shape[2] // GROUPS
                down = dot(g_t_ref[...], act_ref[half, :, group * wide : group * wide + wide])
                height = normed_t_ref.shape[0] * (share // LANES // 2) // GROUPS
                per_tile = normed_t_ref.shape[0] // height
                part = group % per_tile
                up = dot(normed_t_ref[part * height : part * height + height, :], pre_ref[half * (share // LANES // 2) + group // per_tile])
                tall = low_t_ref.shape[0] // 2 // GROUPS
                low_rows = pl.ds(pl.multiple_of(half * (low_t_ref.shape[0] // 2) + group * tall, tall), tall)
                out = dot(low_t_ref[low_rows, :], mid_low_ref[...])
                if runs:
                    extra = group_of_qkv(half, group, extra_refs)
                for quarter in range(quarters):
                    rows = slice(quarter * LANES, quarter * LANES + LANES)
                    pieces = [
                        jnp.concatenate([columns(down[rows], which) for which in range(wide // LANES)], axis=0),
                        columns(up, quarter),
                        columns(out, quarter),
                    ]
                    if runs:
                        pieces.append(columns(extra, quarter))
                    base = 0
                    for piece in pieces:
                        put(end_ref, ids, piece, quarter, base)
                        base += piece.shape[0] // count


def piece_shapes(parts, quarters, width, hidden):
    rows = hidden // parts + width * (hidden // quarters // LANES) // parts + width // parts
    return (parts // 2, quarters, rows, LANES)


def lower_body(layer, runs, parts, id_ref, *refs):
    extra = 3 * runs + 1
    step = pl.program_id(0)
    *refs, sems = refs
    late = refs[len(refs) - extra - 1 :]
    refs = refs[: len(refs) - extra - 1]
    low_t = extra + 2
    fetch(step, 0, pl.num_programs(0) - 2 * GROUPS, list(refs[:extra]) + [refs[low_t]], late, sems)
    ff_bwd_body(layer, False, runs, parts, step, id_ref, *late[:extra], *refs[extra:low_t], late[extra], *refs[low_t + 1 :])


def ff_bwd(layer, ids, parts, quarters, grad, low_t, gains, shifts, up, up_bias, down, wo, mid, qkv, after=()):
    length, width = grad.shape
    hidden = up.shape[2]
    tiles = length // BLOCK
    portions = parts // 2
    group = portions // GROUPS
    rows = pl.BlockSpec((BLOCK, width), lambda i, ids: (jnp.minimum(i, tiles - 1), 0))
    live = pl.BlockSpec((BLOCK, width), lambda i, ids: (jnp.minimum(i, BLOCKS - 1), 0))
    extra = [qkv[0]] + [part for run in qkv[1] for part in run]
    end = piece_shapes(parts, quarters, width, hidden)
    end = end[:2] + (end[2] + 3 * width // parts, LANES)

    def end_spec(first):
        return pl.BlockSpec((group,) + end[1:], lambda i, ids: (jnp.clip(i - first, 0, GROUPS - 1) ^ ((ids[0] & (portions - 1)) // group), 0, 0, 0))

    return call(
        functools.partial(lower_body, layer, len(extra) // 3, parts),
        after,
        grid=(tiles + 2 * GROUPS,),
        prefetch=[ids],
        operands=extra + [mid, grad, low_t, gains, shifts, up, up_bias, down, wo],
        in_specs=[anywhere() for _ in extra]
        + [rows, rows, anywhere(), constant(*gains.shape), constant(*shifts.shape), of_layer(layer, up), constant(*up_bias.shape)]
        + [of_layer(layer, down), of_layer(layer, wo)],
        out_specs=[rows, live, resident(8, width), resident(1, hidden), end_spec(tiles), end_spec(tiles + GROUPS)],
        scratch=ff_bwd_scratch(length, width, hidden, quarters)
        + [pltpu.VMEM(array.shape, array.dtype) for array in extra + [low_t]]
        + [pltpu.SemaphoreType.DMA((len(extra) + 1,))],
        out_shape=[
            jax.ShapeDtypeStruct((length, width), F32),
            jax.ShapeDtypeStruct((LIVE, width), F32),
            jax.ShapeDtypeStruct((8, width), F32),
            jax.ShapeDtypeStruct((1, hidden), F32),
            jax.ShapeDtypeStruct(end, F32),
            jax.ShapeDtypeStruct(end, F32),
        ],
        us=18.0,
        name="ff_backward",
    )


def ff_bwd_scratch(length, width, hidden, quarters):
    return [
        pltpu.VMEM((2, length, hidden // 2), BF16),
        pltpu.VMEM((hidden // quarters // LANES, length, quarters * LANES), BF16),
        pltpu.VMEM((width, length), BF16),
        pltpu.VMEM((width, length), BF16),
        pltpu.VMEM((LIVE, width), BF16),
    ]


def layer_body(layer, top, pairs, parts, len_ref, id_ref, *refs):
    x_ref, gain_ref, shift_ref, w_ref, fm_ref, wo_ref, up_ref, up_bias_ref, down_ref, down_bias_ref = refs[:10]
    refs = refs[10:]
    *refs, wo_late, up_late, down_late, sems = refs
    step = pl.program_id(0)
    fetch(step, 0, pairs, [ref.at[layer] for ref in (wo_ref, up_ref, down_ref)], [wo_late, up_late, down_late], sems)
    wo_ref, up_ref, down_ref = wo_late, up_late, down_late
    refs = tuple(refs)
    if top:
        (g_ref, *outs) = refs[:9]
        out_ref, mid_g_ref, att_g_ref, small_ref, up_bias_g_ref, kept_ref, low_t_ref = refs[9:15] + refs[21:22]
        attn_scratch, low_ref = refs[15:20], refs[20]
        ff_scratch = refs[22:]
    else:
        outs = refs[:8]
        low_t_ref, out_ref, mid_ref = refs[8:11]
        attn_scratch, low_ref = refs[11:16], refs[16]

    @pl.when(step < pairs)
    def _():
        attn_fwd_body(layer, step, low_ref, low_t_ref, len_ref, x_ref, gain_ref, shift_ref, w_ref, fm_ref, *outs, *attn_scratch)

    @pl.when(step >= pairs)
    def _():
        tile = step - pairs
        x_tile = x_ref.at[pl.ds(pl.multiple_of(jnp.minimum(tile, x_ref.shape[0] // BLOCK - 1) * BLOCK, BLOCK), BLOCK)]
        low_tile = low_ref.at[pl.ds(pl.multiple_of(jnp.minimum(tile, BLOCKS - 1) * BLOCK, BLOCK), BLOCK)]
        weight_refs = (gain_ref, shift_ref, up_ref, up_bias_ref, down_ref, down_bias_ref)
        if top:
            ff_bwd_body(layer, True, 0, parts, tile, id_ref, x_tile, low_tile, g_ref, low_t_ref, *weight_refs, wo_ref,
                        out_ref, mid_g_ref, att_g_ref, small_ref, up_bias_g_ref, kept_ref, *ff_scratch)
        else:
            ff_fwd_body(layer, tile, x_tile, low_tile, wo_ref, *weight_refs, out_ref, mid_ref)


def layer_forward(layer, lengths, ids, parts, quarters, x, gains, shifts, w, fm, wo, up, up_bias, down, down_bias, grad=None, after=()):
    length, width = x.shape
    hidden = up.shape[2]
    pairs = fm.shape[1] // 2
    heads = 2 * pairs
    tiles = length // BLOCK
    top = grad is not None
    pair = lambda i: jnp.minimum(i, pairs - 1)
    tile = lambda i: jnp.clip(i - pairs, 0, tiles - 1)
    per_pair = pl.BlockSpec((1, LIVE, LANES), lambda i, *_: (pair(i), 0, 0))
    per_head = pl.BlockSpec((2, LIVE, 256), lambda i, *_: (pair(i), 0, 0))
    rows = pl.BlockSpec((BLOCK, width), lambda i, *_: (tile(i), 0))
    live = pl.BlockSpec((BLOCK, width), lambda i, *_: (jnp.minimum(tile(i), BLOCKS - 1), 0))
    out_specs = [resident(width, LIVE), per_head, per_head] + [per_pair] * 5
    out_shape = [jax.ShapeDtypeStruct((width, LIVE), BF16)] + [jax.ShapeDtypeStruct((heads, LIVE, 256), BF16)] * 2
    out_shape += [jax.ShapeDtypeStruct((pairs, LIVE, LANES), dtype) for dtype in (F32, F32, BF16, F32, F32)]
    scratch = [
        pltpu.VMEM((LIVE, width), BF16),
        pltpu.VMEM((3, pairs, LIVE, LANES), F32),
        pltpu.VMEM((BLOCKS, BLOCK, BLOCK), BF16),
        pltpu.VMEM((BLOCKS - 1, REACH, BLOCK), BF16),
        pltpu.VMEM((2, BLOCK, 256), F32),
        pltpu.VMEM((LIVE, width), BF16),
    ]
    if top:
        end = piece_shapes(parts, quarters, width, hidden)
        group = end[0] // GROUPS
        out_specs += [rows, rows, live, resident(8, width), resident(1, hidden)]
        out_specs.append(pl.BlockSpec((group,) + end[1:], lambda i, *_: (jnp.clip(i - pairs - tiles, 0, 2 * GROUPS - 1), 0, 0, 0)))
        out_shape += [jax.ShapeDtypeStruct(shape, F32) for shape in ((length, width), (length, width), (LIVE, width), (8, width), (1, hidden), (parts,) + end[1:])]
        scratch += [pltpu.VMEM((width, LIVE), BF16)] + ff_bwd_scratch(length, width, hidden, quarters) + [pltpu.VMEM((BLOCK, width), F32)]
    else:
        out_specs += [resident(width, LIVE), rows, rows]
        out_shape += [jax.ShapeDtypeStruct((width, LIVE), BF16)] + [jax.ShapeDtypeStruct((length, width), F32)] * 2
    return call(
        functools.partial(layer_body, layer, top, pairs, parts),
        after,
        grid=(pairs + tiles + (2 * GROUPS if top else 0),),
        prefetch=[lengths, ids],
        operands=[x, gains, shifts, w, fm, wo, up, up_bias, down, down_bias] + ([grad] if top else []),
        in_specs=[
            constant(*x.shape),
            constant(*gains.shape),
            constant(*shifts.shape),
            of_layer(layer, w),
            pl.BlockSpec((None, 2) + fm.shape[2:], lambda i, *_: (layer, pair(i), 0, 0)),
            anywhere(),
            anywhere(),
            constant(*up_bias.shape),
            anywhere(),
            constant(*down_bias.shape),
        ]
        + ([rows] if top else []),
        out_specs=out_specs,
        scratch=scratch + [pltpu.VMEM(array.shape[1:], array.dtype) for array in (wo, up, down)] + [pltpu.SemaphoreType.DMA((3,))],
        out_shape=out_shape,
        us=20.0,
        name="layer_top" if top else "layer_forward",
    )


def input_bwd_body(layer, runs, parts, order, ends, id_ref, *refs, step=None, tiles=None):
    left_refs = refs[: 3 * runs]
    w_ref, normed_t_ref, x_ref, gain_ref, mid_g_ref = refs[3 * runs : 3 * runs + 5]
    small_refs = refs[3 * runs + 5 : -4]
    if ends:
        out_ref, small_ref, sent_ref, kept_ref = refs[-4:]
    else:
        out_ref, small_ref = refs[-2:]
    if step is None:
        step = pl.program_id(0)
        tiles = pl.num_programs(0) - (2 if ends else 0)

    @pl.when(step == 0)
    def _():
        small_ref[...] = jnp.zeros_like(small_ref)

    @pl.when(step < BLOCKS)
    def _():
        rows = pl.ds(pl.multiple_of(step * BLOCK, BLOCK), BLOCK)
        back = jnp.zeros(x_ref.shape, F32)
        for run in range(runs):
            for j in range(3):
                left = left_refs[3 * run + j]
                wide = left.shape[1]
                back = back + dot_nt(left[rows, :], w_ref[j, :, run * wide : run * wide + wide])
        unit, rstd = normalize(x_ref[...])
        out_ref[...] = mid_g_ref[...] + norm_pull(back, gain_ref[layer, 0:1, :], unit, rstd)
        small_ref[0:1, :] += jnp.sum(back * unit, axis=0, keepdims=True)
        small_ref[1:2, :] += jnp.sum(back, axis=0, keepdims=True)

    @pl.when((step >= BLOCKS) & (step < tiles))
    def _():
        out_ref[...] = mid_g_ref[...]

    if not ends:
        return
    count, quarters = sent_ref.shape[:2]
    ids = (id_ref[0] & (count - 1), id_ref[1])
    for when, flip, end_ref in ((tiles, 1, sent_ref), (tiles + 1, 0, kept_ref)):
        half = (id_ref[0] // (parts // 2)) ^ flip

        @pl.when(step == when)
        def _(half=half, end_ref=end_ref):
            tall = normed_t_ref.shape[0] // 2
            normed_t = normed_t_ref[pl.ds(pl.multiple_of(half * tall, tall), tall), :]
            totals = [jnp.concatenate([dot(normed_t, left_refs[3 * run + j][...]) for run in range(runs)], axis=1) for j in range(3)]
            for quarter in range(quarters):
                put(end_ref, ids, jnp.concatenate([columns(total, quarter) for total in totals], axis=0), quarter, 0)
            base = 3 * tall // count
            if order:
                room = end_ref.shape[2] - base
                end_ref[:, :, base:, :] = jnp.zeros((count, quarters, room, LANES), F32)

                @pl.when(half == 0)
                def _():
                    for at, (array, row, first) in enumerate(order):
                        portion, offset = divmod(at, room)
                        source = small_ref if array < 0 else small_refs[array]
                        per = source.shape[1] // quarters
                        for quarter in range(quarters):
                            start = quarter * per + first
                            end_ref[portion ^ ids[0], quarter ^ ids[1], base + offset : base + offset + 1, :] = source[row : row + 1, start : start + LANES]


def attn_input_body(layer, pairs, len_ref, *refs):
    att_refs, (w_any, x_ref, gain_ref, mid_g_ref, *outs) = refs[:9], refs[9:]
    proj_refs, out_ref, small_ref = outs[:3], outs[3], outs[4]
    attn_scratch, late, w_ref, sems = outs[5:16], outs[16:19], outs[19], outs[20]
    step = pl.program_id(0)
    fetch(step, 0, pairs, [w_any.at[layer]], [w_ref], sems)

    @pl.when(step < pairs)
    def _():
        attn_bwd_body(len_ref, *att_refs, *proj_refs, *attn_scratch)
        for one, whole in zip(proj_refs, late):
            whole[:, pl.ds(pl.multiple_of(step * LANES, LANES), LANES)] = one[...]

    @pl.when(step >= pairs)
    def _():
        tile = step - pairs
        input_bwd_body(layer, 1, 1, (), False, None, *late, w_ref, None, x_ref, gain_ref, mid_g_ref, out_ref, small_ref, step=tile, tiles=pl.num_programs(0) - pairs)


def attn_input_bwd(layer, lengths, att_g, att, rden, phi_q, phi_k, uq, uk, v, fm, w, x, gains, mid_g, after=()):
    length, width = x.shape
    tiles = length // BLOCK
    pairs = fm.shape[1] // 2
    pair = lambda i: jnp.minimum(i, pairs - 1)
    per_pair = pl.BlockSpec((1, LIVE, LANES), lambda i, *_: (pair(i), 0, 0))
    per_head = pl.BlockSpec((2, LIVE, 256), lambda i, *_: (pair(i), 0, 0))
    column = pl.BlockSpec((LIVE, LANES), lambda i, *_: (0, pair(i)))
    rows = pl.BlockSpec((BLOCK, width), lambda i, *_: (jnp.clip(i - pairs, 0, tiles - 1), 0))
    return call(
        functools.partial(attn_input_body, layer, pairs),
        after,
        grid=(pairs + tiles,),
        prefetch=[lengths],
        operands=[att_g, att, rden, phi_q, phi_k, uq, uk, v, fm, w, x, gains, mid_g],
        in_specs=[column, per_pair, per_pair, per_head, per_head, per_pair, per_pair, per_pair]
        + [pl.BlockSpec((None, 2) + fm.shape[2:], lambda i, *_: (layer, pair(i), 0, 0)), anywhere(), rows, constant(*gains.shape), rows],
        out_specs=[column] * 3 + [rows, resident(8, width)],
        scratch=attn_bwd_scratch()
        + [pltpu.VMEM((LIVE, width), BF16)] * 3
        + [pltpu.VMEM(w.shape[1:], w.dtype), pltpu.SemaphoreType.DMA((1,))],
        out_shape=[jax.ShapeDtypeStruct((LIVE, width), BF16)] * 3 + [jax.ShapeDtypeStruct((length, width), F32), jax.ShapeDtypeStruct((8, width), F32)],
        us=1.0,
        name="attn_input_backward",
    )


def input_bwd(layer, ids, parts, quarters, proj_g, w, normed_t, x, gains, mid_g, smalls=(), order=(), ends=True, after=()):
    length, width = x.shape
    tiles = length // BLOCK
    rows = pl.BlockSpec((BLOCK, width), lambda i, ids: (jnp.minimum(i, tiles - 1), 0))
    lefts = [part for run in proj_g for part in run]
    small_rows = small_rows_of(len(order), parts, 3 * width // parts)
    end = (parts // 2, quarters, 3 * width // parts + small_rows, LANES)
    return call(
        functools.partial(input_bwd_body, layer, len(proj_g), parts, tuple(order), ends),
        after,
        grid=(tiles + (2 if ends else 0),),
        prefetch=[ids],
        operands=lefts + [w, normed_t, x, gains, mid_g] + list(smalls),
        in_specs=[constant(*a.shape) for a in lefts]
        + [of_layer(layer, w), constant(*normed_t.shape), rows, constant(*gains.shape), rows]
        + [constant(*a.shape) for a in smalls],
        out_specs=[rows, resident(8, width)] + [resident(*end)] * (2 if ends else 0),
        out_shape=[jax.ShapeDtypeStruct((length, width), F32), jax.ShapeDtypeStruct((8, width), F32)] + [jax.ShapeDtypeStruct(end, F32)] * (2 if ends else 0),
        us=1.0,
        name="input_backward",
    )


def small_rows_of(count, parts, others):
    least = -(-count // (8 * parts)) * 8
    return least + (others + least) % 16


class Share:
    def __init__(self, terms, names, rows):
        self.terms, self.names, self.rows, self.done = terms, names, rows, ()

    def operands(self, step, over):
        specs = []
        for _, names, which in self.terms:
            at = [0 if name in self.done else 1 if name == step else None for name in names]
            block = [2 if index is None and name not in over else None for name, index in zip(names, at)]

            def index_map(*grid, names=names, at=at, which=which):
                free = [grid[over.index(name)] if name in over else 0 for name in names]
                return tuple(one if index is None else index for one, index in zip(free, at)) + (which, 0)

            specs.append(pl.BlockSpec(tuple(block) + (self.rows, LANES), index_map))
        return [array for array, _, _ in self.terms], specs

    def left(self, step):
        return [name for name in self.names if name not in self.done and name != step]

    def take(self, step, array):
        self.terms.append((array, tuple(self.left(step)), 0))
        self.done += (step,)


def sums_body(counts, *refs):
    outs = refs[len(refs) - len(counts) :]
    first = 0
    for count, out in zip(counts, outs):
        out[...] = sum(ref[...] for ref in refs[first : first + count])
        first += count


def sums_to_send(shares, steps, over, after):
    operands, in_specs, out_specs, out_shape = [], [], [], []
    for part, step in zip(shares, steps):
        arrays, specs = part.operands(step, over)
        operands += arrays
        in_specs += specs
        left = part.left(step)
        out_shape.append(jax.ShapeDtypeStruct((2,) * len(left) + (part.rows, LANES), F32))
        block = tuple(None if name in over else 2 for name in left) + (part.rows, LANES)
        out_specs.append(pl.BlockSpec(block, lambda *grid, left=left: tuple(grid[over.index(n)] if n in over else 0 for n in left) + (0, 0)))
    return call(
        functools.partial(sums_body, tuple(len(part.terms) for part in shares)),
        after,
        grid=(2,) * len(over) if over else (1,),
        prefetch=[],
        operands=operands,
        in_specs=in_specs,
        out_specs=out_specs,
        out_shape=out_shape,
        us=2.0,
        name="sums_to_send",
    )


def last_add_body(counts, *refs):
    upper_ref, lower_ref = refs[-2:]
    cut = upper_ref.shape[0]
    first, base = 0, 0
    for count in counts:
        total = sum(ref[...] for ref in refs[first : first + count])
        first += count
        rows = total.shape[0]
        split = min(max(cut - base, 0), rows)
        if split:
            upper_ref[base : base + split, :] = total[:split]
        if split < rows:
            lower_ref[base + split - cut : base + rows - cut, :] = total[split:]
        base += rows


def last_add(shares, after):
    rows = sum(part.rows for part in shares)
    cut = rows // 2
    operands, in_specs = [], []
    for part in shares:
        arrays, specs = part.operands(None, ())
        operands += arrays
        in_specs += specs
    return call(
        functools.partial(last_add_body, tuple(len(part.terms) for part in shares)),
        after,
        grid=(1,),
        prefetch=[],
        operands=operands,
        in_specs=in_specs,
        out_specs=[resident(cut, LANES), resident(rows - cut, LANES)],
        out_shape=[jax.ShapeDtypeStruct((cut, LANES), F32), jax.ShapeDtypeStruct((rows - cut, LANES), F32)],
        us=1.5,
        name="last_terms",
    )


def hold_body(*refs):
    del refs


def hold(block, after):
    return call(
        hold_body,
        after,
        grid=(1,),
        prefetch=[],
        operands=[block],
        in_specs=[pl.BlockSpec(memory_space=pl.ANY)],
        out_specs=pl.BlockSpec(memory_space=pl.ANY),
        out_shape=jax.ShapeDtypeStruct(block.shape, block.dtype),
        aliases=[(0, 0)],
        us=1.0,
        name="hold",
    )


def swap(block, axis_name, bit):
    return lax.ppermute(block, axis_name, [(i, i ^ bit) for i in range(lax.axis_size(axis_name))])


def bits_of(extent):
    return [1 << i for i in range(extent.bit_length() - 1)]


class Line:
    def __init__(self):
        self.last = []

    def __call__(self, function, *args, **kwargs):
        made = function(*args, after=self.last, **kwargs)
        leaves = jax.tree.leaves(made)
        self.last = [min(leaves, key=lambda a: a.size)]
        return made

    def wait(self, *chains):
        self.last = self.last + [array for chain in chains for array in chain.pending]


def scatter(line, sent, kept, parts, quarters):
    dp_bits, batch_bits = bits_of(parts), bits_of(quarters)
    near, far = dp_bits[0], dp_bits[1:]
    got = swap(sent, "dp", near)
    yield [got]
    batch_names = [("batch", bit) for bit in batch_bits[::-1]]
    names = tuple([("dp", bit) for bit in far] + batch_names)
    rows = kept.shape[2] // 2
    whole = [part.reshape((2,) * len(names) + part.shape[2:]) for part in (kept, got)]
    shares = [Share([(part, names, which) for part in whole], names, rows) for which in range(2)]
    orders = [[("dp", bit) for bit in order] + [("batch", bit) for bit in last] for order, last in ((far, batch_bits), (far[::-1], batch_bits[::-1]))]
    for count, steps in enumerate(zip(*orders)):
        large = rows * 2 ** (len(names) - count) > 2**12
        sums = line(sums_to_send, shares, steps, tuple(batch_names) if large and steps[0][0] == "dp" else ())
        moved = [swap(block, *step) for block, step in zip(sums, steps)]
        for part, step, block in zip(shares, steps, moved):
            part.take(step, block)
        yield moved
    return shares


def spread(halves, parts):
    dp_bits = bits_of(parts)
    near, far = dp_bits[0], dp_bits[1:]
    streams = list(halves)
    names = [[], []]
    for bits in zip(far[::-1], far):
        moved = [swap(stream, "dp", bit) for stream, bit in zip(streams, bits)]
        yield moved
        for which, bit in enumerate(bits):
            names[which].append(bit)
            names[which].sort()
            streams[which] = jnp.stack([streams[which], moved[which]], axis=names[which].index(bit))
    block = jnp.concatenate(streams, axis=-2)
    block = block.reshape(parts // 2, block.shape[-2], LANES)
    moved = swap(block, "dp", near)
    yield [moved]
    return block, moved


class Chain:
    def __init__(self, steps):
        self.steps, self.result, self.pending = steps, None, []

    def step(self):
        if self.result is None:
            try:
                self.pending = next(self.steps)
            except StopIteration as stop:
                self.result = stop.value

    def finish(self):
        while self.result is None:
            self.step()
        return self.result


def unpack_body(names, bases, pieces, inputs, filled, id_ref, *refs):
    out_refs = dict(zip(names, refs[inputs + filled :]))
    down_ref, small_ref = refs[-2:]
    me = id_ref[0] if inputs == 2 else 0
    for top in range(inputs):
        ref = refs[top]
        portions = ref.shape[0]
        for slot in range(portions):
            portion = (slot + top * portions) ^ me
            half = portions * inputs // 2
            upper, inner = portion // half, portion % half
            for name, layer, first, rows in pieces:
                values = ref[slot, first : first + rows, :]
                if name == "small":
                    small_ref[pl.ds(pl.multiple_of(portion * rows, 8), rows), :] = values
                    continue
                out_ref = out_refs[name]
                layer = layer - bases[name]
                if name == "qkv":
                    width = out_ref.shape[1] // 3
                    unit = math.gcd(rows, width // 2)
                    for k in range(0, rows, unit):
                        flat = inner * rows + k
                        start = (flat // (width // 2)) * width + upper * (width // 2) + flat % (width // 2)
                        out_ref[layer, pl.ds(pl.multiple_of(start, 8), unit), :] = values[k : k + unit]
                elif name == "up":
                    height = out_ref.shape[1]
                    flat = portion * rows
                    tile, start = flat // height, flat % height
                    out_ref[layer, pl.ds(pl.multiple_of(start, 8), rows), pl.ds(pl.multiple_of(tile * LANES, LANES), LANES)] = values
                elif name == "down":
                    down_ref[pl.ds(pl.multiple_of(portion * rows, 8), rows), :] = values
                else:
                    out_ref[layer, pl.ds(pl.multiple_of(portion * rows, 8), rows), :] = values
    if "down" in out_refs:
        for first in range(0, down_ref.shape[0], LANES):
            out_refs["down"][0, first : first + LANES, :] = down_ref[first : first + LANES, :].T
    if "gains" in out_refs:
        layers, wide = out_refs["up_bias"].shape
        row = 0
        for layer in range(layers):
            for name, count in (("gains", 2), ("shifts", 2)):
                out_refs[name][layer] = small_ref[row : row + count, :]
                row += count
            for k in range(wide // LANES):
                out_refs["up_bias"][layer : layer + 1, k * LANES : k * LANES + LANES] = small_ref[row : row + 1, :]
                row += 1
            out_refs["down_bias"][layer : layer + 1, :] = small_ref[row : row + 1, :]
            row += 1


def unpack(ids, pair, pieces, layers, width, hidden, quarters, filled=(), after=()):
    shapes = {"down": (layers, hidden, LANES), "up": (layers, width, hidden // quarters), "out": (layers, width, LANES), "qkv": (layers, 3 * width, LANES)}
    found = {name: [layer for piece, layer, _, _ in pieces if piece == name] for name in shapes}
    names = tuple(name for name in shapes if found[name])
    bases = {name: min(found[name]) for name in names}
    out_specs = [
        pl.BlockSpec((len(found[name]),) + shapes[name][1:], lambda *_, name=name: (bases[name] // len(found[name]), 0, 0)) for name in names
    ]
    out_shape = [jax.ShapeDtypeStruct(shapes[name], F32) for name in names]
    small = [rows for piece, _, _, rows in pieces if piece == "small"]
    if small:
        names += ("gains", "shifts", "up_bias", "down_bias")
        for shape in ((layers, 2, LANES), (layers, 2, LANES), (layers, hidden // quarters), (layers, LANES)):
            out_specs.append(resident(*shape))
            out_shape.append(jax.ShapeDtypeStruct(shape, F32))
    return call(
        functools.partial(unpack_body, names, bases, pieces, len(pair), len(filled)),
        after,
        grid=(1,),
        prefetch=[ids],
        operands=list(pair) + list(filled),
        in_specs=[constant(*a.shape) for a in pair] + [pl.BlockSpec(memory_space=pl.ANY)] * len(filled),
        out_specs=out_specs,
        scratch=[
            pltpu.VMEM((hidden if found["down"] else 8, LANES), F32),
            pltpu.VMEM((len(pair) * pair[0].shape[0] * small[0] if small else 8, LANES), F32),
        ],
        out_shape=out_shape,
        aliases=[(len(pair) + which, which) for which in range(len(filled))],
        mib=32,
        us=4.0,
        name="unpack",
    )


def reverse_bits(value, extent):
    return sum(((value // bit) % 2) * (extent // (2 * bit)) for bit in bits_of(extent))


def per_device(activations_in, gains, shifts, qkv_weights, out_weights, up_weights, up_bias, down_weights, down_bias, feature_maps, lengths, cotangent):
    layers, _, width = gains.shape
    hidden = up_bias.shape[1]
    parts, quarters = lax.axis_size("dp"), lax.axis_size("batch")
    ids = jnp.stack([reverse_bits(lax.axis_index("dp"), parts), lax.axis_index("batch")]).astype(jnp.int32)
    proteins = lengths[0]
    pairs = feature_maps.shape[1] // 2
    half = pairs // 2
    line = Line()
    last = layers - 1
    weights = (gains, shifts, qkv_weights, feature_maps, out_weights, up_weights, up_bias, down_weights, down_bias)
    x_one = activations_in[0]
    normed_zero_t, *kept_zero, low_t, x_two, mid = layer_forward(0, proteins, ids, parts, quarters, x_one, *weights)
    normed_one_t, *kept_one, values, mid_g, att_g, small_two, up_bias_g, first = layer_forward(1, proteins, ids, parts, quarters, x_two, *weights, grad=cotangent[0])
    line.last = [up_bias_g]
    smalls = [[None, None, None], [None, small_two, up_bias_g]]
    saved = ((x_one, normed_zero_t, kept_zero), (x_two, normed_one_t, kept_one))

    def attn_part(layer, att_g, first, count, us):
        phi_q, phi_k, uq, uk, v, att, rden = saved[layer][2]
        return line(attn_bwd, layer, proteins, att_g, att, rden, phi_q, phi_k, uq, uk, v, feature_maps, first, count, us)

    def input_part(layer, proj_g, mid_g, **rest):
        grad, smalls[layer][0], *ends = line(
            input_bwd, layer, ids, parts, quarters, proj_g, qkv_weights, saved[layer][1], saved[layer][0], gains, mid_g, **rest
        )
        return grad, Chain(scatter(line, *ends, parts, quarters)) if ends else None

    wide = hidden // quarters // LANES
    ff_rows = (hidden // parts, width * wide // parts, width // parts)
    ff_total, qkv_rows = sum(ff_rows), 3 * width // parts
    sizes = (layers, width, hidden, quarters)

    def ff_pieces(layer, base):
        return (("down", layer, base, ff_rows[0]), ("up", layer, base + ff_rows[0], ff_rows[1]), ("out", layer, base + ff_rows[0] + ff_rows[1], ff_rows[2]))

    first = lax.psum_scatter(first.reshape(-1, LANES), "dp", scatter_dimension=0, tiled=True)
    phi_q, phi_k, uq, uk, v, att, rden = kept_one
    *proj_g, grad, smalls[1][0] = line(
        attn_input_bwd, 1, proteins, att_g, att, rden, phi_q, phi_k, uq, uk, v, feature_maps, qkv_weights, x_two, gains, mid_g
    )
    runs = [proj_g]
    mid_g, att_g, smalls[0][1], smalls[0][2], sent, kept = line(
        ff_bwd, 0, ids, parts, quarters, grad, low_t, gains, shifts, up_weights, up_bias, down_weights, out_weights, mid, (normed_one_t, runs)
    )
    second = Chain(scatter(line, sent, kept, parts, quarters))
    second.step()
    runs = [attn_part(0, att_g, 0, half, 60.0)]
    second.step()
    first = lax.psum_scatter(line(hold, first), "batch", scatter_dimension=0, tiled=True)
    runs.append(attn_part(0, att_g, half, pairs - half, 1.0))
    flat = [array for layer in range(layers) for array in smalls[layer]]
    order = []
    for layer in range(layers):
        one, two, bias = (3 * layer + k for k in range(3))
        order += [(one, 0, 0), (two, 0, 0), (one, 1, 0), (two, 1, 0)] + [(bias, 0, k * LANES) for k in range(wide)] + [(two, 2, 0)]
    present = [k for k, array in enumerate(flat) if array is not None]
    order = [(present.index(array) if array in present else -1, row, first_col) for array, row, first_col in order]
    grad, third = input_part(0, runs, mid_g, smalls=[flat[k] for k in present], order=order)
    third.step()
    second.step()
    third.step()
    second.step()
    third.step()
    first = lax.all_gather(line(hold, first), "dp", tiled=True).reshape(parts, -1, LANES)
    third.step()
    second.step()
    third.step()
    down, up, out = line(unpack, ids, [first], ff_pieces(1, 0), *sizes)
    pair = Chain(spread(line(last_add, second.finish() + third.finish()), parts)).finish()
    pieces = ff_pieces(0, 0) + (("qkv", 1, ff_total, qkv_rows), ("qkv", 0, ff_total + qkv_rows, qkv_rows))
    pieces += (("small", 0, ff_total + 2 * qkv_rows, small_rows_of(len(order), parts, qkv_rows)),)
    down, up, out, qkv, gains_g, shifts_g, up_bias_g, down_bias_g = line(unpack, ids, pair, pieces, *sizes, (down, up, out))
    return (
        values[None],
        grad[None],
        gains_g,
        shifts_g,
        qkv.reshape(layers, 3, width, LANES),
        out,
        up,
        up_bias_g,
        down,
        down_bias_g,
    )


def solution(mesh):
    rows = P(("dp", "batch"), None, None)
    return jax.shard_map(
        per_device,
        mesh=mesh,
        in_specs=(rows,) + (P(),) * 9 + (P(("dp", "batch"), None), rows),
        out_specs=(
            rows,
            rows,
            P(None, None, "batch"),
            P(None, None, "batch"),
            P(None, None, None, "batch"),
            P(None, None, "batch"),
            P(None, None, "batch"),
            P(None, "batch"),
            P(None, None, "batch"),
            P(None, "batch"),
        ),
        check_vma=False,
    )
```
